32 devices in a mesh: groups: 2 (over y), streams: 8 (over z, x), segment: 2 (over core).
Axes of the slice: x: 2, y: 2, z: 4, core: 2. Of those that a mesh axis runs over, the one named last changes fastest.
Arguments:
- latent: bfloat16 [4096, 1024], P(('groups', 'streams'), 'segment'), parts along dimension 0, may hold values from -6 to 6
- conv_weight: bfloat16 [1024, 16, 512], P('streams', None, 'segment'), may hold values from -0.1875 to 0.1875
- conv_bias: float32 [512], P('segment'), may hold values from -3 to 3
- tail_cache: bfloat16 [128, 8, 512], P(('groups', 'streams'), None, 'segment'), parts along dimension 0, may hold values from -6 to 6
- input_cache: bfloat16 [128, 2, 512], P(('groups', 'streams'), None, 'segment'), parts along dimension 0, may hold values from -0.8984375 to 2
- resume_slot: int32 [128], P(('groups', 'streams')), parts along dimension 0, may hold values from -1 to 255, as said below
- res_weight: bfloat16 [3, 512, 256], P(None, 'segment'), may hold values from -0.15625 to 0.15625
- res_bias: float32 [256], replicated, may hold values from -3 to 3
- skip_weight: bfloat16 [256, 512], P(None, 'segment'), may hold values from -0.375 to 0.375
- skip_bias: float32 [512], P('segment'), may hold values from -3 to 3
Outputs:
- decoded: bfloat16 [4096, 8, 512], P(('groups', 'streams'), None, 'segment'), parts along dimension 0
- new_tail: bfloat16 [4096, 8, 512], P(('groups', 'streams'), None, 'segment'), parts along dimension 0
The draws below stay inside these ranges and needn't reach their ends.
There are 2 independent parts, one for each index of `groups`. The reference program is written for one: setup_inputs(seed, part) draws one part's arguments, and reference() takes and returns one part's arrays. A program takes and returns all parts, laid end to end along the dimension named above; an argument that names none is the same for every part. Nothing has to cross between parts.
Inputs may be any that keep to these rules, and one draw needn't show every extreme that they name: `resume_slot`: slot k of an owner device's store serves decoder device k // 1 of the same index range; an entry is -1 (slot unused) or the position, among that decoder device's 256 rows in decoder order, of the session that resumes from it. No decoder row is named by two slots. In every draw there is one decoder device all of whose reserved slots are in use (none is -1).
All inputs are finite; a program needn't handle non-finite values.
Results may differ from the reference program's by a relative error of at most 0.0042.
Values may be sent and summed in bfloat16 or wider, within the bound.
No kernel may reach another device: no remote copies, remote signals or barrier semaphores. Data moves between devices by JAX's collectives and lax.ppermute only.
A program may use at most 64 MiB of HBM per device.

```python
import jax
import jax.numpy as jnp
from jax import lax

D = 1024
C1 = 512
HID = 256
STRIDE = 8
RES_K = 3
CAP = 1
S_DEV = 256
KERNEL = 16
SESSIONS = 2048
SLOTS = 64
N_STREAMS = 8


def draw_resume_slot(key, part):
    incoming_count = N_STREAMS * CAP
    device_keys = jax.random.split(jax.random.fold_in(key, 11), N_STREAMS)
    orders = jax.vmap(lambda single: jax.random.permutation(single, S_DEV))(device_keys)
    incoming = orders[:, :incoming_count].astype(jnp.int32)
    full_device = jax.random.randint(jax.random.fold_in(key, 12), (), 0, N_STREAMS)
    device_ids = jnp.arange(N_STREAMS, dtype=jnp.int32)[:, None]
    offsets = jnp.where(device_ids == full_device, S_DEV - 1 - incoming[:, :1], 0)
    incoming = (incoming + offsets) % S_DEV
    coins = jax.random.randint(jax.random.fold_in(key, 13), (N_STREAMS, incoming_count), 0, 2)
    used = (coins == 1) | (device_ids == full_device)
    named = jnp.where(used, incoming, -1)
    named = named.reshape(N_STREAMS, N_STREAMS, CAP).transpose(1, 0, 2)
    return named.reshape(-1).astype(jnp.int32)


def levels(rng, dims, cuts, low, top_value):
    loudness, own = 1.0, jax.random.fold_in(rng, 6)
    for position, blocks in cuts:
        heights = jnp.exp(jax.random.uniform(jax.random.fold_in(own, position), (blocks,), jnp.float32, low / len(cuts), top_value / len(cuts)))
        loudness = loudness * jnp.repeat(heights, dims[position] // blocks).reshape([-1 if axis == position else 1 for axis in range(len(dims))])
    return loudness


def noise(key, shape, scale, bound, cuts=(), held_as=jnp.bfloat16):
    drawn = scale * jax.random.normal(key, shape, jnp.float32)
    if cuts:
        drawn = drawn * levels(key, shape, cuts, -0.22, 0.18)
    return jnp.clip(drawn, -bound, bound).astype(held_as)


def setup_inputs(seed: int = 0, part: int = 0) -> dict:
    streams_of = jax.random.split(jax.random.key(seed), 11)
    part_splits = jax.random.split(jax.random.fold_in(streams_of[10], part), 11)
    latent = noise(part_splits[0], (SESSIONS, D), 1.0, 6.0, ((0, 8), (1, 2)))
    conv_weight = noise(streams_of[1], (D, KERNEL, C1), D ** -0.5, 0.1875, ((0, 8), (2, 2)))
    conv_bias = noise(streams_of[2], (C1,), 0.5, 3.0, ((0, 2),), jnp.float32)
    tail_cache = noise(part_splits[3], (SLOTS, STRIDE, C1), 1.0, 6.0, ((0, 8), (2, 2)))
    input_cache = jnp.clip(-0.8984375 + 2.8984375 * jax.random.uniform(part_splits[4], (SLOTS, RES_K - 1, C1), jnp.float32) ** levels(part_splits[4], (SLOTS, RES_K - 1, C1), ((0, 8), (2, 2)), -0.2, 0.2), -0.8984375, 2.0).astype(jnp.bfloat16)
    resume_slot = draw_resume_slot(jax.random.fold_in(jax.random.fold_in(streams_of[10], part), 71), part)
    res_weight = noise(streams_of[6], (RES_K, C1, HID), (RES_K * C1) ** -0.5, 0.15625, ((1, 2),))
    res_bias = noise(streams_of[7], (HID,), 0.5, 3.0, (), jnp.float32)
    skip_weight = noise(streams_of[8], (HID, C1), HID ** -0.5, 0.375, ((1, 2),))
    skip_bias = noise(streams_of[9], (C1,), 0.5, 3.0, ((0, 2),), jnp.float32)
    return dict(latent=latent, conv_weight=conv_weight, conv_bias=conv_bias, tail_cache=tail_cache, input_cache=input_cache, resume_slot=resume_slot, res_weight=res_weight, res_bias=res_bias, skip_weight=skip_weight, skip_bias=skip_bias)


def apply_elu(values):
    return jnp.where(values > 0, values, jnp.expm1(jnp.minimum(values, 0.0)))


def reference(latent, conv_weight, conv_bias, tail_cache, input_cache, resume_slot, res_weight, res_bias, skip_weight, skip_bias):
    lanes = N_STREAMS
    portion = S_DEV // lanes
    ordered = latent.reshape(lanes, lanes, portion, D).transpose(1, 0, 2, 3).reshape(lanes, S_DEV, D)
    tails = tail_cache.reshape(lanes, lanes, CAP, STRIDE * C1).transpose(1, 0, 2, 3).reshape(lanes, lanes * CAP, STRIDE * C1)
    inputs = input_cache.reshape(lanes, lanes, CAP, (RES_K - 1) * C1).transpose(1, 0, 2, 3).reshape(lanes, lanes * CAP, (RES_K - 1) * C1)
    slots = resume_slot.reshape(lanes, lanes, CAP).transpose(1, 0, 2).reshape(lanes, lanes * CAP)
    kernel_flat = conv_weight.reshape(D, KERNEL * C1)
    positions = jnp.arange(S_DEV, dtype=jnp.int32)

    def one_block(block):
        rows_in, tail_rows, input_rows, slot_rows = block
        excitation = apply_elu(rows_in.astype(jnp.float32)).astype(jnp.bfloat16)
        spread = jnp.dot(excitation, kernel_flat, preferred_element_type=jnp.float32).reshape(S_DEV, KERNEL, C1)
        one_hot = (slot_rows[None, :] == positions[:, None]).astype(jnp.bfloat16)
        prev_tail = jnp.dot(one_hot, tail_rows, preferred_element_type=jnp.float32).reshape(S_DEV, STRIDE, C1)
        prev_input = jnp.dot(one_hot, input_rows, preferred_element_type=jnp.float32).reshape(S_DEV, RES_K - 1, C1)
        upsampled = spread[:, :STRIDE] + prev_tail + conv_bias
        carried = spread[:, STRIDE:].astype(jnp.bfloat16)
        excited = apply_elu(upsampled).astype(jnp.bfloat16)
        window = jnp.concatenate([prev_input.astype(jnp.bfloat16), excited], axis=1).astype(jnp.float32)
        branch = jnp.zeros((S_DEV, STRIDE, HID), jnp.float32) + res_bias
        for offset in range(RES_K):
            branch = branch + jnp.einsum("stc,ch->sth", window[:, offset:offset + STRIDE], res_weight[offset].astype(jnp.float32))
        hidden = apply_elu(branch).astype(jnp.bfloat16)
        mixed = upsampled + jnp.einsum("sth,hc->stc", hidden.astype(jnp.float32), skip_weight.astype(jnp.float32)) + skip_bias
        return mixed.astype(jnp.bfloat16), carried

    decoded, new_tail = lax.map(one_block, (ordered, tails, inputs, slots))
    return decoded.reshape(lanes * S_DEV, STRIDE, C1), new_tail.reshape(lanes * S_DEV, STRIDE, C1)
```

```python
import functools

import jax
import jax.numpy as jnp
from jax import lax
from jax.experimental import pallas as pl
from jax.experimental.pallas import tpu as pltpu
from jax.sharding import PartitionSpec as P

VMEM_LIMIT = 48 * 1024 * 1024
F32 = jnp.float32
BF16 = jnp.bfloat16


def apply_elu(values):
    return jnp.where(values > 0, values, jnp.exp(jnp.minimum(values, 0.0)) - 1.0)


def ring_order(count):
    return [2 * p if p < count // 2 else 2 * (count - 1 - p) + 1 for p in range(count)]


def ring_place(stream, count):
    return jnp.where(stream % 2 == 0, stream // 2, count - 1 - stream // 2)


def ring_stream(place, count):
    return jnp.where(place < count // 2, 2 * place, 2 * (count - 1 - place) + 1)


def spread_kernel(count, steps, *refs):
    blocks = refs[: len(steps)]
    near_ref, far_ref, home_ref, away_ref, kernel_rows, sems = refs[len(steps) :]
    rows = blocks[0].shape[1]
    place = ring_place(lax.axis_index("streams"), count)
    copies = []
    for slot, (step, block) in enumerate(zip(steps, blocks)):
        if step is None:
            target = kernel_rows
        else:
            stream = ring_stream(lax.rem(place + step + count, count), count)
            target = kernel_rows.at[:, pl.ds(pl.multiple_of(stream * rows, rows), rows), :]
        copy = pltpu.make_async_copy(block, target, sems.at[slot])
        copy.start()
        copies.append(copy)
    for copy in copies:
        copy.wait()

    @pl.loop(0, kernel_rows.shape[0])
    def _(tap):
        weights = kernel_rows[tap]
        home_ref[tap] = jnp.dot(near_ref[...], weights, preferred_element_type=F32).astype(
            home_ref.dtype
        )
        away_ref[tap] = jnp.dot(far_ref[...], weights, preferred_element_type=F32).astype(
            away_ref.dtype
        )


def spread_taps(near, far, blocks, steps, count, home_type):
    taps, _, width = blocks[0].shape
    sessions, depth = near.shape
    vmem = pl.BlockSpec(memory_space=pltpu.VMEM)
    return pl.pallas_call(
        functools.partial(spread_kernel, count, steps),
        out_shape=(
            jax.ShapeDtypeStruct((taps, sessions, width), home_type),
            jax.ShapeDtypeStruct((taps, sessions, width), BF16),
        ),
        in_specs=[pl.BlockSpec(memory_space=pl.ANY)] * len(blocks) + [vmem, vmem],
        out_specs=(vmem, vmem),
        scratch_shapes=[
            pltpu.VMEM((taps, depth, width), BF16),
            pltpu.SemaphoreType.DMA((len(blocks),)),
        ],
        compiler_params=pltpu.CompilerParams(vmem_limit_bytes=VMEM_LIMIT),
        cost_estimate=pl.CostEstimate(
            flops=4 * taps * sessions * depth * width,
            bytes_accessed=2 * taps * depth * width + 4 * sessions * depth + 6 * taps * sessions * width,
            transcendentals=0,
        ),
    )(*blocks, near, far)


def excite_kernel(group_ref, own_ref, other_ref, prev_ref, bias_ref, up_ref, window_ref):
    taps = own_ref.shape[0]
    bias = bias_ref[...]
    group = group_ref[0]
    history = prev_ref.shape[0] - 2 * taps
    for step in range(history):
        window_ref[step] = prev_ref[2 * taps + step]
    for half in range(2):
        for tap in range(taps):
            value = jnp.where(group == half, own_ref[tap], other_ref[tap].astype(F32))
            step = half * taps + tap
            up = value + prev_ref[step].astype(F32) + bias
            up_ref[step] = up
            window_ref[history + step] = apply_elu(up).astype(BF16)


def excite(group, own, other, prev, bias):
    taps, sessions, width = own.shape
    vmem = pl.BlockSpec(memory_space=pltpu.VMEM)
    return pl.pallas_call(
        excite_kernel,
        out_shape=(
            jax.ShapeDtypeStruct((2 * taps, sessions, width), F32),
            jax.ShapeDtypeStruct((prev.shape[0], sessions, width), BF16),
        ),
        in_specs=[pl.BlockSpec(memory_space=pltpu.SMEM), vmem, vmem, vmem, vmem],
        out_specs=(vmem, vmem),
        compiler_params=pltpu.CompilerParams(vmem_limit_bytes=VMEM_LIMIT),
    )(group, own, other, prev, bias)


def residual_kernel(
    up_ref, mine_ref, theirs_ref, res_mine_ref, res_theirs_ref, res_bias_ref, skip_ref, skip_bias_ref, out_ref
):
    @pl.loop(0, up_ref.shape[0])
    def _(step):
        branch = jnp.zeros(up_ref.shape[1:2] + res_mine_ref.shape[2:], F32)
        for offset in range(res_mine_ref.shape[0]):
            branch += jnp.dot(
                mine_ref[step + offset], res_mine_ref[offset], preferred_element_type=F32
            )
            branch += jnp.dot(
                theirs_ref[step + offset], res_theirs_ref[offset], preferred_element_type=F32
            )
        hidden = apply_elu(branch + res_bias_ref[...]).astype(BF16)
        projected = jnp.dot(hidden, skip_ref[...], preferred_element_type=F32)
        out_ref[step] = (up_ref[step] + projected + skip_bias_ref[...]).astype(BF16)


def residual(up, mine, theirs, res_mine, res_theirs, res_bias, skip_weight, skip_bias):
    vmem = pl.BlockSpec(memory_space=pltpu.VMEM)
    return pl.pallas_call(
        residual_kernel,
        out_shape=jax.ShapeDtypeStruct(up.shape, BF16),
        in_specs=[vmem] * 8,
        out_specs=vmem,
        compiler_params=pltpu.CompilerParams(vmem_limit_bytes=VMEM_LIMIT),
    )(up, mine, theirs, res_mine, res_theirs, res_bias, skip_weight, skip_bias)


def swap(value, axis):
    return lax.ppermute(value, axis, [(0, 1), (1, 0)])


def local(
    count,
    latent,
    conv_weight,
    conv_bias,
    tail_cache,
    input_cache,
    resume_slot,
    res_weight,
    res_bias,
    skip_weight,
    skip_bias,
):
    group = lax.axis_index("groups")
    rows, tap_count, width = conv_weight.shape
    sessions = latent.shape[0]
    taps = tap_count // 4

    halves = []
    for first in (0, tap_count // 2):
        part = lax.dynamic_slice_in_dim(conv_weight, first + group * taps, taps, axis=1)
        halves.append(part.transpose(1, 0, 2))

    portion = sessions // count
    cap = tail_cache.shape[0] // count
    half_taps, history = tail_cache.shape[1], input_cache.shape[1]
    slot_step = jnp.broadcast_to(
        resume_slot.astype(BF16)[:, None, None], (count * cap, 1, width)
    )
    filler = jnp.zeros((count * cap, half_taps - history - 1, width), BF16)
    beside = jnp.concatenate([input_cache, slot_step, filler], axis=1)
    stored = jnp.concatenate([tail_cache, beside], axis=2).reshape(count, cap * half_taps, 2 * width)
    parcel = jnp.concatenate([latent.reshape(count, portion, 2 * width), stored], axis=1)
    parcel = lax.all_to_all(parcel, "streams", split_axis=0, concat_axis=0, tiled=True)
    handed = parcel[:, :portion].reshape(sessions, 2 * width)
    stored = parcel[:, portion:].reshape(count * cap, half_taps, 2 * width)

    near_half = apply_elu(handed.astype(F32)).astype(BF16)
    far_half = swap(near_half, "groups")
    near = lax.all_gather(near_half, "segment", axis=1, tiled=True)
    far = lax.all_gather(far_half, "segment", axis=1, tiled=True)

    slots = stored[:, history, width:].astype(jnp.int32)[:, :1]
    one_hot = (slots == jnp.arange(sessions, dtype=jnp.int32)[None, :]).astype(BF16)
    packed = jnp.concatenate([stored[:, :, :width], stored[:, :history, width:]], axis=1)
    prev = jnp.einsum("js,jkc->ksc", one_hot, packed, preferred_element_type=F32).astype(BF16)

    res_theirs = swap(res_weight, "segment")

    if rows % 128 == 0 and count % 2 == 0:
        order = ring_order(count)
        onward = [(order[p], order[(p + 1) % count]) for p in range(count)]
        back = [(b, a) for a, b in onward]
        gathered = []
        for phase, own in enumerate(halves):
            blocks, steps = [own], [0]
            up_count = count // 2 - phase
            item = own
            ahead = own
            for r in range(1, count // 2 + 1):
                if r <= up_count:
                    item = lax.ppermute(item, "streams", onward)
                    blocks.append(item)
                    steps.append(-r)
                if r <= count - 1 - up_count:
                    ahead = lax.ppermute(ahead, "streams", back)
                    blocks.append(ahead)
                    steps.append(r)
            gathered.append((blocks, steps))
    else:
        gathered = [
            ([lax.all_gather(own, "streams", axis=1, tiled=True)], [None]) for own in halves
        ]

    own_up, away_up = spread_taps(near, far, *gathered[0], count, F32)
    other_up = swap(away_up, "groups")
    own_tail, away_tail = spread_taps(near, far, *gathered[1], count, BF16)
    other_tail = swap(away_tail, "groups")

    up, mine = excite(group[None].astype(jnp.int32), own_up, other_up, prev, conv_bias[None])
    theirs = swap(mine, "segment")
    decoded = residual(
        up, mine, theirs, res_weight, res_theirs, res_bias[None], skip_weight, skip_bias[None]
    )
    decoded = decoded.transpose(1, 0, 2)
    first = jnp.where(group == 0, own_tail, other_tail)
    second = jnp.where(group == 0, other_tail, own_tail)
    new_tail = jnp.concatenate([first, second], axis=0).transpose(1, 0, 2)
    return decoded, new_tail


def solution(mesh):
    placed = (
        P(("groups", "streams"), "segment"),
        P("streams", None, "segment"),
        P("segment"),
        P(("groups", "streams"), None, "segment"),
        P(("groups", "streams"), None, "segment"),
        P(("groups", "streams")),
        P(None, "segment", None),
        P(),
        P(None, "segment"),
        P("segment"),
    )
    return jax.shard_map(
        functools.partial(local, mesh.shape["streams"]),
        mesh=mesh,
        in_specs=placed,
        out_specs=(
            P(("groups", "streams"), None, "segment"),
            P(("groups", "streams"), None, "segment"),
        ),
        check_vma=False,
    )
```

```python
import functools

import jax
import jax.numpy as jnp
from jax import lax
from jax.experimental import pallas as pl
from jax.experimental.pallas import tpu as pltpu
from jax.sharding import PartitionSpec as P

VMEM_LIMIT = 48 * 1024 * 1024
F32 = jnp.float32
BF16 = jnp.bfloat16


def apply_elu(values):
    return jnp.where(values > 0, values, jnp.exp(jnp.minimum(values, 0.0)) - 1.0)


def ring_order(count):
    return [2 * p if p < count // 2 else 2 * (count - 1 - p) + 1 for p in range(count)]


def ring_place(stream, count):
    return jnp.where(stream % 2 == 0, stream // 2, count - 1 - stream // 2)


def ring_stream(place, count):
    return jnp.where(place < count // 2, 2 * place, 2 * (count - 1 - place) + 1)


def spread_kernel(count, steps, *refs):
    blocks = refs[: len(steps)]
    sides, (home_ref, away_ref) = refs[len(steps) : len(steps) + 4], refs[len(steps) + 4 : -3]
    kernel_rows, inputs, sems = refs[-3:]
    rows = blocks[0].shape[-2]
    place = ring_place(lax.axis_index("streams"), count)
    copies = []
    for step, block in zip(steps, blocks):
        if step is None:
            pieces = [
                (block.at[stream], kernel_rows.at[:, pl.ds(stream * rows, rows), :])
                for stream in range(count)
            ]
        else:
            stream = ring_stream(lax.rem(place + step + count, count), count)
            pieces = [
                (block, kernel_rows.at[:, pl.ds(pl.multiple_of(stream * rows, rows), rows), :])
            ]
        for source, target in pieces:
            copy = pltpu.make_async_copy(source, target, sems.at[len(copies)])
            copy.start()
            copies.append(copy)
    half = sides[0].shape[1]
    mine = lax.axis_index("segment")
    for index, side in enumerate(sides):
        column = mine if index % 2 == 0 else 1 - mine
        inputs[index // 2, :, pl.ds(pl.multiple_of(column * half, half), half)] = side[...]
    for copy in copies:
        copy.wait()

    @pl.loop(0, kernel_rows.shape[0])
    def _(tap):
        weights = kernel_rows[tap]
        home_ref[tap] = jnp.dot(inputs[0], weights, preferred_element_type=F32).astype(
            home_ref.dtype
        )
        away_ref[tap] = jnp.dot(inputs[1], weights, preferred_element_type=F32).astype(
            away_ref.dtype
        )


def spread_taps(sides, blocks, steps, count, home_type):
    taps, _, width = blocks[0].shape[-3:]
    sessions, depth = sides[0].shape[0], 2 * sides[0].shape[1]
    vmem = pl.BlockSpec(memory_space=pltpu.VMEM)
    return pl.pallas_call(
        functools.partial(spread_kernel, count, steps),
        out_shape=(
            jax.ShapeDtypeStruct((taps, sessions, width), home_type),
            jax.ShapeDtypeStruct((taps, sessions, width), BF16),
        ),
        in_specs=[pl.BlockSpec(memory_space=pl.ANY)] * len(blocks) + [vmem] * 4,
        out_specs=(vmem, vmem),
        scratch_shapes=[
            pltpu.VMEM((taps, depth, width), BF16),
            pltpu.VMEM((2, sessions, depth), BF16),
            pltpu.SemaphoreType.DMA((count,)),
        ],
        compiler_params=pltpu.CompilerParams(vmem_limit_bytes=VMEM_LIMIT),
        cost_estimate=pl.CostEstimate(
            flops=4 * taps * sessions * depth * width,
            bytes_accessed=2 * taps * depth * width + 4 * sessions * depth + 6 * taps * sessions * width,
            transcendentals=0,
        ),
    )(*blocks, *sides)


def excite_kernel(group_ref, own_ref, other_ref, prev_ref, bias_ref, up_ref, window_ref):
    taps = own_ref.shape[0]
    bias = bias_ref[...]
    group = group_ref[0]
    history = prev_ref.shape[0] - 2 * taps
    for step in range(history):
        window_ref[step] = prev_ref[2 * taps + step]
    for half in range(2):
        for tap in range(taps):
            value = jnp.where(group == half, own_ref[tap], other_ref[tap].astype(F32))
            step = half * taps + tap
            up = value + prev_ref[step].astype(F32) + bias
            up_ref[step] = up
            window_ref[history + step] = apply_elu(up).astype(BF16)


def excite(group, own, other, prev, bias):
    taps, sessions, width = own.shape
    vmem = pl.BlockSpec(memory_space=pltpu.VMEM)
    return pl.pallas_call(
        excite_kernel,
        out_shape=(
            jax.ShapeDtypeStruct((2 * taps, sessions, width), F32),
            jax.ShapeDtypeStruct((prev.shape[0], sessions, width), BF16),
        ),
        in_specs=[pl.BlockSpec(memory_space=pltpu.SMEM), vmem, vmem, vmem, vmem],
        out_specs=(vmem, vmem),
        compiler_params=pltpu.CompilerParams(vmem_limit_bytes=VMEM_LIMIT),
        cost_estimate=pl.CostEstimate(
            flops=20 * taps * sessions * width,
            bytes_accessed=40 * taps * sessions * width,
            transcendentals=2 * taps * sessions * width,
        ),
    )(group, own, other, prev, bias)


def residual_kernel(
    up_ref, mine_ref, theirs_ref, res_mine_ref, res_theirs_ref, res_bias_ref, skip_ref, skip_bias_ref, out_ref
):
    @pl.loop(0, up_ref.shape[0])
    def _(step):
        branch = jnp.zeros(up_ref.shape[1:2] + res_mine_ref.shape[2:], F32)
        for offset in range(res_mine_ref.shape[0]):
            branch += jnp.dot(
                mine_ref[step + offset], res_mine_ref[offset], preferred_element_type=F32
            )
            branch += jnp.dot(
                theirs_ref[step + offset], res_theirs_ref[offset], preferred_element_type=F32
            )
        hidden = apply_elu(branch + res_bias_ref[...]).astype(BF16)
        projected = jnp.dot(hidden, skip_ref[...], preferred_element_type=F32)
        out_ref[step] = (up_ref[step] + projected + skip_bias_ref[...]).astype(BF16)


def residual(up, mine, theirs, res_mine, res_theirs, res_bias, skip_weight, skip_bias):
    vmem = pl.BlockSpec(memory_space=pltpu.VMEM)
    return pl.pallas_call(
        residual_kernel,
        out_shape=jax.ShapeDtypeStruct(up.shape, BF16),
        in_specs=[vmem] * 8,
        out_specs=vmem,
        compiler_params=pltpu.CompilerParams(vmem_limit_bytes=VMEM_LIMIT),
        cost_estimate=pl.CostEstimate(
            flops=2 * up.size * (2 * res_mine.shape[0] + 1) * res_mine.shape[2],
            bytes_accessed=12 * up.size,
            transcendentals=up.size,
        ),
    )(up, mine, theirs, res_mine, res_theirs, res_bias, skip_weight, skip_bias)


def swap(value, axis):
    return lax.ppermute(value, axis, [(0, 1), (1, 0)])


def local(
    count,
    latent,
    conv_weight,
    conv_bias,
    tail_cache,
    input_cache,
    resume_slot,
    res_weight,
    res_bias,
    skip_weight,
    skip_bias,
):
    group = lax.axis_index("groups")
    rows, tap_count, width = conv_weight.shape
    sessions = latent.shape[0]
    taps = tap_count // 4

    halves = []
    for first in (0, tap_count // 2):
        part = lax.dynamic_slice_in_dim(conv_weight, first + group * taps, taps, axis=1)
        halves.append(part.transpose(1, 0, 2))

    portion = sessions // count
    cap = tail_cache.shape[0] // count
    half_taps, history = tail_cache.shape[1], input_cache.shape[1]
    slot_step = jnp.broadcast_to(
        resume_slot.astype(BF16)[:, None, None], (count * cap, 1, width)
    )
    filler = jnp.zeros((count * cap, half_taps - history - 1, width), BF16)
    beside = jnp.concatenate([input_cache, slot_step, filler], axis=1)
    stored = jnp.concatenate([tail_cache, beside], axis=2).reshape(count, cap * half_taps, 2 * width)
    parcel = jnp.concatenate([latent.reshape(count, portion, 2 * width), stored], axis=1)
    parcel = lax.all_to_all(parcel, "streams", split_axis=0, concat_axis=0, tiled=True)
    handed = parcel[:, :portion].reshape(sessions, 2 * width)
    stored = parcel[:, portion:].reshape(count * cap, half_taps, 2 * width)

    near_half = apply_elu(handed.astype(F32)).astype(BF16)
    far_half = swap(near_half, "groups")
    sides = (near_half, swap(near_half, "segment"), far_half, swap(far_half, "segment"))

    slots = stored[:, history, width:].astype(jnp.int32)[:, :1]
    one_hot = (slots == jnp.arange(sessions, dtype=jnp.int32)[None, :]).astype(BF16)
    packed = jnp.concatenate([stored[:, :, :width], stored[:, :history, width:]], axis=1)
    prev = jnp.einsum("js,jkc->ksc", one_hot, packed, preferred_element_type=F32).astype(BF16)

    res_theirs = swap(res_weight, "segment")

    def gather_all(own):
        return [lax.all_gather(own, "streams", axis=0)], [None]

    def gather_ring(own):
        order = ring_order(count)
        onward = [(order[p], order[(p + 1) % count]) for p in range(count)]
        back = [(b, a) for a, b in onward]
        blocks, steps = [own], [0]
        item = ahead = own
        for r in range(1, count // 2 + 1):
            item = lax.ppermute(item, "streams", onward)
            blocks.append(item)
            steps.append(-r)
            if 2 * r < count:
                ahead = lax.ppermute(ahead, "streams", back)
                blocks.append(ahead)
                steps.append(r)
        return blocks, steps

    use_ring = rows % 128 == 0 and count % 2 == 0
    gathered = [(gather_ring if use_ring else gather_all)(halves[0]), gather_all(halves[1])]

    own_up, away_up = spread_taps(sides, *gathered[0], count, F32)
    other_up = swap(away_up, "groups")
    own_tail, away_tail = spread_taps(sides, *gathered[1], count, BF16)
    other_tail = swap(away_tail, "groups")

    up, mine = excite(group[None].astype(jnp.int32), own_up, other_up, prev, conv_bias[None])
    theirs = swap(mine, "segment")
    decoded = residual(
        up, mine, theirs, res_weight, res_theirs, res_bias[None], skip_weight, skip_bias[None]
    )
    decoded = decoded.transpose(1, 0, 2)
    decoded, other_tail = lax.optimization_barrier((decoded, other_tail))
    first = jnp.where(group == 0, own_tail, other_tail)
    second = jnp.where(group == 0, other_tail, own_tail)
    new_tail = jnp.concatenate([first, second], axis=0).transpose(1, 0, 2)
    return decoded, new_tail


def solution(mesh):
    placed = (
        P(("groups", "streams"), "segment"),
        P("streams", None, "segment"),
        P("segment"),
        P(("groups", "streams"), None, "segment"),
        P(("groups", "streams"), None, "segment"),
        P(("groups", "streams")),
        P(None, "segment", None),
        P(),
        P(None, "segment"),
        P("segment"),
    )
    return jax.shard_map(
        functools.partial(local, mesh.shape["streams"]),
        mesh=mesh,
        in_specs=placed,
        out_specs=(
            P(("groups", "streams"), None, "segment"),
            P(("groups", "streams"), None, "segment"),
        ),
        check_vma=False,
    )
```

```python
import functools

import jax
import jax.numpy as jnp
from jax import lax
from jax.experimental import pallas as pl
from jax.experimental.pallas import tpu as pltpu
from jax.sharding import PartitionSpec as P

VMEM_LIMIT = 48 * 1024 * 1024
F32 = jnp.float32
BF16 = jnp.bfloat16
VMEM = pl.BlockSpec(memory_space=pltpu.VMEM)


def apply_elu(values):
    return jnp.where(values > 0, values, jnp.exp(jnp.minimum(values, 0.0)) - 1.0)


def ring_order(count):
    return [2 * p if p < count // 2 else 2 * (count - 1 - p) + 1 for p in range(count)]


def ring_place(stream, count):
    return jnp.where(stream % 2 == 0, stream // 2, count - 1 - stream // 2)


def ring_stream(place, count):
    return jnp.where(place < count // 2, 2 * place, 2 * (count - 1 - place) + 1)


def spread_kernel(count, steps, *refs):
    blocks = refs[: len(steps)]
    sides, (home_ref, away_ref) = refs[len(steps) : len(steps) + 4], refs[len(steps) + 4 : -3]
    kernel_rows, inputs, sems = refs[-3:]
    taps = kernel_rows.shape[0]
    rows = blocks[0].shape[-2]
    core = lax.axis_index("segment")
    place = ring_place(lax.axis_index("streams"), count)
    copies = []
    for slot, (step, block) in enumerate(zip(steps, blocks)):
        if step is None:
            source, target = block, kernel_rows
        else:
            distance, passed = step
            taker = 1 - core if passed else core
            stream = ring_stream(
                lax.rem(place + (2 * taker - 1) * distance + count, count), count
            )
            source = block if len(block.shape) == 3 else block.at[0]
            part = source.shape[0]
            first = 0 if part == taps else taker * part
            target = kernel_rows.at[
                pl.ds(first, part), pl.ds(pl.multiple_of(stream * rows, rows), rows), :
            ]
        copy = pltpu.make_async_copy(source, target, sems.at[slot])
        copy.start()
        copies.append(copy)
    half = sides[0].shape[1]
    for index, side in enumerate(sides):
        column = core if index % 2 == 0 else 1 - core
        inputs[index // 2, :, pl.ds(pl.multiple_of(column * half, half), half)] = side[...]
    for copy in copies:
        copy.wait()

    @pl.loop(0, taps)
    def _(tap):
        weights = kernel_rows[tap]
        home_ref[tap] = jnp.dot(inputs[0], weights, preferred_element_type=F32).astype(
            home_ref.dtype
        )
        away_ref[tap] = jnp.dot(inputs[1], weights, preferred_element_type=F32).astype(
            away_ref.dtype
        )


def spread_taps(sides, blocks, steps, count, home_type):
    taps, _, width = blocks[0].shape
    sessions, depth = sides[0].shape[0], 2 * sides[0].shape[1]
    return pl.pallas_call(
        functools.partial(spread_kernel, count, steps),
        out_shape=(
            jax.ShapeDtypeStruct((taps, sessions, width), home_type),
            jax.ShapeDtypeStruct((taps, sessions, width), BF16),
        ),
        in_specs=[pl.BlockSpec(memory_space=pl.ANY)] * len(blocks) + [VMEM] * 4,
        out_specs=(VMEM, VMEM),
        scratch_shapes=[
            pltpu.VMEM((taps, depth, width), BF16),
            pltpu.VMEM((2, sessions, depth), BF16),
            pltpu.SemaphoreType.DMA((len(blocks),)),
        ],
        compiler_params=pltpu.CompilerParams(vmem_limit_bytes=VMEM_LIMIT),
        cost_estimate=pl.CostEstimate(
            flops=4 * taps * sessions * depth * width,
            bytes_accessed=2 * taps * depth * width + 4 * sessions * depth + 6 * taps * sessions * width,
            transcendentals=0,
        ),
    )(*blocks, *sides)


def excite_kernel(group_ref, own_ref, other_ref, prev_ref, bias_ref, up_ref, window_ref):
    taps = own_ref.shape[0]
    bias = bias_ref[...]
    group = group_ref[0]
    history = prev_ref.shape[0] - 2 * taps
    for step in range(history):
        window_ref[step] = prev_ref[2 * taps + step]
    for half in range(2):
        for tap in range(taps):
            value = jnp.where(group == half, own_ref[tap], other_ref[tap].astype(F32))
            step = half * taps + tap
            up = value + prev_ref[step].astype(F32) + bias
            up_ref[step] = up
            window_ref[history + step] = apply_elu(up).astype(BF16)


def excite(group, own, other, prev, bias):
    taps, sessions, width = own.shape
    return pl.pallas_call(
        excite_kernel,
        out_shape=(
            jax.ShapeDtypeStruct((2 * taps, sessions, width), F32),
            jax.ShapeDtypeStruct((prev.shape[0], sessions, width), BF16),
        ),
        in_specs=[pl.BlockSpec(memory_space=pltpu.SMEM), VMEM, VMEM, VMEM, VMEM],
        out_specs=(VMEM, VMEM),
        compiler_params=pltpu.CompilerParams(vmem_limit_bytes=VMEM_LIMIT),
        cost_estimate=pl.CostEstimate(
            flops=20 * taps * sessions * width,
            bytes_accessed=40 * taps * sessions * width,
            transcendentals=2 * taps * sessions * width,
        ),
    )(group, own, other, prev, bias)


def residual_kernel(
    up_ref, mine_ref, theirs_ref, res_mine_ref, res_theirs_ref, res_bias_ref, skip_ref, skip_bias_ref, out_ref, frames
):
    steps, block, width = up_ref.shape
    branch = None
    for source, weights in ((mine_ref, res_mine_ref), (theirs_ref, res_theirs_ref)):
        for offset in range(weights.shape[0]):
            term = jnp.dot(
                source[offset : offset + steps].reshape(steps * block, width),
                weights[offset],
                preferred_element_type=F32,
            )
            branch = term if branch is None else branch + term
    hidden = apply_elu(branch + res_bias_ref[...]).astype(BF16)
    projected = jnp.dot(hidden, skip_ref[...], preferred_element_type=F32)
    mixed = up_ref[...] + projected.reshape(steps, block, width) + skip_bias_ref[...]
    for step in range(steps):
        for part in range(width // 128):
            frames.at[part][pl.ds(step, block, stride=steps), :] = mixed[
                step, :, part * 128 : (part + 1) * 128
            ]
    for part in range(width // 128):
        out_ref[:, part * 128 : (part + 1) * 128] = frames[part].astype(BF16)


def residual(up, mine, theirs, res_mine, res_theirs, res_bias, skip_weight, skip_bias):
    steps, sessions, width = up.shape
    window, block = mine.shape[0], sessions // 4
    frames = pl.BlockSpec((window, block, width), lambda i: (0, i, 0))
    return pl.pallas_call(
        residual_kernel,
        out_shape=jax.ShapeDtypeStruct((sessions * steps, width), BF16),
        grid=(4,),
        in_specs=[pl.BlockSpec((steps, block, width), lambda i: (0, i, 0)), frames, frames]
        + [VMEM] * 5,
        out_specs=pl.BlockSpec((block * steps, width), lambda i: (i, 0)),
        scratch_shapes=[pltpu.VMEM((width // 128, block * steps, 128), F32)],
        compiler_params=pltpu.CompilerParams(vmem_limit_bytes=VMEM_LIMIT),
        cost_estimate=pl.CostEstimate(
            flops=2 * up.size * (2 * res_mine.shape[0] + 1) * res_mine.shape[2],
            bytes_accessed=12 * up.size,
            transcendentals=up.size,
        ),
    )(up, mine, theirs, res_mine, res_theirs, res_bias, skip_weight, skip_bias)


def weave_kernel(group_ref, *refs):
    owns, others, (out_ref, frames) = refs[: len(refs) // 2 - 1], refs[len(refs) // 2 - 1 : -2], refs[-2:]
    group = group_ref[0]
    block, width = owns[0].shape[1:]
    steps = frames.shape[1] // block
    for half in range(2):
        step = half * steps // 2
        for own, other in zip(owns, others):
            for tap in range(own.shape[0]):
                value = jnp.where(group == half, own[tap].astype(F32), other[tap].astype(F32))
                for part in range(width // 128):
                    frames.at[part][pl.ds(step, block, stride=steps), :] = value[
                        :, part * 128 : (part + 1) * 128
                    ]
                step += 1
    for part in range(width // 128):
        out_ref[:, part * 128 : (part + 1) * 128] = frames[part].astype(BF16)


def weave(group, owns, others):
    sessions, width = owns[0].shape[1:]
    steps, block = 2 * sum(own.shape[0] for own in owns), sessions // 4
    taps = [
        pl.BlockSpec((own.shape[0], block, width), lambda i: (0, i, 0)) for own in owns + others
    ]
    return pl.pallas_call(
        weave_kernel,
        out_shape=jax.ShapeDtypeStruct((sessions * steps, width), BF16),
        grid=(4,),
        in_specs=[pl.BlockSpec(memory_space=pltpu.SMEM)] + taps,
        out_specs=pl.BlockSpec((block * steps, width), lambda i: (i, 0)),
        scratch_shapes=[pltpu.VMEM((width // 128, block * steps, 128), F32)],
        compiler_params=pltpu.CompilerParams(vmem_limit_bytes=VMEM_LIMIT),
        cost_estimate=pl.CostEstimate(
            flops=0, bytes_accessed=4 * sessions * steps * width, transcendentals=0
        ),
    )(group, *owns, *others)


def swap(value, axis):
    return lax.ppermute(value, axis, [(0, 1), (1, 0)])


def after(value, earlier):
    return lax.optimization_barrier((value, earlier))[0]


class Ring:
    def __init__(self, count, own, other):
        order = ring_order(count)
        self.count = count
        self.pairs = []
        for p in range(count):
            here, there = order[p], order[(p + 1) % count]
            self.pairs += [(2 * here, 2 * there), (2 * there + 1, 2 * here + 1)]
        self.item = jnp.stack([own, other])
        self.blocks, self.steps, self.rounds = [own], [(0, 0)], 0

    def round(self, earlier=None):
        self.rounds += 1
        item = self.item
        if 2 * self.rounds == self.count:
            part = item.shape[1] // 2
            item = lax.dynamic_slice_in_dim(item, lax.axis_index("segment") * part, part, axis=1)
        if earlier is not None:
            item = after(item, earlier)
        item = lax.ppermute(item, ("streams", "segment"), self.pairs)
        self.item = item
        self.blocks += [item, swap(item[1], "segment")]
        self.steps += [(self.rounds, 0), (self.rounds, 1)]
        return item


def local(
    count,
    latent,
    conv_weight,
    conv_bias,
    tail_cache,
    input_cache,
    resume_slot,
    res_weight,
    res_bias,
    skip_weight,
    skip_bias,
):
    group = lax.axis_index("groups")
    group_word = group[None].astype(jnp.int32)
    rows, tap_count, width = conv_weight.shape
    sessions = latent.shape[0]
    taps = tap_count // 4

    halves = []
    for first in (0, tap_count // 2):
        part = lax.dynamic_slice_in_dim(conv_weight, first + group * taps, taps, axis=1)
        halves.append(part.transpose(1, 0, 2))
    own = jnp.concatenate(halves, axis=0)
    cuts = ((0, taps), (taps, taps + taps // 2), (taps + taps // 2, 2 * taps))

    if rows % 128 == 0 and count % 2 == 0:
        other = swap(own, "segment")
        rings = [Ring(count, own[a:b], other[a:b]) for a, b in cuts]
        up_ring, first_ring, second_ring = rings
        first_done = up_ring.round()
        first_ring.round()
        last = first_done
        for r in range(2, count // 2 + 1):
            behind = last
            last = up_ring.round()
            first_ring.round()
            if r >= 3:
                second_ring.round(behind)
        while second_ring.rounds < count // 2:
            second_ring.round()
        gathered = [(ring.blocks, ring.steps) for ring in rings]
    else:
        gathered = [
            ([lax.all_gather(own[a:b], "streams", axis=1, tiled=True)], [None]) for a, b in cuts
        ]
        first_done = own

    portion = sessions // count
    cap = tail_cache.shape[0] // count
    half_taps, history = tail_cache.shape[1], input_cache.shape[1]
    slot_step = jnp.broadcast_to(
        resume_slot.astype(BF16)[:, None, None], (count * cap, 1, width)
    )
    filler = jnp.zeros((count * cap, half_taps - history - 1, width), BF16)
    beside = jnp.concatenate([input_cache, slot_step, filler], axis=1)
    stored = jnp.concatenate([tail_cache, beside], axis=2).reshape(count, cap * half_taps, 2 * width)
    parcel = jnp.concatenate([latent.reshape(count, portion, 2 * width), stored], axis=1)
    parcel = after(parcel, first_done)
    parcel = lax.all_to_all(parcel, "streams", split_axis=0, concat_axis=0, tiled=True)
    handed = parcel[:, :portion].reshape(sessions, 2 * width)
    stored = parcel[:, portion:].reshape(count * cap, half_taps, 2 * width)

    near_half = apply_elu(handed.astype(F32)).astype(BF16)
    far_half = swap(near_half, "groups")
    sides = (near_half, swap(near_half, "segment"), far_half, swap(far_half, "segment"))

    slots = stored[:, history, width:].astype(jnp.int32)[:, :1]
    one_hot = (slots == jnp.arange(sessions, dtype=jnp.int32)[None, :]).astype(BF16)
    packed = jnp.concatenate([stored[:, :, :width], stored[:, :history, width:]], axis=1)
    prev = jnp.einsum("js,jkc->ksc", one_hot, packed, preferred_element_type=F32).astype(BF16)

    res_theirs = swap(res_weight, "segment")

    own_up, away_up = spread_taps(sides, *gathered[0], count, F32)
    other_up = swap(away_up, "groups")
    owns, others = [], []
    for blocks, steps in gathered[1:]:
        own_tail, away_tail = spread_taps(sides, blocks, steps, count, BF16)
        owns.append(own_tail)
        others.append(swap(away_tail, "groups"))

    up, mine = excite(group_word, own_up, other_up, prev, conv_bias[None])
    theirs = swap(mine, "segment")
    decoded = residual(
        up, mine, theirs, res_weight, res_theirs, res_bias[None], skip_weight, skip_bias[None]
    )
    decoded, others[-1] = lax.optimization_barrier((decoded, others[-1]))
    new_tail = weave(group_word, owns, others)
    shape = (sessions, half_taps, width)
    return decoded.reshape(shape), new_tail.reshape(shape)


def solution(mesh):
    placed = (
        P(("groups", "streams"), "segment"),
        P("streams", None, "segment"),
        P("segment"),
        P(("groups", "streams"), None, "segment"),
        P(("groups", "streams"), None, "segment"),
        P(("groups", "streams")),
        P(None, "segment", None),
        P(),
        P(None, "segment"),
        P("segment"),
    )
    return jax.shard_map(
        functools.partial(local, mesh.shape["streams"]),
        mesh=mesh,
        in_specs=placed,
        out_specs=(
            P(("groups", "streams"), None, "segment"),
            P(("groups", "streams"), None, "segment"),
        ),
        check_vma=False,
    )
```

```python
import functools

import jax
import jax.numpy as jnp
from jax import lax
from jax.experimental import pallas as pl
from jax.experimental.pallas import tpu as pltpu
from jax.sharding import PartitionSpec as P

VMEM_LIMIT = 48 * 1024 * 1024
F32 = jnp.float32
BF16 = jnp.bfloat16
VMEM = pl.BlockSpec(memory_space=pltpu.VMEM)


def apply_elu(values):
    return jnp.where(values > 0, values, jnp.exp(jnp.minimum(values, 0.0)) - 1.0)


def ring_order(count):
    return [2 * p if p < count // 2 else 2 * (count - 1 - p) + 1 for p in range(count)]


def ring_place(stream, count):
    return jnp.where(stream % 2 == 0, stream // 2, count - 1 - stream // 2)


def ring_stream(place, count):
    return jnp.where(place < count // 2, 2 * place, 2 * (count - 1 - place) + 1)


def spread_kernel(count, steps, *refs):
    blocks = refs[: len(steps)]
    sides, (home_ref, away_ref) = refs[len(steps) : len(steps) + 4], refs[len(steps) + 4 : -3]
    kernel_rows, inputs, sems = refs[-3:]
    taps = kernel_rows.shape[0]
    rows = blocks[0].shape[-2]
    core = lax.axis_index("segment")
    place = ring_place(lax.axis_index("streams"), count)
    copies = []
    for slot, (step, block) in enumerate(zip(steps, blocks)):
        if step is None:
            source, target = block, kernel_rows
        else:
            distance, passed = step
            taker = 1 - core if passed else core
            stream = ring_stream(
                lax.rem(place + (2 * taker - 1) * distance + count, count), count
            )
            source = block if len(block.shape) == 3 else block.at[0]
            part = source.shape[0]
            first = 0 if part == taps else taker * part
            target = kernel_rows.at[
                pl.ds(first, part), pl.ds(pl.multiple_of(stream * rows, rows), rows), :
            ]
        copy = pltpu.make_async_copy(source, target, sems.at[slot])
        copy.start()
        copies.append(copy)
    half = sides[0].shape[1]
    for index, side in enumerate(sides):
        column = core if index % 2 == 0 else 1 - core
        inputs[index // 2, :, pl.ds(pl.multiple_of(column * half, half), half)] = side[...]
    for copy in copies:
        copy.wait()

    @pl.loop(0, taps)
    def _(tap):
        weights = kernel_rows[tap]
        home_ref[tap] = jnp.dot(inputs[0], weights, preferred_element_type=F32).astype(
            home_ref.dtype
        )
        away_ref[tap] = jnp.dot(inputs[1], weights, preferred_element_type=F32).astype(
            away_ref.dtype
        )


def spread_taps(sides, blocks, steps, count, home_type):
    taps, _, width = blocks[0].shape
    sessions, depth = sides[0].shape[0], 2 * sides[0].shape[1]
    return pl.pallas_call(
        functools.partial(spread_kernel, count, steps),
        out_shape=(
            jax.ShapeDtypeStruct((taps, sessions, width), home_type),
            jax.ShapeDtypeStruct((taps, sessions, width), BF16),
        ),
        in_specs=[pl.BlockSpec(memory_space=pl.ANY)] * len(blocks) + [VMEM] * 4,
        out_specs=(VMEM, VMEM),
        scratch_shapes=[
            pltpu.VMEM((taps, depth, width), BF16),
            pltpu.VMEM((2, sessions, depth), BF16),
            pltpu.SemaphoreType.DMA((len(blocks),)),
        ],
        compiler_params=pltpu.CompilerParams(vmem_limit_bytes=VMEM_LIMIT),
        cost_estimate=pl.CostEstimate(
            flops=4 * taps * sessions * depth * width,
            bytes_accessed=2 * taps * depth * width + 4 * sessions * depth + 6 * taps * sessions * width,
            transcendentals=0,
        ),
    )(*blocks, *sides)


def excite_kernel(group_ref, own_ref, other_ref, prev_ref, bias_ref, up_ref, window_ref):
    taps = own_ref.shape[0]
    bias = bias_ref[...]
    group = group_ref[0]
    history = prev_ref.shape[0] - 2 * taps
    for step in range(history):
        window_ref[step] = prev_ref[2 * taps + step]
    for half in range(2):
        for tap in range(taps):
            value = jnp.where(group == half, own_ref[tap], other_ref[tap].astype(F32))
            step = half * taps + tap
            up = value + prev_ref[step].astype(F32) + bias
            up_ref[step] = up
            window_ref[history + step] = apply_elu(up).astype(BF16)


def excite(group, own, other, prev, bias):
    taps, sessions, width = own.shape
    return pl.pallas_call(
        excite_kernel,
        out_shape=(
            jax.ShapeDtypeStruct((2 * taps, sessions, width), F32),
            jax.ShapeDtypeStruct((prev.shape[0], sessions, width), BF16),
        ),
        in_specs=[pl.BlockSpec(memory_space=pltpu.SMEM), VMEM, VMEM, VMEM, VMEM],
        out_specs=(VMEM, VMEM),
        compiler_params=pltpu.CompilerParams(vmem_limit_bytes=VMEM_LIMIT),
        cost_estimate=pl.CostEstimate(
            flops=20 * taps * sessions * width,
            bytes_accessed=40 * taps * sessions * width,
            transcendentals=2 * taps * sessions * width,
        ),
    )(group, own, other, prev, bias)


def residual_kernel(
    up_ref, mine_ref, theirs_ref, res_mine_ref, res_theirs_ref, res_bias_ref, skip_ref, skip_bias_ref, out_ref, frames
):
    steps, block, width = up_ref.shape
    branch = None
    for source, weights in ((mine_ref, res_mine_ref), (theirs_ref, res_theirs_ref)):
        for offset in range(weights.shape[0]):
            term = jnp.dot(
                source[offset : offset + steps].reshape(steps * block, width),
                weights[offset],
                preferred_element_type=F32,
            )
            branch = term if branch is None else branch + term
    hidden = apply_elu(branch + res_bias_ref[...]).astype(BF16)
    projected = jnp.dot(hidden, skip_ref[...], preferred_element_type=F32)
    mixed = up_ref[...] + projected.reshape(steps, block, width) + skip_bias_ref[...]
    for step in range(steps):
        for part in range(width // 128):
            frames.at[part][pl.ds(step, block, stride=steps), :] = mixed[
                step, :, part * 128 : (part + 1) * 128
            ]
    for part in range(width // 128):
        out_ref[:, part * 128 : (part + 1) * 128] = frames[part].astype(BF16)


def residual(up, mine, theirs, res_mine, res_theirs, res_bias, skip_weight, skip_bias):
    steps, sessions, width = up.shape
    window, block = mine.shape[0], sessions // 4
    frames = pl.BlockSpec((window, block, width), lambda i: (0, i, 0))
    return pl.pallas_call(
        residual_kernel,
        out_shape=jax.ShapeDtypeStruct((sessions * steps, width), BF16),
        grid=(4,),
        in_specs=[pl.BlockSpec((steps, block, width), lambda i: (0, i, 0)), frames, frames]
        + [VMEM] * 5,
        out_specs=pl.BlockSpec((block * steps, width), lambda i: (i, 0)),
        scratch_shapes=[pltpu.VMEM((width // 128, block * steps, 128), F32)],
        compiler_params=pltpu.CompilerParams(vmem_limit_bytes=VMEM_LIMIT),
        cost_estimate=pl.CostEstimate(
            flops=2 * up.size * (2 * res_mine.shape[0] + 1) * res_mine.shape[2],
            bytes_accessed=12 * up.size,
            transcendentals=up.size,
        ),
    )(up, mine, theirs, res_mine, res_theirs, res_bias, skip_weight, skip_bias)


def weave_kernel(group_ref, *refs):
    owns, others, (out_ref, frames) = refs[: len(refs) // 2 - 1], refs[len(refs) // 2 - 1 : -2], refs[-2:]
    group = group_ref[0]
    block, width = owns[0].shape[1:]
    steps = frames.shape[1] // block
    for half in range(2):
        step = half * steps // 2
        for own, other in zip(owns, others):
            for tap in range(own.shape[0]):
                value = jnp.where(group == half, own[tap].astype(F32), other[tap].astype(F32))
                for part in range(width // 128):
                    frames.at[part][pl.ds(step, block, stride=steps), :] = value[
                        :, part * 128 : (part + 1) * 128
                    ]
                step += 1
    for part in range(width // 128):
        out_ref[:, part * 128 : (part + 1) * 128] = frames[part].astype(BF16)


def weave(group, owns, others):
    sessions, width = owns[0].shape[1:]
    steps, block = 2 * sum(own.shape[0] for own in owns), sessions // 4
    taps = [
        pl.BlockSpec((own.shape[0], block, width), lambda i: (0, i, 0)) for own in owns + others
    ]
    return pl.pallas_call(
        weave_kernel,
        out_shape=jax.ShapeDtypeStruct((sessions * steps, width), BF16),
        grid=(4,),
        in_specs=[pl.BlockSpec(memory_space=pltpu.SMEM)] + taps,
        out_specs=pl.BlockSpec((block * steps, width), lambda i: (i, 0)),
        scratch_shapes=[pltpu.VMEM((width // 128, block * steps, 128), F32)],
        compiler_params=pltpu.CompilerParams(vmem_limit_bytes=VMEM_LIMIT),
        cost_estimate=pl.CostEstimate(
            flops=0, bytes_accessed=4 * sessions * steps * width, transcendentals=0
        ),
    )(group, *owns, *others)


def swap(value, axis):
    return lax.ppermute(value, axis, [(0, 1), (1, 0)])


def after(value, earlier):
    return lax.optimization_barrier((value, earlier))[0]


class Ring:
    def __init__(self, count, own, other):
        order = ring_order(count)
        self.count = count
        self.pairs = []
        for p in range(count):
            here, there = order[p], order[(p + 1) % count]
            self.pairs += [(2 * here, 2 * there), (2 * there + 1, 2 * here + 1)]
        self.item = jnp.stack([own, other])
        self.blocks, self.steps, self.rounds = [own], [(0, 0)], 0

    def round(self, earlier=None):
        self.rounds += 1
        item = self.item
        if 2 * self.rounds == self.count:
            part = item.shape[1] // 2
            item = lax.dynamic_slice_in_dim(item, lax.axis_index("segment") * part, part, axis=1)
        if earlier is not None:
            item = after(item, earlier)
        item = lax.ppermute(item, ("streams", "segment"), self.pairs)
        self.item = item
        self.blocks += [item, swap(item[1], "segment")]
        self.steps += [(self.rounds, 0), (self.rounds, 1)]
        return item


def local(
    count,
    latent,
    conv_weight,
    conv_bias,
    tail_cache,
    input_cache,
    resume_slot,
    res_weight,
    res_bias,
    skip_weight,
    skip_bias,
):
    group = lax.axis_index("groups")
    group_word = group[None].astype(jnp.int32)
    rows, tap_count, width = conv_weight.shape
    sessions = latent.shape[0]
    taps = tap_count // 4

    halves = []
    for first in (0, tap_count // 2):
        part = lax.dynamic_slice_in_dim(conv_weight, first + group * taps, taps, axis=1)
        halves.append(part.transpose(1, 0, 2))
    own = jnp.concatenate(halves, axis=0)
    cuts = ((0, taps), (taps, 2 * taps))

    if False:
        other = swap(own, "segment")
        rings = [Ring(count, own[a:b], other[a:b]) for a, b in cuts]
        up_ring, first_ring, second_ring = rings
        first_done = up_ring.round()
        first_ring.round()
        last = first_done
        for r in range(2, count // 2 + 1):
            behind = last
            last = up_ring.round()
            first_ring.round()
            if r >= 3:
                second_ring.round(behind)
        while second_ring.rounds < count // 2:
            second_ring.round()
        gathered = [(ring.blocks, ring.steps) for ring in rings]
    else:
        gathered = [
            ([lax.all_gather(own[a:b], "streams", axis=1, tiled=True)], [None]) for a, b in cuts
        ]
        first_done = own

    portion = sessions // count
    cap = tail_cache.shape[0] // count
    half_taps, history = tail_cache.shape[1], input_cache.shape[1]
    slot_step = jnp.broadcast_to(
        resume_slot.astype(BF16)[:, None, None], (count * cap, 1, width)
    )
    filler = jnp.zeros((count * cap, half_taps - history - 1, width), BF16)
    beside = jnp.concatenate([input_cache, slot_step, filler], axis=1)
    stored = jnp.concatenate([tail_cache, beside], axis=2).reshape(count, cap * half_taps, 2 * width)
    parcel = jnp.concatenate([latent.reshape(count, portion, 2 * width), stored], axis=1)
    parcel = after(parcel, first_done)
    parcel = lax.all_to_all(parcel, "streams", split_axis=0, concat_axis=0, tiled=True)
    handed = parcel[:, :portion].reshape(sessions, 2 * width)
    stored = parcel[:, portion:].reshape(count * cap, half_taps, 2 * width)

    near_half = apply_elu(handed.astype(F32)).astype(BF16)
    far_half = swap(near_half, "groups")
    sides = (near_half, swap(near_half, "segment"), far_half, swap(far_half, "segment"))

    slots = stored[:, history, width:].astype(jnp.int32)[:, :1]
    one_hot = (slots == jnp.arange(sessions, dtype=jnp.int32)[None, :]).astype(BF16)
    packed = jnp.concatenate([stored[:, :, :width], stored[:, :history, width:]], axis=1)
    prev = jnp.einsum("js,jkc->ksc", one_hot, packed, preferred_element_type=F32).astype(BF16)

    res_theirs = swap(res_weight, "segment")

    own_up, away_up = spread_taps(sides, *gathered[0], count, F32)
    other_up = swap(away_up, "groups")
    owns, others = [], []
    for blocks, steps in gathered[1:]:
        own_tail, away_tail = spread_taps(sides, blocks, steps, count, BF16)
        owns.append(own_tail)
        others.append(swap(away_tail, "groups"))

    up, mine = excite(group_word, own_up, other_up, prev, conv_bias[None])
    theirs = swap(mine, "segment")
    decoded = residual(
        up, mine, theirs, res_weight, res_theirs, res_bias[None], skip_weight, skip_bias[None]
    )
    decoded, others[-1] = lax.optimization_barrier((decoded, others[-1]))
    new_tail = weave(group_word, owns, others)
    shape = (sessions, half_taps, width)
    return decoded.reshape(shape), new_tail.reshape(shape)


def solution(mesh):
    placed = (
        P(("groups", "streams"), "segment"),
        P("streams", None, "segment"),
        P("segment"),
        P(("groups", "streams"), None, "segment"),
        P(("groups", "streams"), None, "segment"),
        P(("groups", "streams")),
        P(None, "segment", None),
        P(),
        P(None, "segment"),
        P("segment"),
    )
    return jax.shard_map(
        functools.partial(local, mesh.shape["streams"]),
        mesh=mesh,
        in_specs=placed,
        out_specs=(
            P(("groups", "streams"), None, "segment"),
            P(("groups", "streams"), None, "segment"),
        ),
        check_vma=False,
    )
```

```python
import functools

import jax
import jax.numpy as jnp
from jax import lax
from jax.experimental import pallas as pl
from jax.experimental.pallas import tpu as pltpu
from jax.sharding import PartitionSpec as P

VMEM_LIMIT = 48 * 1024 * 1024
F32 = jnp.float32
BF16 = jnp.bfloat16
VMEM = pl.BlockSpec(memory_space=pltpu.VMEM)


def apply_elu(values):
    return jnp.where(values > 0, values, jnp.exp(jnp.minimum(values, 0.0)) - 1.0)


def ring_order(count):
    return [2 * p if p < count // 2 else 2 * (count - 1 - p) + 1 for p in range(count)]


def ring_place(stream, count):
    return jnp.where(stream % 2 == 0, stream // 2, count - 1 - stream // 2)


def ring_stream(place, count):
    return jnp.where(place < count // 2, 2 * place, 2 * (count - 1 - place) + 1)


def spread_kernel(count, steps, *refs):
    blocks = refs[: len(steps)]
    sides, (home_ref, away_ref) = refs[len(steps) : len(steps) + 4], refs[len(steps) + 4 : -3]
    kernel_rows, inputs, sems = refs[-3:]
    taps = kernel_rows.shape[0]
    rows = blocks[0].shape[-2]
    core = lax.axis_index("segment")
    place = ring_place(lax.axis_index("streams"), count)
    copies = []
    for slot, (step, block) in enumerate(zip(steps, blocks)):
        if step is None:
            source, target = block, kernel_rows
        else:
            distance, passed = step
            taker = 1 - core if passed else core
            stream = ring_stream(
                lax.rem(place + (2 * taker - 1) * distance + count, count), count
            )
            source = block if len(block.shape) == 3 else block.at[0]
            part = source.shape[0]
            first = 0 if part == taps else taker * part
            target = kernel_rows.at[
                pl.ds(first, part), pl.ds(pl.multiple_of(stream * rows, rows), rows), :
            ]
        copy = pltpu.make_async_copy(source, target, sems.at[slot])
        copy.start()
        copies.append(copy)
    half = sides[0].shape[1]
    for index, side in enumerate(sides):
        column = core if index % 2 == 0 else 1 - core
        inputs[index // 2, :, pl.ds(pl.multiple_of(column * half, half), half)] = side[...]
    for copy in copies:
        copy.wait()

    @pl.loop(0, taps)
    def _(tap):
        weights = kernel_rows[tap]
        home_ref[tap] = jnp.dot(inputs[0], weights, preferred_element_type=F32).astype(
            home_ref.dtype
        )
        away_ref[tap] = jnp.dot(inputs[1], weights, preferred_element_type=F32).astype(
            away_ref.dtype
        )


def spread_taps(sides, blocks, steps, count, home_type):
    taps, _, width = blocks[0].shape
    sessions, depth = sides[0].shape[0], 2 * sides[0].shape[1]
    return pl.pallas_call(
        functools.partial(spread_kernel, count, steps),
        out_shape=(
            jax.ShapeDtypeStruct((taps, sessions, width), home_type),
            jax.ShapeDtypeStruct((taps, sessions, width), BF16),
        ),
        in_specs=[pl.BlockSpec(memory_space=pl.ANY)] * len(blocks) + [VMEM] * 4,
        out_specs=(VMEM, VMEM),
        scratch_shapes=[
            pltpu.VMEM((taps, depth, width), BF16),
            pltpu.VMEM((2, sessions, depth), BF16),
            pltpu.SemaphoreType.DMA((len(blocks),)),
        ],
        compiler_params=pltpu.CompilerParams(vmem_limit_bytes=VMEM_LIMIT),
        cost_estimate=pl.CostEstimate(
            flops=4 * taps * sessions * depth * width,
            bytes_accessed=2 * taps * depth * width + 4 * sessions * depth + 6 * taps * sessions * width,
            transcendentals=0,
        ),
    )(*blocks, *sides)


def excite_kernel(group_ref, own_ref, other_ref, prev_ref, bias_ref, up_ref, window_ref):
    taps = own_ref.shape[0]
    bias = bias_ref[...]
    group = group_ref[0]
    history = prev_ref.shape[0] - 2 * taps
    for step in range(history):
        window_ref[step] = prev_ref[2 * taps + step]
    for half in range(2):
        for tap in range(taps):
            value = jnp.where(group == half, own_ref[tap], other_ref[tap].astype(F32))
            step = half * taps + tap
            up = value + prev_ref[step].astype(F32) + bias
            up_ref[step] = up
            window_ref[history + step] = apply_elu(up).astype(BF16)


def excite(group, own, other, prev, bias):
    taps, sessions, width = own.shape
    return pl.pallas_call(
        excite_kernel,
        out_shape=(
            jax.ShapeDtypeStruct((2 * taps, sessions, width), F32),
            jax.ShapeDtypeStruct((prev.shape[0], sessions, width), BF16),
        ),
        in_specs=[pl.BlockSpec(memory_space=pltpu.SMEM), VMEM, VMEM, VMEM, VMEM],
        out_specs=(VMEM, VMEM),
        compiler_params=pltpu.CompilerParams(vmem_limit_bytes=VMEM_LIMIT),
        cost_estimate=pl.CostEstimate(
            flops=20 * taps * sessions * width,
            bytes_accessed=40 * taps * sessions * width,
            transcendentals=2 * taps * sessions * width,
        ),
    )(group, own, other, prev, bias)


def residual_kernel(
    up_ref, mine_ref, theirs_ref, res_mine_ref, res_theirs_ref, res_bias_ref, skip_ref, skip_bias_ref, out_ref, frames
):
    steps, block, width = up_ref.shape
    branch = None
    for source, weights in ((mine_ref, res_mine_ref), (theirs_ref, res_theirs_ref)):
        for offset in range(weights.shape[0]):
            term = jnp.dot(
                source[offset : offset + steps].reshape(steps * block, width),
                weights[offset],
                preferred_element_type=F32,
            )
            branch = term if branch is None else branch + term
    hidden = apply_elu(branch + res_bias_ref[...]).astype(BF16)
    projected = jnp.dot(hidden, skip_ref[...], preferred_element_type=F32)
    mixed = up_ref[...] + projected.reshape(steps, block, width) + skip_bias_ref[...]
    for step in range(steps):
        for part in range(width // 128):
            frames.at[part][pl.ds(step, block, stride=steps), :] = mixed[
                step, :, part * 128 : (part + 1) * 128
            ]
    for part in range(width // 128):
        out_ref[:, part * 128 : (part + 1) * 128] = frames[part].astype(BF16)


def residual(up, mine, theirs, res_mine, res_theirs, res_bias, skip_weight, skip_bias):
    steps, sessions, width = up.shape
    window, block = mine.shape[0], sessions // 4
    frames = pl.BlockSpec((window, block, width), lambda i: (0, i, 0))
    return pl.pallas_call(
        residual_kernel,
        out_shape=jax.ShapeDtypeStruct((sessions * steps, width), BF16),
        grid=(4,),
        in_specs=[pl.BlockSpec((steps, block, width), lambda i: (0, i, 0)), frames, frames]
        + [VMEM] * 5,
        out_specs=pl.BlockSpec((block * steps, width), lambda i: (i, 0)),
        scratch_shapes=[pltpu.VMEM((width // 128, block * steps, 128), F32)],
        compiler_params=pltpu.CompilerParams(vmem_limit_bytes=VMEM_LIMIT),
        cost_estimate=pl.CostEstimate(
            flops=2 * up.size * (2 * res_mine.shape[0] + 1) * res_mine.shape[2],
            bytes_accessed=12 * up.size,
            transcendentals=up.size,
        ),
    )(up, mine, theirs, res_mine, res_theirs, res_bias, skip_weight, skip_bias)


def weave_kernel(group_ref, own_ref, other_ref, out_ref, frames):
    group = group_ref[0]
    taps, block, width = own_ref.shape
    for half in range(2):
        for tap in range(taps):
            value = jnp.where(
                group == half, own_ref[tap].astype(F32), other_ref[tap].astype(F32)
            )
            step = half * taps + tap
            for part in range(width // 128):
                frames.at[part][pl.ds(step, block, stride=2 * taps), :] = value[
                    :, part * 128 : (part + 1) * 128
                ]
    for part in range(width // 128):
        out_ref[:, part * 128 : (part + 1) * 128] = frames[part].astype(BF16)


def weave(group, own, other):
    taps, sessions, width = own.shape
    steps, block = 2 * taps, sessions // 4
    part = pl.BlockSpec((taps, block, width), lambda i: (0, i, 0))
    return pl.pallas_call(
        weave_kernel,
        out_shape=jax.ShapeDtypeStruct((sessions * steps, width), BF16),
        grid=(4,),
        in_specs=[pl.BlockSpec(memory_space=pltpu.SMEM), part, part],
        out_specs=pl.BlockSpec((block * steps, width), lambda i: (i, 0)),
        scratch_shapes=[pltpu.VMEM((width // 128, block * steps, 128), F32)],
        compiler_params=pltpu.CompilerParams(vmem_limit_bytes=VMEM_LIMIT),
        cost_estimate=pl.CostEstimate(
            flops=0, bytes_accessed=4 * sessions * steps * width, transcendentals=0
        ),
    )(group, own, other)


def swap(value, axis):
    return lax.ppermute(value, axis, [(0, 1), (1, 0)])


def after(value, earlier):
    return lax.optimization_barrier((value, earlier))[0]


class Ring:
    def __init__(self, count, own, other):
        order = ring_order(count)
        self.count = count
        self.pairs = []
        for p in range(count):
            here, there = order[p], order[(p + 1) % count]
            self.pairs += [(2 * here, 2 * there), (2 * there + 1, 2 * here + 1)]
        self.item = jnp.stack([own, other])
        self.blocks, self.steps, self.rounds = [own], [(0, 0)], 0

    def round(self, earlier=None):
        self.rounds += 1
        item = self.item
        if 2 * self.rounds == self.count:
            part = item.shape[1] // 2
            item = lax.dynamic_slice_in_dim(item, lax.axis_index("segment") * part, part, axis=1)
        if earlier is not None:
            item = after(item, earlier)
        item = lax.ppermute(item, ("streams", "segment"), self.pairs)
        self.item = item
        self.blocks += [item, swap(item[1], "segment")]
        self.steps += [(self.rounds, 0), (self.rounds, 1)]
        return item


def local(
    count,
    latent,
    conv_weight,
    conv_bias,
    tail_cache,
    input_cache,
    resume_slot,
    res_weight,
    res_bias,
    skip_weight,
    skip_bias,
):
    group = lax.axis_index("groups")
    group_word = group[None].astype(jnp.int32)
    rows, tap_count, width = conv_weight.shape
    sessions = latent.shape[0]
    taps = tap_count // 4

    halves = []
    for first in (0, tap_count // 2):
        part = lax.dynamic_slice_in_dim(conv_weight, first + group * taps, taps, axis=1)
        halves.append(part.transpose(1, 0, 2))
    own = jnp.concatenate(halves, axis=0)
    cuts = ((0, taps), (taps, 2 * taps))

    if rows % 128 == 0 and count % 2 == 0:
        other = swap(own, "segment")
        rings = [Ring(count, own[a:b], other[a:b]) for a, b in cuts]
        up_ring, tail_ring = rings
        first_done = up_ring.round()
        behind = None
        for _ in range(2, count // 2 + 1):
            ahead = up_ring.round(behind)
            behind = tail_ring.round(behind_of_ahead) if tail_ring.rounds else tail_ring.round()
            behind_of_ahead = ahead
        nearly_done = behind
        tail_ring.round(behind_of_ahead)
        gathered = [(ring.blocks, ring.steps) for ring in rings]
    else:
        gathered = [
            ([lax.all_gather(own[a:b], "streams", axis=1, tiled=True)], [None]) for a, b in cuts
        ]
        first_done = nearly_done = own

    portion = sessions // count
    cap = tail_cache.shape[0] // count
    half_taps, history = tail_cache.shape[1], input_cache.shape[1]
    slot_step = jnp.broadcast_to(
        resume_slot.astype(BF16)[:, None, None], (count * cap, 1, width)
    )
    filler = jnp.zeros((count * cap, half_taps - history - 1, width), BF16)
    beside = jnp.concatenate([input_cache, slot_step, filler], axis=1)
    stored = jnp.concatenate([tail_cache, beside], axis=2).reshape(count, cap * half_taps, 2 * width)
    parcel = jnp.concatenate([latent.reshape(count, portion, 2 * width), stored], axis=1)
    parcel = after(parcel, first_done)
    parcel = lax.all_to_all(parcel, "streams", split_axis=0, concat_axis=0, tiled=True)
    handed = parcel[:, :portion].reshape(sessions, 2 * width)
    stored = parcel[:, portion:].reshape(count * cap, half_taps, 2 * width)

    near_half = apply_elu(handed.astype(F32)).astype(BF16)
    far_half = swap(near_half, "groups")
    sides = (near_half, swap(near_half, "segment"), far_half, swap(far_half, "segment"))

    slots = stored[:, history, width:].astype(jnp.int32)[:, :1]
    one_hot = (slots == jnp.arange(sessions, dtype=jnp.int32)[None, :]).astype(BF16)
    packed = jnp.concatenate([stored[:, :, :width], stored[:, :history, width:]], axis=1)
    prev = jnp.einsum("js,jkc->ksc", one_hot, packed, preferred_element_type=F32).astype(BF16)

    res_theirs = swap(res_weight, "segment")

    own_up, away_up = spread_taps(sides, *gathered[0], count, F32)
    other_up = swap(after(away_up, nearly_done), "groups")
    own_tail, away_tail = spread_taps(sides, *gathered[1], count, BF16)
    other_tail = swap(away_tail, "groups")

    own_up = after(own_up, away_tail)
    up, mine = excite(group_word, own_up, other_up, prev, conv_bias[None])
    theirs = swap(mine, "segment")
    decoded = residual(
        up, mine, theirs, res_weight, res_theirs, res_bias[None], skip_weight, skip_bias[None]
    )
    decoded, other_tail = lax.optimization_barrier((decoded, other_tail))
    new_tail = weave(group_word, own_tail, other_tail)
    shape = (sessions, half_taps, width)
    return decoded.reshape(shape), new_tail.reshape(shape)


def solution(mesh):
    placed = (
        P(("groups", "streams"), "segment"),
        P("streams", None, "segment"),
        P("segment"),
        P(("groups", "streams"), None, "segment"),
        P(("groups", "streams"), None, "segment"),
        P(("groups", "streams")),
        P(None, "segment", None),
        P(),
        P(None, "segment"),
        P("segment"),
    )
    return jax.shard_map(
        functools.partial(local, mesh.shape["streams"]),
        mesh=mesh,
        in_specs=placed,
        out_specs=(
            P(("groups", "streams"), None, "segment"),
            P(("groups", "streams"), None, "segment"),
        ),
        check_vma=False,
    )
```

```python
import functools

import jax
import jax.numpy as jnp
from jax import lax
from jax.experimental import pallas as pl
from jax.experimental.pallas import tpu as pltpu
from jax.sharding import PartitionSpec as P

VMEM_LIMIT = 48 * 1024 * 1024
F32 = jnp.float32
BF16 = jnp.bfloat16
VMEM = pl.BlockSpec(memory_space=pltpu.VMEM)


def apply_elu(values):
    return jnp.where(values > 0, values, jnp.exp(jnp.minimum(values, 0.0)) - 1.0)


def ring_order(count):
    return [2 * p if p < count // 2 else 2 * (count - 1 - p) + 1 for p in range(count)]


def ring_place(stream, count):
    return jnp.where(stream % 2 == 0, stream // 2, count - 1 - stream // 2)


def ring_stream(place, count):
    return jnp.where(place < count // 2, 2 * place, 2 * (count - 1 - place) + 1)


def spread_kernel(count, steps, *refs):
    blocks = refs[: len(steps)]
    sides, (home_ref, away_ref) = refs[len(steps) : len(steps) + 4], refs[len(steps) + 4 : -3]
    kernel_rows, inputs, sems = refs[-3:]
    taps = kernel_rows.shape[0]
    rows = blocks[0].shape[-2]
    core = lax.axis_index("segment")
    place = ring_place(lax.axis_index("streams"), count)
    copies = []
    for slot, (step, block) in enumerate(zip(steps, blocks)):
        if step is None:
            source, target = block, kernel_rows
        else:
            distance, passed = step
            taker = 1 - core if passed else core
            stream = ring_stream(
                lax.rem(place + (2 * taker - 1) * distance + count, count), count
            )
            source = block if len(block.shape) == 3 else block.at[passed]
            part = source.shape[0]
            first = 0 if part == taps else taker * part
            target = kernel_rows.at[
                pl.ds(first, part), pl.ds(pl.multiple_of(stream * rows, rows), rows), :
            ]
        copy = pltpu.make_async_copy(source, target, sems.at[slot])
        copy.start()
        copies.append(copy)
    half = sides[0].shape[1]
    for index, side in enumerate(sides):
        column = core if index % 2 == 0 else 1 - core
        inputs[index // 2, :, pl.ds(pl.multiple_of(column * half, half), half)] = side[...]
    for copy in copies:
        copy.wait()

    @pl.loop(0, taps)
    def _(tap):
        weights = kernel_rows[tap]
        home_ref[tap] = jnp.dot(inputs[0], weights, preferred_element_type=F32).astype(
            home_ref.dtype
        )
        away_ref[tap] = jnp.dot(inputs[1], weights, preferred_element_type=F32).astype(
            away_ref.dtype
        )


def spread_taps(sides, blocks, steps, count, home_type):
    taps, _, width = blocks[0].shape
    sessions, depth = sides[0].shape[0], 2 * sides[0].shape[1]
    return pl.pallas_call(
        functools.partial(spread_kernel, count, steps),
        out_shape=(
            jax.ShapeDtypeStruct((taps, sessions, width), home_type),
            jax.ShapeDtypeStruct((taps, sessions, width), BF16),
        ),
        in_specs=[pl.BlockSpec(memory_space=pl.ANY)] * len(blocks) + [VMEM] * 4,
        out_specs=(VMEM, VMEM),
        scratch_shapes=[
            pltpu.VMEM((taps, depth, width), BF16),
            pltpu.VMEM((2, sessions, depth), BF16),
            pltpu.SemaphoreType.DMA((len(blocks),)),
        ],
        compiler_params=pltpu.CompilerParams(vmem_limit_bytes=VMEM_LIMIT),
    )(*blocks, *sides)


def excite_kernel(group_ref, own_ref, other_ref, prev_ref, bias_ref, up_ref, window_ref):
    taps = own_ref.shape[0]
    bias = bias_ref[...]
    group = group_ref[0]
    history = prev_ref.shape[0] - 2 * taps
    for step in range(history):
        window_ref[step] = prev_ref[2 * taps + step]
    for half in range(2):
        for tap in range(taps):
            value = jnp.where(group == half, own_ref[tap], other_ref[tap].astype(F32))
            step = half * taps + tap
            up = value + prev_ref[step].astype(F32) + bias
            up_ref[step] = up
            window_ref[history + step] = apply_elu(up).astype(BF16)


def excite(group, own, other, prev, bias):
    taps, sessions, width = own.shape
    return pl.pallas_call(
        excite_kernel,
        out_shape=(
            jax.ShapeDtypeStruct((2 * taps, sessions, width), F32),
            jax.ShapeDtypeStruct((prev.shape[0], sessions, width), BF16),
        ),
        in_specs=[pl.BlockSpec(memory_space=pltpu.SMEM), VMEM, VMEM, VMEM, VMEM],
        out_specs=(VMEM, VMEM),
        compiler_params=pltpu.CompilerParams(vmem_limit_bytes=VMEM_LIMIT),
    )(group, own, other, prev, bias)


def residual_kernel(
    up_ref, mine_ref, theirs_ref, res_mine_ref, res_theirs_ref, res_bias_ref, skip_ref, skip_bias_ref, out_ref, frames
):
    steps, block, width = up_ref.shape
    branch = None
    for source, weights in ((mine_ref, res_mine_ref), (theirs_ref, res_theirs_ref)):
        for offset in range(weights.shape[0]):
            term = jnp.dot(
                source[offset : offset + steps].reshape(steps * block, width),
                weights[offset],
                preferred_element_type=F32,
            )
            branch = term if branch is None else branch + term
    hidden = apply_elu(branch + res_bias_ref[...]).astype(BF16)
    projected = jnp.dot(hidden, skip_ref[...], preferred_element_type=F32)
    mixed = up_ref[...] + projected.reshape(steps, block, width) + skip_bias_ref[...]
    for step in range(steps):
        for part in range(width // 128):
            frames.at[part][pl.ds(step, block, stride=steps), :] = mixed[
                step, :, part * 128 : (part + 1) * 128
            ]
    for part in range(width // 128):
        out_ref[:, part * 128 : (part + 1) * 128] = frames[part].astype(BF16)


def residual(up, mine, theirs, res_mine, res_theirs, res_bias, skip_weight, skip_bias):
    steps, sessions, width = up.shape
    window, block = mine.shape[0], sessions // 4
    frames = pl.BlockSpec((window, block, width), lambda i: (0, i, 0))
    return pl.pallas_call(
        residual_kernel,
        out_shape=jax.ShapeDtypeStruct((sessions * steps, width), BF16),
        grid=(4,),
        in_specs=[pl.BlockSpec((steps, block, width), lambda i: (0, i, 0)), frames, frames]
        + [VMEM] * 5,
        out_specs=pl.BlockSpec((block * steps, width), lambda i: (i, 0)),
        scratch_shapes=[pltpu.VMEM((width // 128, block * steps, 128), F32)],
        compiler_params=pltpu.CompilerParams(vmem_limit_bytes=VMEM_LIMIT),
    )(up, mine, theirs, res_mine, res_theirs, res_bias, skip_weight, skip_bias)


def weave_kernel(group_ref, *refs):
    owns, others = refs[: len(refs) // 2 - 1], refs[len(refs) // 2 - 1 : -2]
    out_ref, frames = refs[-2:]
    group = group_ref[0]
    block, width = owns[0].shape[1:]
    steps = frames.shape[1] // block
    for half in range(2):
        step = half * steps // 2
        for own, other in zip(owns, others):
            for tap in range(own.shape[0]):
                value = jnp.where(group == half, own[tap].astype(F32), other[tap].astype(F32))
                for part in range(width // 128):
                    frames.at[part][pl.ds(step, block, stride=steps), :] = value[
                        :, part * 128 : (part + 1) * 128
                    ]
                step += 1
    for part in range(width // 128):
        out_ref[:, part * 128 : (part + 1) * 128] = frames[part].astype(BF16)


def weave(group, owns, others):
    sessions, width = owns[0].shape[1:]
    steps, block = 2 * sum(own.shape[0] for own in owns), sessions // 4
    taps = [
        pl.BlockSpec((own.shape[0], block, width), lambda i: (0, i, 0)) for own in owns + others
    ]
    return pl.pallas_call(
        weave_kernel,
        out_shape=jax.ShapeDtypeStruct((sessions * steps, width), BF16),
        grid=(4,),
        in_specs=[pl.BlockSpec(memory_space=pltpu.SMEM)] + taps,
        out_specs=pl.BlockSpec((block * steps, width), lambda i: (i, 0)),
        scratch_shapes=[pltpu.VMEM((width // 128, block * steps, 128), F32)],
        compiler_params=pltpu.CompilerParams(vmem_limit_bytes=VMEM_LIMIT),
    )(group, *owns, *others)


def swap(value, axis):
    return lax.ppermute(value, axis, [(0, 1), (1, 0)])


def after(value, earlier):
    return lax.optimization_barrier((value, earlier))[0]


class Ring:
    def __init__(self, count, own, other):
        order = ring_order(count)
        self.count = count
        self.pairs = []
        for p in range(count):
            here, there = order[p], order[(p + 1) % count]
            self.pairs += [(2 * here, 2 * there), (2 * there + 1, 2 * here + 1)]
        self.item = jnp.stack([own, other])
        self.blocks, self.steps, self.rounds = [own], [(0, 0)], 0

    def round(self, earlier=None):
        self.rounds += 1
        item = self.item
        if 2 * self.rounds == self.count:
            part = item.shape[1] // 2
            item = lax.dynamic_slice_in_dim(item, lax.axis_index("segment") * part, part, axis=1)
        if earlier is not None:
            item = after(item, earlier)
        item = lax.ppermute(item, ("streams", "segment"), self.pairs)
        self.item = item
        self.blocks += [item, swap(item, "segment")]
        self.steps += [(self.rounds, 0), (self.rounds, 1)]
        return item


def local(
    count,
    latent,
    conv_weight,
    conv_bias,
    tail_cache,
    input_cache,
    resume_slot,
    res_weight,
    res_bias,
    skip_weight,
    skip_bias,
):
    group = lax.axis_index("groups")
    group_word = group[None].astype(jnp.int32)
    rows, tap_count, width = conv_weight.shape
    sessions = latent.shape[0]
    taps = tap_count // 4

    halves = []
    for first in (0, tap_count // 2):
        part = lax.dynamic_slice_in_dim(conv_weight, first + group * taps, taps, axis=1)
        halves.append(part.transpose(1, 0, 2))
    own = jnp.concatenate(halves, axis=0)
    cuts = ((0, taps), (taps, taps + taps // 2), (taps + taps // 2, 2 * taps))

    if rows % 128 == 0 and count % 2 == 0:
        other = swap(own, "segment")
        rings = [Ring(count, own[a:b], other[a:b]) for a, b in cuts]
        up_ring, first_ring, second_ring = rings
        up_seen, first_seen = [], []
        for r in range(count // 2):
            up_seen.append(up_ring.round(first_seen[r - 2] if r > 1 else None))
            first_seen.append(first_ring.round(up_seen[r - 1] if r else None))
        second_seen = []
        for r in range(count // 2):
            second_seen.append(second_ring.round(None if r else up_seen[-2]))
        first_done, nearly_done = up_seen[0], (first_seen[-2], second_seen[0])
        gathered = [(ring.blocks, ring.steps) for ring in rings]
    else:
        gathered = [
            ([lax.all_gather(own[a:b], "streams", axis=1, tiled=True)], [None]) for a, b in cuts
        ]
        first_done = nearly_done = own

    portion = sessions // count
    cap = tail_cache.shape[0] // count
    half_taps, history = tail_cache.shape[1], input_cache.shape[1]
    slot_step = jnp.broadcast_to(
        resume_slot.astype(BF16)[:, None, None], (count * cap, 1, width)
    )
    filler = jnp.zeros((count * cap, half_taps - history - 1, width), BF16)
    beside = jnp.concatenate([input_cache, slot_step, filler], axis=1)
    stored = jnp.concatenate([tail_cache, beside], axis=2).reshape(count, cap * half_taps, 2 * width)
    parcel = jnp.concatenate([latent.reshape(count, portion, 2 * width), stored], axis=1)
    parcel = after(parcel, first_done)
    parcel = lax.all_to_all(parcel, "streams", split_axis=0, concat_axis=0, tiled=True)
    handed = parcel[:, :portion].reshape(sessions, 2 * width)
    stored = parcel[:, portion:].reshape(count * cap, half_taps, 2 * width)

    near_half = apply_elu(handed.astype(F32)).astype(BF16)
    far_half = swap(near_half, "groups")
    sides = (near_half, swap(near_half, "segment"), far_half, swap(far_half, "segment"))

    slots = stored[:, history, width:].astype(jnp.int32)[:, :1]
    one_hot = (slots == jnp.arange(sessions, dtype=jnp.int32)[None, :]).astype(BF16)
    packed = jnp.concatenate([stored[:, :, :width], stored[:, :history, width:]], axis=1)
    prev = jnp.einsum("js,jkc->ksc", one_hot, packed, preferred_element_type=F32).astype(BF16)

    res_theirs = swap(res_weight, "segment")

    own_up, away_up = spread_taps(sides, *gathered[0], count, F32)
    other_up = swap(after(away_up, nearly_done), "groups")
    owns, others = [], []
    for blocks, steps in gathered[1:]:
        own_tail, away_tail = spread_taps(sides, blocks, steps, count, BF16)
        own_up = after(own_up, away_tail)
        owns.append(own_tail)
        others.append(swap(away_tail, "groups"))

    up, mine = excite(group_word, own_up, other_up, prev, conv_bias[None])
    theirs = swap(mine, "segment")
    decoded = residual(
        up, mine, theirs, res_weight, res_theirs, res_bias[None], skip_weight, skip_bias[None]
    )
    decoded, others[-1] = lax.optimization_barrier((decoded, others[-1]))
    new_tail = weave(group_word, owns, others)
    shape = (sessions, half_taps, width)
    return decoded.reshape(shape), new_tail.reshape(shape)


def solution(mesh):
    placed = (
        P(("groups", "streams"), "segment"),
        P("streams", None, "segment"),
        P("segment"),
        P(("groups", "streams"), None, "segment"),
        P(("groups", "streams"), None, "segment"),
        P(("groups", "streams")),
        P(None, "segment", None),
        P(),
        P(None, "segment"),
        P("segment"),
    )
    return jax.shard_map(
        functools.partial(local, mesh.shape["streams"]),
        mesh=mesh,
        in_specs=placed,
        out_specs=(
            P(("groups", "streams"), None, "segment"),
            P(("groups", "streams"), None, "segment"),
        ),
        check_vma=False,
    )
```

```python
import functools

import jax
import jax.numpy as jnp
from jax import lax
from jax.experimental import pallas as pl
from jax.experimental.pallas import tpu as pltpu
from jax.sharding import PartitionSpec as P

VMEM_LIMIT = 48 * 1024 * 1024
F32 = jnp.float32
BF16 = jnp.bfloat16
VMEM = pl.BlockSpec(memory_space=pltpu.VMEM)


def apply_elu(values):
    return jnp.where(values > 0, values, jnp.exp(jnp.minimum(values, 0.0)) - 1.0)


def ring_order(count):
    return [2 * p if p < count // 2 else 2 * (count - 1 - p) + 1 for p in range(count)]


def ring_place(stream, count):
    return jnp.where(stream % 2 == 0, stream // 2, count - 1 - stream // 2)


def ring_stream(place, count):
    return jnp.where(place < count // 2, 2 * place, 2 * (count - 1 - place) + 1)


def spread_kernel(count, steps, *refs):
    blocks = refs[: len(steps)]
    sides, (home_ref, away_ref) = refs[len(steps) : len(steps) + 4], refs[len(steps) + 4 : -3]
    kernel_rows, inputs, sems = refs[-3:]
    taps = kernel_rows.shape[0]
    rows = blocks[0].shape[-2]
    core = lax.axis_index("segment")
    place = ring_place(lax.axis_index("streams"), count)
    copies = []
    for slot, (step, block) in enumerate(zip(steps, blocks)):
        if step is None:
            source, target = block, kernel_rows
        else:
            distance, passed = step
            taker = 1 - core if passed else core
            stream = ring_stream(
                lax.rem(place + (2 * taker - 1) * distance + count, count), count
            )
            source = block if len(block.shape) == 3 else block.at[passed]
            part = source.shape[0]
            first = 0 if part == taps else taker * part
            target = kernel_rows.at[
                pl.ds(first, part), pl.ds(pl.multiple_of(stream * rows, rows), rows), :
            ]
        copy = pltpu.make_async_copy(source, target, sems.at[slot])
        copy.start()
        copies.append(copy)
    half = sides[0].shape[1]
    for index, side in enumerate(sides):
        column = core if index % 2 == 0 else 1 - core
        inputs[index // 2, :, pl.ds(pl.multiple_of(column * half, half), half)] = side[...]
    for copy in copies:
        copy.wait()

    @pl.loop(0, taps)
    def _(tap):
        weights = kernel_rows[tap]
        home_ref[tap] = jnp.dot(inputs[0], weights, preferred_element_type=F32).astype(
            home_ref.dtype
        )
        away_ref[tap] = jnp.dot(inputs[1], weights, preferred_element_type=F32).astype(
            away_ref.dtype
        )


def spread_taps(sides, blocks, steps, count, home_type):
    taps, _, width = blocks[0].shape
    sessions, depth = sides[0].shape[0], 2 * sides[0].shape[1]
    return pl.pallas_call(
        functools.partial(spread_kernel, count, steps),
        out_shape=(
            jax.ShapeDtypeStruct((taps, sessions, width), home_type),
            jax.ShapeDtypeStruct((taps, sessions, width), BF16),
        ),
        in_specs=[pl.BlockSpec(memory_space=pl.ANY)] * len(blocks) + [VMEM] * 4,
        out_specs=(VMEM, VMEM),
        scratch_shapes=[
            pltpu.VMEM((taps, depth, width), BF16),
            pltpu.VMEM((2, sessions, depth), BF16),
            pltpu.SemaphoreType.DMA((len(blocks),)),
        ],
        compiler_params=pltpu.CompilerParams(vmem_limit_bytes=VMEM_LIMIT),
    )(*blocks, *sides)


def upsampled(group, own_ref, other_ref, prev_ref, bias, step):
    half, tap = divmod(step, own_ref.shape[0])
    value = jnp.where(group == half, own_ref[tap], other_ref[tap].astype(F32))
    return value + prev_ref[step].astype(F32) + bias


def excite_kernel(group_ref, own_ref, other_ref, prev_ref, bias_ref, window_ref):
    steps = 2 * own_ref.shape[0]
    history = prev_ref.shape[0] - steps
    for step in range(history):
        window_ref[step] = prev_ref[steps + step]
    for step in range(steps):
        up = upsampled(group_ref[0], own_ref, other_ref, prev_ref, bias_ref[...], step)
        window_ref[history + step] = apply_elu(up).astype(BF16)


def excite(group, own, other, prev, bias):
    return pl.pallas_call(
        excite_kernel,
        out_shape=jax.ShapeDtypeStruct(prev.shape, BF16),
        in_specs=[pl.BlockSpec(memory_space=pltpu.SMEM), VMEM, VMEM, VMEM, VMEM],
        out_specs=VMEM,
        compiler_params=pltpu.CompilerParams(vmem_limit_bytes=VMEM_LIMIT),
    )(group, own, other, prev, bias)


def residual_kernel(
    group_ref,
    own_ref,
    other_ref,
    prev_ref,
    mine_ref,
    theirs_ref,
    bias_ref,
    res_mine_ref,
    res_theirs_ref,
    res_bias_ref,
    skip_ref,
    skip_bias_ref,
    out_ref,
    frames,
):
    taps, block, width = own_ref.shape
    steps = 2 * taps
    branch = None
    for source, weights in ((mine_ref, res_mine_ref), (theirs_ref, res_theirs_ref)):
        for offset in range(weights.shape[0]):
            term = jnp.dot(
                source[offset : offset + steps].reshape(steps * block, width),
                weights[offset],
                preferred_element_type=F32,
            )
            branch = term if branch is None else branch + term
    hidden = apply_elu(branch + res_bias_ref[...]).astype(BF16)
    projected = jnp.dot(hidden, skip_ref[...], preferred_element_type=F32)
    for step in range(steps):
        up = upsampled(group_ref[0], own_ref, other_ref, prev_ref, bias_ref[...], step)
        mixed = up + projected[step * block : (step + 1) * block] + skip_bias_ref[...]
        for part in range(width // 128):
            frames.at[part][pl.ds(step, block, stride=steps), :] = mixed[
                :, part * 128 : (part + 1) * 128
            ]
    for part in range(width // 128):
        out_ref[:, part * 128 : (part + 1) * 128] = frames[part].astype(BF16)


def residual(group, own, other, prev, mine, theirs, *parameters):
    taps, sessions, width = own.shape
    steps, block = 2 * taps, sessions // 4

    def blocks(array):
        return pl.BlockSpec((array.shape[0], block, width), lambda i: (0, i, 0))

    arrays = (own, other, prev, mine, theirs)
    return pl.pallas_call(
        residual_kernel,
        out_shape=jax.ShapeDtypeStruct((sessions * steps, width), BF16),
        grid=(4,),
        in_specs=[pl.BlockSpec(memory_space=pltpu.SMEM)]
        + [blocks(array) for array in arrays]
        + [VMEM] * len(parameters),
        out_specs=pl.BlockSpec((block * steps, width), lambda i: (i, 0)),
        scratch_shapes=[pltpu.VMEM((width // 128, block * steps, 128), F32)],
        compiler_params=pltpu.CompilerParams(vmem_limit_bytes=VMEM_LIMIT),
    )(group, *arrays, *parameters)


def weave_kernel(group_ref, own_ref, other_ref, out_ref, frames):
    group = group_ref[0]
    taps, block, width = own_ref.shape
    for half in range(2):
        for tap in range(taps):
            value = jnp.where(
                group == half, own_ref[tap].astype(F32), other_ref[tap].astype(F32)
            )
            step = half * taps + tap
            for part in range(width // 128):
                frames.at[part][pl.ds(step, block, stride=2 * taps), :] = value[
                    :, part * 128 : (part + 1) * 128
                ]
    for part in range(width // 128):
        out_ref[:, part * 128 : (part + 1) * 128] = frames[part].astype(BF16)


def weave(group, own, other):
    taps, sessions, width = own.shape
    steps, block = 2 * taps, sessions // 4
    part = pl.BlockSpec((taps, block, width), lambda i: (0, i, 0))
    return pl.pallas_call(
        weave_kernel,
        out_shape=jax.ShapeDtypeStruct((sessions * steps, width), BF16),
        grid=(4,),
        in_specs=[pl.BlockSpec(memory_space=pltpu.SMEM), part, part],
        out_specs=pl.BlockSpec((block * steps, width), lambda i: (i, 0)),
        scratch_shapes=[pltpu.VMEM((width // 128, block * steps, 128), F32)],
        compiler_params=pltpu.CompilerParams(vmem_limit_bytes=VMEM_LIMIT),
    )(group, own, other)


def swap(value, axis):
    return lax.ppermute(value, axis, [(0, 1), (1, 0)])


def after(value, earlier):
    return lax.optimization_barrier((value, earlier))[0]


class Ring:
    def __init__(self, count, own, other):
        order = ring_order(count)
        self.count = count
        self.pairs = []
        for p in range(count):
            here, there = order[p], order[(p + 1) % count]
            self.pairs += [(2 * here, 2 * there), (2 * there + 1, 2 * here + 1)]
        self.item = jnp.stack([own, other])
        self.blocks, self.steps, self.rounds = [own], [(0, 0)], 0

    def round(self, earlier=None):
        self.rounds += 1
        item = self.item
        if 2 * self.rounds == self.count:
            part = item.shape[1] // 2
            item = lax.dynamic_slice_in_dim(item, lax.axis_index("segment") * part, part, axis=1)
        if earlier is not None:
            item = after(item, earlier)
        item = lax.ppermute(item, ("streams", "segment"), self.pairs)
        self.item = item
        self.blocks += [item, swap(item, "segment")]
        self.steps += [(self.rounds, 0), (self.rounds, 1)]
        return item


def local(
    count,
    latent,
    conv_weight,
    conv_bias,
    tail_cache,
    input_cache,
    resume_slot,
    res_weight,
    res_bias,
    skip_weight,
    skip_bias,
):
    group = lax.axis_index("groups")
    group_word = group[None].astype(jnp.int32)
    rows, tap_count, width = conv_weight.shape
    sessions = latent.shape[0]
    taps = tap_count // 4

    halves = []
    for first in (0, tap_count // 2):
        part = lax.dynamic_slice_in_dim(conv_weight, first + group * taps, taps, axis=1)
        halves.append(part.transpose(1, 0, 2))
    own = jnp.concatenate(halves, axis=0)
    cuts = ((0, taps), (taps, 2 * taps))

    if rows % 128 == 0 and count % 2 == 0:
        other = swap(own, "segment")
        rings = [Ring(count, own[a:b], other[a:b]) for a, b in cuts]
        up_ring, tail_ring = rings
        up_seen, tail_seen = [], []
        for _ in range(count // 2):
            up_seen.append(up_ring.round())
            tail_seen.append(tail_ring.round())
        first_done = up_seen[0]
        up_ring.blocks[0] = after(up_ring.blocks[0], tail_seen[-2])
        nearly_done = tail_seen[-1]
        gathered = [(ring.blocks, ring.steps) for ring in rings]
    else:
        gathered = [
            ([lax.all_gather(own[a:b], "streams", axis=1, tiled=True)], [None]) for a, b in cuts
        ]
        first_done = nearly_done = own

    portion = sessions // count
    cap = tail_cache.shape[0] // count
    half_taps, history = tail_cache.shape[1], input_cache.shape[1]
    slot_step = jnp.broadcast_to(
        resume_slot.astype(BF16)[:, None, None], (count * cap, 1, width)
    )
    filler = jnp.zeros((count * cap, half_taps - history - 1, width), BF16)
    beside = jnp.concatenate([input_cache, slot_step, filler], axis=1)
    stored = jnp.concatenate([tail_cache, beside], axis=2).reshape(count, cap * half_taps, 2 * width)
    parcel = jnp.concatenate([latent.reshape(count, portion, 2 * width), stored], axis=1)
    parcel = after(parcel, first_done)
    parcel = lax.all_to_all(parcel, "streams", split_axis=0, concat_axis=0, tiled=True)
    handed = parcel[:, :portion].reshape(sessions, 2 * width)
    stored = parcel[:, portion:].reshape(count * cap, half_taps, 2 * width)

    near_half = apply_elu(handed.astype(F32)).astype(BF16)
    far_half = swap(near_half, "groups")
    sides = (near_half, swap(near_half, "segment"), far_half, swap(far_half, "segment"))

    slots = stored[:, history, width:].astype(jnp.int32)[:, :1]
    one_hot = (slots == jnp.arange(sessions, dtype=jnp.int32)[None, :]).astype(BF16)
    packed = jnp.concatenate([stored[:, :, :width], stored[:, :history, width:]], axis=1)
    prev = jnp.einsum("js,jkc->ksc", one_hot, packed, preferred_element_type=F32).astype(BF16)

    res_theirs = swap(res_weight, "segment")

    own_up, away_up = spread_taps(sides, *gathered[0], count, F32)
    other_up = swap(after(away_up, nearly_done), "groups")
    own_tail, away_tail = spread_taps(sides, *gathered[1], count, BF16)
    other_tail = swap(away_tail, "groups")

    own_up = after(own_up, (away_tail, res_theirs))
    bias = conv_bias[None]
    mine = excite(group_word, own_up, other_up, prev, bias)
    theirs = swap(mine, "segment")
    decoded = residual(
        group_word,
        own_up,
        other_up,
        prev,
        mine,
        theirs,
        bias,
        res_weight,
        res_theirs,
        res_bias[None],
        skip_weight,
        skip_bias[None],
    )
    decoded, other_tail = lax.optimization_barrier((decoded, other_tail))
    new_tail = weave(group_word, own_tail, other_tail)
    shape = (sessions, half_taps, width)
    return decoded.reshape(shape), new_tail.reshape(shape)


def solution(mesh):
    placed = (
        P(("groups", "streams"), "segment"),
        P("streams", None, "segment"),
        P("segment"),
        P(("groups", "streams"), None, "segment"),
        P(("groups", "streams"), None, "segment"),
        P(("groups", "streams")),
        P(None, "segment", None),
        P(),
        P(None, "segment"),
        P("segment"),
    )
    return jax.shard_map(
        functools.partial(local, mesh.shape["streams"]),
        mesh=mesh,
        in_specs=placed,
        out_specs=(
            P(("groups", "streams"), None, "segment"),
            P(("groups", "streams"), None, "segment"),
        ),
        check_vma=False,
    )
```

```python
import functools

import jax
import jax.numpy as jnp
from jax import lax
from jax.experimental import pallas as pl
from jax.experimental.pallas import tpu as pltpu
from jax.sharding import PartitionSpec as P

VMEM_LIMIT = 48 * 1024 * 1024
F32 = jnp.float32
BF16 = jnp.bfloat16
VMEM = pl.BlockSpec(memory_space=pltpu.VMEM)


def apply_elu(values):
    return jnp.where(values > 0, values, jnp.exp(jnp.minimum(values, 0.0)) - 1.0)


def ring_order(count):
    return [2 * p if p < count // 2 else 2 * (count - 1 - p) + 1 for p in range(count)]


def ring_place(stream, count):
    return jnp.where(stream % 2 == 0, stream // 2, count - 1 - stream // 2)


def ring_stream(place, count):
    return jnp.where(place < count // 2, 2 * place, 2 * (count - 1 - place) + 1)


def spread_kernel(count, steps, *refs):
    blocks = refs[: len(steps)]
    sides, (home_ref, away_ref) = refs[len(steps) : len(steps) + 4], refs[len(steps) + 4 : -3]
    kernel_rows, inputs, sems = refs[-3:]
    taps = kernel_rows.shape[0]
    rows = blocks[0].shape[-2]
    core = lax.axis_index("segment")
    place = ring_place(lax.axis_index("streams"), count)
    copies = []
    for slot, (step, block) in enumerate(zip(steps, blocks)):
        if step is None:
            source, target = block, kernel_rows
        else:
            distance, passed = step
            taker = 1 - core if passed else core
            stream = ring_stream(
                lax.rem(place + (2 * taker - 1) * distance + count, count), count
            )
            source = block if len(block.shape) == 3 else block.at[passed]
            part = source.shape[0]
            first = 0 if part == taps else taker * part
            target = kernel_rows.at[
                pl.ds(first, part), pl.ds(pl.multiple_of(stream * rows, rows), rows), :
            ]
        copy = pltpu.make_async_copy(source, target, sems.at[slot])
        copy.start()
        copies.append(copy)
    half = sides[0].shape[1]
    for index, side in enumerate(sides):
        column = core if index % 2 == 0 else 1 - core
        inputs[index // 2, :, pl.ds(pl.multiple_of(column * half, half), half)] = side[...]
    for copy in copies:
        copy.wait()

    @pl.loop(0, taps)
    def _(tap):
        weights = kernel_rows[tap]
        home_ref[tap] = jnp.dot(inputs[0], weights, preferred_element_type=F32).astype(
            home_ref.dtype
        )
        away_ref[tap] = jnp.dot(inputs[1], weights, preferred_element_type=F32).astype(
            away_ref.dtype
        )


def spread_taps(sides, blocks, steps, count, home_type):
    taps, _, width = blocks[0].shape
    sessions, depth = sides[0].shape[0], 2 * sides[0].shape[1]
    return pl.pallas_call(
        functools.partial(spread_kernel, count, steps),
        out_shape=(
            jax.ShapeDtypeStruct((taps, sessions, width), home_type),
            jax.ShapeDtypeStruct((taps, sessions, width), BF16),
        ),
        in_specs=[pl.BlockSpec(memory_space=pl.ANY)] * len(blocks) + [VMEM] * 4,
        out_specs=(VMEM, VMEM),
        scratch_shapes=[
            pltpu.VMEM((taps, depth, width), BF16),
            pltpu.VMEM((2, sessions, depth), BF16),
            pltpu.SemaphoreType.DMA((len(blocks),)),
        ],
        compiler_params=pltpu.CompilerParams(vmem_limit_bytes=VMEM_LIMIT),
    )(*blocks, *sides)


def each_step(group, own_ref, other_ref):
    taps = own_ref.shape[0]
    for index, source in enumerate((own_ref, other_ref)):
        first = (group if index == 0 else 1 - group) * taps
        for tap in range(taps):
            yield first + tap, source[tap].astype(F32)


def excite_kernel(group_ref, own_ref, other_ref, prev_ref, bias_ref, window_ref):
    steps = 2 * own_ref.shape[0]
    history = prev_ref.shape[0] - steps
    for step in range(history):
        window_ref[step] = prev_ref[steps + step]
    for step, value in each_step(group_ref[0], own_ref, other_ref):
        up = value + prev_ref[step].astype(F32) + bias_ref[...]
        window_ref[history + step] = apply_elu(up).astype(BF16)


def excite(group, own, other, prev, bias):
    return pl.pallas_call(
        excite_kernel,
        out_shape=jax.ShapeDtypeStruct(prev.shape, BF16),
        in_specs=[pl.BlockSpec(memory_space=pltpu.SMEM), VMEM, VMEM, VMEM, VMEM],
        out_specs=VMEM,
        compiler_params=pltpu.CompilerParams(vmem_limit_bytes=VMEM_LIMIT),
    )(group, own, other, prev, bias)


def residual_kernel(
    group_ref,
    own_ref,
    other_ref,
    prev_ref,
    mine_ref,
    theirs_ref,
    bias_ref,
    res_mine_ref,
    res_theirs_ref,
    res_bias_ref,
    skip_ref,
    skip_bias_ref,
    out_ref,
    products,
    frames,
):
    taps, block, width = own_ref.shape
    steps = 2 * taps
    branch = None
    for source, weights in ((mine_ref, res_mine_ref), (theirs_ref, res_theirs_ref)):
        for offset in range(weights.shape[0]):
            term = jnp.dot(
                source[offset : offset + steps].reshape(steps * block, width),
                weights[offset],
                preferred_element_type=F32,
            )
            branch = term if branch is None else branch + term
    hidden = apply_elu(branch + res_bias_ref[...]).astype(BF16)
    projected = jnp.dot(hidden, skip_ref[...], preferred_element_type=F32)
    products[...] = projected.reshape(products.shape)
    for step, value in each_step(group_ref[0], own_ref, other_ref):
        up = value + prev_ref[step].astype(F32) + bias_ref[...]
        mixed = up + products[step] + skip_bias_ref[...]
        for part in range(width // 128):
            frames.at[part][pl.ds(step, block, stride=steps), :] = mixed[
                :, part * 128 : (part + 1) * 128
            ]
    for part in range(width // 128):
        out_ref[:, part * 128 : (part + 1) * 128] = frames[part].astype(BF16)


def residual(group, own, other, prev, mine, theirs, *parameters):
    taps, sessions, width = own.shape
    steps, block = 2 * taps, sessions // 4

    def blocks(array):
        return pl.BlockSpec((array.shape[0], block, width), lambda i: (0, i, 0))

    arrays = (own, other, prev, mine, theirs)
    return pl.pallas_call(
        residual_kernel,
        out_shape=jax.ShapeDtypeStruct((sessions * steps, width), BF16),
        grid=(4,),
        in_specs=[pl.BlockSpec(memory_space=pltpu.SMEM)]
        + [blocks(array) for array in arrays]
        + [VMEM] * len(parameters),
        out_specs=pl.BlockSpec((block * steps, width), lambda i: (i, 0)),
        scratch_shapes=[
            pltpu.VMEM((steps, block, width), F32),
            pltpu.VMEM((width // 128, block * steps, 128), F32),
        ],
        compiler_params=pltpu.CompilerParams(vmem_limit_bytes=VMEM_LIMIT),
    )(group, *arrays, *parameters)


def weave_kernel(group_ref, own_ref, other_ref, out_ref, frames):
    taps, block, width = own_ref.shape
    for step, value in each_step(group_ref[0], own_ref, other_ref):
        for part in range(width // 128):
            frames.at[part][pl.ds(step, block, stride=2 * taps), :] = value[
                :, part * 128 : (part + 1) * 128
            ]
    for part in range(width // 128):
        out_ref[:, part * 128 : (part + 1) * 128] = frames[part].astype(BF16)


def weave(group, own, other):
    taps, sessions, width = own.shape
    steps, block = 2 * taps, sessions // 4
    part = pl.BlockSpec((taps, block, width), lambda i: (0, i, 0))
    return pl.pallas_call(
        weave_kernel,
        out_shape=jax.ShapeDtypeStruct((sessions * steps, width), BF16),
        grid=(4,),
        in_specs=[pl.BlockSpec(memory_space=pltpu.SMEM), part, part],
        out_specs=pl.BlockSpec((block * steps, width), lambda i: (i, 0)),
        scratch_shapes=[pltpu.VMEM((width // 128, block * steps, 128), F32)],
        compiler_params=pltpu.CompilerParams(vmem_limit_bytes=VMEM_LIMIT),
    )(group, own, other)


def swap(value, axis):
    return lax.ppermute(value, axis, [(0, 1), (1, 0)])


def after(value, earlier):
    return lax.optimization_barrier((value, earlier))[0]


class Ring:
    def __init__(self, count, own, other):
        order = ring_order(count)
        self.count = count
        self.pairs = []
        for p in range(count):
            here, there = order[p], order[(p + 1) % count]
            self.pairs += [(2 * here, 2 * there), (2 * there + 1, 2 * here + 1)]
        self.item = jnp.stack([own, other])
        self.blocks, self.steps, self.rounds = [own], [(0, 0)], 0

    def round(self, earlier=None):
        self.rounds += 1
        item = self.item
        if 2 * self.rounds == self.count:
            part = item.shape[1] // 2
            item = lax.dynamic_slice_in_dim(item, lax.axis_index("segment") * part, part, axis=1)
        if earlier is not None:
            item = after(item, earlier)
        item = lax.ppermute(item, ("streams", "segment"), self.pairs)
        self.item = item
        self.blocks += [item, swap(item, "segment")]
        self.steps += [(self.rounds, 0), (self.rounds, 1)]
        return item


def local(
    count,
    latent,
    conv_weight,
    conv_bias,
    tail_cache,
    input_cache,
    resume_slot,
    res_weight,
    res_bias,
    skip_weight,
    skip_bias,
):
    group = lax.axis_index("groups")
    group_word = group[None].astype(jnp.int32)
    rows, tap_count, width = conv_weight.shape
    sessions = latent.shape[0]
    taps = tap_count // 4

    halves = []
    for first in (0, tap_count // 2):
        part = lax.dynamic_slice_in_dim(conv_weight, first + group * taps, taps, axis=1)
        halves.append(part.transpose(1, 0, 2))

    if rows % 128 == 0 and count % 2 == 0:
        up_ring, tail_ring = (Ring(count, own, swap(own, "segment")) for own in halves)
        up_seen, tail_seen = [up_ring.round()], []
        tail_seen.append(tail_ring.round(up_seen[0]))
        for _ in range(2, count // 2):
            up_seen.append(up_ring.round())
            tail_seen.append(tail_ring.round())
        up_ring.round()
        up_ring.blocks[0] = after(up_ring.blocks[0], tail_seen[-2])
        first_done, nearly_done = up_seen[0], tail_seen[-1]
    else:
        tail_ring = None
        first_done = nearly_done = halves[0]

    portion = sessions // count
    cap = tail_cache.shape[0] // count
    half_taps, history = tail_cache.shape[1], input_cache.shape[1]
    slot_step = jnp.broadcast_to(
        resume_slot.astype(BF16)[:, None, None], (count * cap, 1, width)
    )
    filler = jnp.zeros((count * cap, half_taps - history - 1, width), BF16)
    beside = jnp.concatenate([input_cache, slot_step, filler], axis=1)
    stored = jnp.concatenate([tail_cache, beside], axis=2).reshape(count, cap * half_taps, 2 * width)
    parcel = jnp.concatenate([latent.reshape(count, portion, 2 * width), stored], axis=1)
    parcel = after(parcel, first_done)
    parcel = lax.all_to_all(parcel, "streams", split_axis=0, concat_axis=0, tiled=True)
    handed = parcel[:, :portion].reshape(sessions, 2 * width)
    stored = parcel[:, portion:].reshape(count * cap, half_taps, 2 * width)

    near_half = apply_elu(handed.astype(F32)).astype(BF16)
    far_half = swap(near_half, "groups")
    sides = (near_half, swap(near_half, "segment"), far_half, swap(far_half, "segment"))

    slots = stored[:, history, width:].astype(jnp.int32)[:, :1]
    one_hot = (slots == jnp.arange(sessions, dtype=jnp.int32)[None, :]).astype(BF16)
    packed = jnp.concatenate([stored[:, :, :width], stored[:, :history, width:]], axis=1)
    prev = jnp.einsum("js,jkc->ksc", one_hot, packed, preferred_element_type=F32).astype(BF16)

    res_theirs = swap(res_weight, "segment")

    if tail_ring is None:
        whole = [lax.all_gather(own, "streams", axis=1, tiled=True) for own in halves]
        own_up, away_up = spread_taps(sides, [whole[0]], [None], count, F32)
        other_up = swap(away_up, "groups")
        own_tail, away_tail = spread_taps(sides, [whole[1]], [None], count, BF16)
    else:
        own_up, away_up = spread_taps(sides, up_ring.blocks, up_ring.steps, count, F32)
        tail_ring.round(away_up)
        other_up = swap(after(away_up, nearly_done), "groups")
        own_tail, away_tail = spread_taps(sides, tail_ring.blocks, tail_ring.steps, count, BF16)
    other_tail = swap(away_tail, "groups")

    own_up = after(own_up, (away_tail, res_theirs))
    bias = conv_bias[None]
    mine = excite(group_word, own_up, other_up, prev, bias)
    theirs = swap(mine, "segment")
    decoded = residual(
        group_word,
        own_up,
        other_up,
        prev,
        mine,
        theirs,
        bias,
        res_weight,
        res_theirs,
        res_bias[None],
        skip_weight,
        skip_bias[None],
    )
    decoded, other_tail = lax.optimization_barrier((decoded, other_tail))
    new_tail = weave(group_word, own_tail, other_tail)
    shape = (sessions, half_taps, width)
    return decoded.reshape(shape), new_tail.reshape(shape)


def solution(mesh):
    placed = (
        P(("groups", "streams"), "segment"),
        P("streams", None, "segment"),
        P("segment"),
        P(("groups", "streams"), None, "segment"),
        P(("groups", "streams"), None, "segment"),
        P(("groups", "streams")),
        P(None, "segment", None),
        P(),
        P(None, "segment"),
        P("segment"),
    )
    return jax.shard_map(
        functools.partial(local, mesh.shape["streams"]),
        mesh=mesh,
        in_specs=placed,
        out_specs=(
            P(("groups", "streams"), None, "segment"),
            P(("groups", "streams"), None, "segment"),
        ),
        check_vma=False,
    )
```

```python
import functools

import jax
import jax.numpy as jnp
from jax import lax
from jax.experimental import pallas as pl
from jax.experimental.pallas import tpu as pltpu
from jax.sharding import PartitionSpec as P

VMEM_LIMIT = 48 * 1024 * 1024
F32 = jnp.float32
BF16 = jnp.bfloat16
VMEM = pl.BlockSpec(memory_space=pltpu.VMEM)


def apply_elu(values):
    return jnp.where(values > 0, values, jnp.exp(jnp.minimum(values, 0.0)) - 1.0)


def ring_order(count):
    return [2 * p if p < count // 2 else 2 * (count - 1 - p) + 1 for p in range(count)]


def ring_place(stream, count):
    return jnp.where(stream % 2 == 0, stream // 2, count - 1 - stream // 2)


def ring_stream(place, count):
    return jnp.where(place < count // 2, 2 * place, 2 * (count - 1 - place) + 1)


def spread_kernel(count, steps, *refs):
    blocks = refs[: len(steps)]
    sides, outs = refs[len(steps) : len(steps) + 4], refs[len(steps) + 4 : -3]
    home_ref, away_refs = outs[0], outs[1:]
    kernel_rows, inputs, sems = refs[-3:]
    taps = kernel_rows.shape[0]
    rows = blocks[0].shape[-2]
    core = lax.axis_index("segment")
    place = ring_place(lax.axis_index("streams"), count)
    copies = []
    for slot, (step, block) in enumerate(zip(steps, blocks)):
        if step is None:
            source, target = block, kernel_rows
        else:
            distance, passed = step
            taker = 1 - core if passed else core
            stream = ring_stream(
                lax.rem(place + (2 * taker - 1) * distance + count, count), count
            )
            source = block if len(block.shape) == 3 else block.at[passed]
            part = source.shape[0]
            first = 0 if part == taps else taker * part
            target = kernel_rows.at[
                pl.ds(first, part), pl.ds(pl.multiple_of(stream * rows, rows), rows), :
            ]
        copy = pltpu.make_async_copy(source, target, sems.at[slot])
        copy.start()
        copies.append(copy)
    sessions, half = sides[0].shape
    for index, side in enumerate(sides):
        column = core if index % 2 == 0 else 1 - core
        first = index // 2 * sessions
        inputs[first : first + sessions, pl.ds(pl.multiple_of(column * half, half), half)] = side[...]
    for copy in copies:
        copy.wait()

    for part, away_ref in enumerate(away_refs):

        @pl.loop(0, away_ref.shape[0])
        def _(index):
            tap = part * away_ref.shape[0] + index
            product = jnp.dot(inputs[...], kernel_rows[tap], preferred_element_type=F32)
            home_ref[tap] = product[:sessions].astype(home_ref.dtype)
            away_ref[index] = product[sessions:].astype(away_ref.dtype)


def spread_taps(sides, blocks, steps, count, home_type):
    taps, _, width = blocks[0].shape
    sessions, depth = sides[0].shape[0], 2 * sides[0].shape[1]
    return pl.pallas_call(
        functools.partial(spread_kernel, count, steps),
        out_shape=(
            jax.ShapeDtypeStruct((taps, sessions, width), home_type),
            jax.ShapeDtypeStruct((taps // 2, sessions, width), BF16),
            jax.ShapeDtypeStruct((taps // 2, sessions, width), BF16),
        ),
        in_specs=[pl.BlockSpec(memory_space=pl.ANY)] * len(blocks) + [VMEM] * 4,
        out_specs=(VMEM, VMEM, VMEM),
        scratch_shapes=[
            pltpu.VMEM((taps, depth, width), BF16),
            pltpu.VMEM((2 * sessions, depth), BF16),
            pltpu.SemaphoreType.DMA((len(blocks),)),
        ],
        compiler_params=pltpu.CompilerParams(vmem_limit_bytes=VMEM_LIMIT),
    )(*blocks, *sides)


def each_step(group, own_ref, other_refs):
    taps = own_ref.shape[0]
    for tap in range(taps):
        yield group * taps + tap, own_ref[tap].astype(F32)
    for tap in range(taps):
        part, index = divmod(tap, other_refs[0].shape[0])
        yield (1 - group) * taps + tap, other_refs[part][index].astype(F32)


def excite_kernel(group_ref, own_ref, first_ref, second_ref, prev_ref, bias_ref, window_ref):
    steps = 2 * own_ref.shape[0]
    history = prev_ref.shape[0] - steps
    for step in range(history):
        window_ref[step] = prev_ref[steps + step]
    for step, value in each_step(group_ref[0], own_ref, (first_ref, second_ref)):
        up = value + prev_ref[step].astype(F32) + bias_ref[...]
        window_ref[history + step] = apply_elu(up).astype(BF16)


def excite(group, own, other, prev, bias):
    return pl.pallas_call(
        excite_kernel,
        out_shape=jax.ShapeDtypeStruct(prev.shape, BF16),
        in_specs=[pl.BlockSpec(memory_space=pltpu.SMEM)] + [VMEM] * 5,
        out_specs=VMEM,
        compiler_params=pltpu.CompilerParams(vmem_limit_bytes=VMEM_LIMIT),
    )(group, own, *other, prev, bias)


def residual_kernel(
    group_ref,
    own_ref,
    first_ref,
    second_ref,
    prev_ref,
    mine_ref,
    theirs_ref,
    bias_ref,
    res_mine_ref,
    res_theirs_ref,
    res_bias_ref,
    skip_ref,
    skip_bias_ref,
    out_ref,
    products,
    frames,
):
    taps, block, width = own_ref.shape
    steps = 2 * taps
    branch = None
    for source, weights in ((mine_ref, res_mine_ref), (theirs_ref, res_theirs_ref)):
        for offset in range(weights.shape[0]):
            term = jnp.dot(
                source[offset : offset + steps].reshape(steps * block, width),
                weights[offset],
                preferred_element_type=F32,
            )
            branch = term if branch is None else branch + term
    hidden = apply_elu(branch + res_bias_ref[...]).astype(BF16)
    projected = jnp.dot(hidden, skip_ref[...], preferred_element_type=F32)
    products[...] = projected.reshape(products.shape)
    for step, value in each_step(group_ref[0], own_ref, (first_ref, second_ref)):
        up = value + prev_ref[step].astype(F32) + bias_ref[...]
        mixed = up + products[step] + skip_bias_ref[...]
        for part in range(width // 128):
            frames.at[part][pl.ds(step, block, stride=steps), :] = mixed[
                :, part * 128 : (part + 1) * 128
            ]
    for part in range(width // 128):
        out_ref[:, part * 128 : (part + 1) * 128] = frames[part].astype(BF16)


def residual(group, own, other, prev, mine, theirs, *parameters):
    taps, sessions, width = own.shape
    steps, block = 2 * taps, sessions // 4

    def blocks(array):
        return pl.BlockSpec((array.shape[0], block, width), lambda i: (0, i, 0))

    arrays = (own, *other, prev, mine, theirs)
    return pl.pallas_call(
        residual_kernel,
        out_shape=jax.ShapeDtypeStruct((sessions * steps, width), BF16),
        grid=(4,),
        in_specs=[pl.BlockSpec(memory_space=pltpu.SMEM)]
        + [blocks(array) for array in arrays]
        + [VMEM] * len(parameters),
        out_specs=pl.BlockSpec((block * steps, width), lambda i: (i, 0)),
        scratch_shapes=[
            pltpu.VMEM((steps, block, width), F32),
            pltpu.VMEM((width // 128, block * steps, 128), F32),
        ],
        compiler_params=pltpu.CompilerParams(vmem_limit_bytes=VMEM_LIMIT),
    )(group, *arrays, *parameters)


def weave_kernel(group_ref, own_ref, first_ref, second_ref, out_ref, frames):
    taps, block, width = own_ref.shape
    for step, value in each_step(group_ref[0], own_ref, (first_ref, second_ref)):
        for part in range(width // 128):
            frames.at[part][pl.ds(step, block, stride=2 * taps), :] = value[
                :, part * 128 : (part + 1) * 128
            ]
    for part in range(width // 128):
        out_ref[:, part * 128 : (part + 1) * 128] = frames[part].astype(BF16)


def weave(group, own, other):
    taps, sessions, width = own.shape
    steps, block = 2 * taps, sessions // 4
    arrays = (own, *other)
    taken = [pl.BlockSpec((array.shape[0], block, width), lambda i: (0, i, 0)) for array in arrays]
    return pl.pallas_call(
        weave_kernel,
        out_shape=jax.ShapeDtypeStruct((sessions * steps, width), BF16),
        grid=(4,),
        in_specs=[pl.BlockSpec(memory_space=pltpu.SMEM)] + taken,
        out_specs=pl.BlockSpec((block * steps, width), lambda i: (i, 0)),
        scratch_shapes=[pltpu.VMEM((width // 128, block * steps, 128), F32)],
        compiler_params=pltpu.CompilerParams(vmem_limit_bytes=VMEM_LIMIT),
    )(group, *arrays)


def swap(value, axis):
    return lax.ppermute(value, axis, [(0, 1), (1, 0)])


def after(value, earlier):
    return lax.optimization_barrier((value, earlier))[0]


class Ring:
    def __init__(self, count, own, other):
        order = ring_order(count)
        self.count = count
        self.pairs = []
        for p in range(count):
            here, there = order[p], order[(p + 1) % count]
            self.pairs += [(2 * here, 2 * there), (2 * there + 1, 2 * here + 1)]
        self.item = jnp.stack([own, other])
        self.blocks, self.steps, self.rounds = [own], [(0, 0)], 0

    def round(self, earlier=None):
        self.rounds += 1
        item = self.item
        if 2 * self.rounds == self.count:
            part = item.shape[1] // 2
            item = lax.dynamic_slice_in_dim(item, lax.axis_index("segment") * part, part, axis=1)
        if earlier is not None:
            item = after(item, earlier)
        item = lax.ppermute(item, ("streams", "segment"), self.pairs)
        self.item = item
        self.blocks += [item, swap(item, "segment")]
        self.steps += [(self.rounds, 0), (self.rounds, 1)]
        return item


def local(
    count,
    latent,
    conv_weight,
    conv_bias,
    tail_cache,
    input_cache,
    resume_slot,
    res_weight,
    res_bias,
    skip_weight,
    skip_bias,
):
    group = lax.axis_index("groups")
    group_word = group[None].astype(jnp.int32)
    rows, tap_count, width = conv_weight.shape
    sessions = latent.shape[0]
    taps = tap_count // 4

    halves = []
    for first in (0, tap_count // 2):
        part = lax.dynamic_slice_in_dim(conv_weight, first + group * taps, taps, axis=1)
        halves.append(part.transpose(1, 0, 2))

    if rows % 128 == 0 and count % 2 == 0:
        other = swap(halves[0], "segment")
        up_ring = Ring(count, halves[0], other)
        prepared = swap(after(halves[1], other), "segment")
        tail_ring = Ring(count, halves[1], prepared)
        tail_seen = []
        for _ in range(count // 2):
            up_ring.round()
            tail_seen.append(tail_ring.round())
        up_ring.blocks[0] = after(up_ring.blocks[0], tail_seen[-2])
        nearly_done = tail_seen[-1]
    else:
        tail_ring = None
        prepared = halves[1]

    portion = sessions // count
    cap = tail_cache.shape[0] // count
    half_taps, history = tail_cache.shape[1], input_cache.shape[1]
    slot_step = jnp.broadcast_to(
        resume_slot.astype(BF16)[:, None, None], (count * cap, 1, width)
    )
    filler = jnp.zeros((count * cap, half_taps - history - 1, width), BF16)
    beside = jnp.concatenate([input_cache, slot_step, filler], axis=1)
    stored = jnp.concatenate([tail_cache, beside], axis=2).reshape(count, cap * half_taps, 2 * width)
    parcel = jnp.concatenate([latent.reshape(count, portion, 2 * width), stored], axis=1)
    parcel = after(parcel, prepared)
    parcel = lax.all_to_all(parcel, "streams", split_axis=0, concat_axis=0, tiled=True)
    handed = parcel[:, :portion].reshape(sessions, 2 * width)
    stored = parcel[:, portion:].reshape(count * cap, half_taps, 2 * width)

    near_half = apply_elu(handed.astype(F32)).astype(BF16)
    far_half = swap(near_half, "groups")
    sides = (near_half, swap(near_half, "segment"), far_half, swap(far_half, "segment"))

    slots = stored[:, history, width:].astype(jnp.int32)[:, :1]
    one_hot = (slots == jnp.arange(sessions, dtype=jnp.int32)[None, :]).astype(BF16)
    packed = jnp.concatenate([stored[:, :, :width], stored[:, :history, width:]], axis=1)
    prev = jnp.einsum("js,jkc->ksc", one_hot, packed, preferred_element_type=F32).astype(BF16)

    res_theirs = swap(res_weight, "segment")

    if tail_ring is None:
        whole = [lax.all_gather(own, "streams", axis=1, tiled=True) for own in halves]
        own_up, *away_up = spread_taps(sides, [whole[0]], [None], count, F32)
        own_tail, *away_tail = spread_taps(sides, [whole[1]], [None], count, BF16)
    else:
        own_up, *away_up = spread_taps(sides, up_ring.blocks, up_ring.steps, count, F32)
        away_up = list(after(away_up, nearly_done))
        own_tail, *away_tail = spread_taps(sides, tail_ring.blocks, tail_ring.steps, count, BF16)
    other_up = [swap(part, "groups") for part in away_up]
    other_tail = [swap(part, "groups") for part in away_tail]

    own_up = after(own_up, (away_tail, res_theirs))
    bias = conv_bias[None]
    mine = excite(group_word, own_up, other_up, prev, bias)
    theirs = swap(mine, "segment")
    decoded = residual(
        group_word,
        own_up,
        other_up,
        prev,
        mine,
        theirs,
        bias,
        res_weight,
        res_theirs,
        res_bias[None],
        skip_weight,
        skip_bias[None],
    )
    decoded, other_tail = lax.optimization_barrier((decoded, other_tail))
    new_tail = weave(group_word, own_tail, other_tail)
    shape = (sessions, half_taps, width)
    return decoded.reshape(shape), new_tail.reshape(shape)


def solution(mesh):
    placed = (
        P(("groups", "streams"), "segment"),
        P("streams", None, "segment"),
        P("segment"),
        P(("groups", "streams"), None, "segment"),
        P(("groups", "streams"), None, "segment"),
        P(("groups", "streams")),
        P(None, "segment", None),
        P(),
        P(None, "segment"),
        P("segment"),
    )
    return jax.shard_map(
        functools.partial(local, mesh.shape["streams"]),
        mesh=mesh,
        in_specs=placed,
        out_specs=(
            P(("groups", "streams"), None, "segment"),
            P(("groups", "streams"), None, "segment"),
        ),
        check_vma=False,
    )
```

```python
import functools

import jax
import jax.numpy as jnp
from jax import lax
from jax.experimental import pallas as pl
from jax.experimental.pallas import tpu as pltpu
from jax.sharding import PartitionSpec as P

VMEM_LIMIT = 16 * 1024 * 1024
F32 = jnp.float32
BF16 = jnp.bfloat16
VMEM = pl.BlockSpec(memory_space=pltpu.VMEM)


def apply_elu(values):
    return jnp.where(values > 0, values, jnp.exp(jnp.minimum(values, 0.0)) - 1.0)


def ring_order(count):
    return [2 * p if p < count // 2 else 2 * (count - 1 - p) + 1 for p in range(count)]


def ring_place(stream, count):
    return jnp.where(stream % 2 == 0, stream // 2, count - 1 - stream // 2)


def ring_stream(place, count):
    return jnp.where(place < count // 2, 2 * place, 2 * (count - 1 - place) + 1)


def spread_kernel(count, steps, *refs):
    blocks = refs[: len(steps)]
    sides, (home_ref, away_ref) = refs[len(steps) : len(steps) + 4], refs[len(steps) + 4 : -3]
    kernel_rows, inputs, sems = refs[-3:]
    taps = kernel_rows.shape[0]
    rows = blocks[0].shape[-2]
    core = lax.axis_index("segment")
    place = ring_place(lax.axis_index("streams"), count)
    copies = []
    for slot, (step, block) in enumerate(zip(steps, blocks)):
        if step is None:
            source, target = block, kernel_rows
        else:
            distance, passed = step
            taker = 1 - core if passed else core
            stream = ring_stream(
                lax.rem(place + (2 * taker - 1) * distance + count, count), count
            )
            source = block if len(block.shape) == 3 else block.at[passed]
            part = source.shape[0]
            first = 0 if part == taps else taker * part
            target = kernel_rows.at[
                pl.ds(first, part), pl.ds(pl.multiple_of(stream * rows, rows), rows), :
            ]
        copy = pltpu.make_async_copy(source, target, sems.at[slot])
        copy.start()
        copies.append(copy)
    sessions, half = sides[0].shape
    for index, side in enumerate(sides):
        column = core if index % 2 == 0 else 1 - core
        first = index // 2 * sessions
        inputs[first : first + sessions, pl.ds(pl.multiple_of(column * half, half), half)] = side[...]
    for copy in copies:
        copy.wait()

    @pl.loop(0, taps)
    def _(tap):
        product = jnp.dot(inputs[...], kernel_rows[tap], preferred_element_type=F32)
        home_ref[tap] = product[:sessions].astype(home_ref.dtype)
        away_ref[tap] = product[sessions:].astype(away_ref.dtype)


def spread_taps(sides, blocks, steps, count, home_type):
    taps, _, width = blocks[0].shape
    sessions, depth = sides[0].shape[0], 2 * sides[0].shape[1]
    return pl.pallas_call(
        functools.partial(spread_kernel, count, steps),
        out_shape=(
            jax.ShapeDtypeStruct((taps, sessions, width), home_type),
            jax.ShapeDtypeStruct((taps, sessions, width), BF16),
        ),
        in_specs=[pl.BlockSpec(memory_space=pl.ANY)] * len(blocks) + [VMEM] * 4,
        out_specs=(VMEM, VMEM),
        scratch_shapes=[
            pltpu.VMEM((taps, depth, width), BF16),
            pltpu.VMEM((2 * sessions, depth), BF16),
            pltpu.SemaphoreType.DMA((len(blocks),)),
        ],
        compiler_params=pltpu.CompilerParams(vmem_limit_bytes=VMEM_LIMIT),
        cost_estimate=pl.CostEstimate(
            flops=4 * taps * sessions * depth * width,
            bytes_accessed=2 * taps * depth * width + 4 * sessions * depth + 6 * taps * sessions * width,
            transcendentals=0,
        ),
    )(*blocks, *sides)


def each_step(group, own_ref, other_ref):
    taps = own_ref.shape[0]
    for index, source in enumerate((own_ref, other_ref)):
        first = (group if index == 0 else 1 - group) * taps
        for tap in range(taps):
            yield first + tap, source[tap].astype(F32)


def excite_kernel(group_ref, own_ref, other_ref, prev_ref, bias_ref, window_ref):
    steps = 2 * own_ref.shape[0]
    history = prev_ref.shape[0] - steps
    for step in range(history):
        window_ref[step] = prev_ref[steps + step]
    for step, value in each_step(group_ref[0], own_ref, other_ref):
        up = value + prev_ref[step].astype(F32) + bias_ref[...]
        window_ref[history + step] = apply_elu(up).astype(BF16)


def excite(group, own, other, prev, bias):
    return pl.pallas_call(
        excite_kernel,
        out_shape=jax.ShapeDtypeStruct(prev.shape, BF16),
        in_specs=[pl.BlockSpec(memory_space=pltpu.SMEM)] + [VMEM] * 4,
        out_specs=VMEM,
        compiler_params=pltpu.CompilerParams(vmem_limit_bytes=VMEM_LIMIT),
    )(group, own, other, prev, bias)


def residual_kernel(
    group_ref,
    own_ref,
    other_ref,
    prev_ref,
    mine_ref,
    theirs_ref,
    bias_ref,
    res_mine_ref,
    res_theirs_ref,
    res_bias_ref,
    skip_ref,
    skip_bias_ref,
    out_ref,
    products,
    frames,
):
    taps, block, width = own_ref.shape
    steps = 2 * taps
    branch = None
    for source, weights in ((mine_ref, res_mine_ref), (theirs_ref, res_theirs_ref)):
        for offset in range(weights.shape[0]):
            term = jnp.dot(
                source[offset : offset + steps].reshape(steps * block, width),
                weights[offset],
                preferred_element_type=F32,
            )
            branch = term if branch is None else branch + term
    hidden = apply_elu(branch + res_bias_ref[...]).astype(BF16)
    projected = jnp.dot(hidden, skip_ref[...], preferred_element_type=F32)
    products[...] = projected.reshape(products.shape)
    for step, value in each_step(group_ref[0], own_ref, other_ref):
        up = value + prev_ref[step].astype(F32) + bias_ref[...]
        mixed = up + products[step] + skip_bias_ref[...]
        for part in range(width // 128):
            frames.at[part][pl.ds(step, block, stride=steps), :] = mixed[
                :, part * 128 : (part + 1) * 128
            ]
    for part in range(width // 128):
        out_ref[:, part * 128 : (part + 1) * 128] = frames[part].astype(BF16)


def residual(group, own, other, prev, mine, theirs, *parameters):
    taps, sessions, width = own.shape
    steps, block = 2 * taps, sessions // 4

    def blocks(array):
        return pl.BlockSpec((array.shape[0], block, width), lambda i: (0, i, 0))

    arrays = (own, other, prev, mine, theirs)
    return pl.pallas_call(
        residual_kernel,
        out_shape=jax.ShapeDtypeStruct((sessions * steps, width), BF16),
        grid=(4,),
        in_specs=[pl.BlockSpec(memory_space=pltpu.SMEM)]
        + [blocks(array) for array in arrays]
        + [VMEM] * len(parameters),
        out_specs=pl.BlockSpec((block * steps, width), lambda i: (i, 0)),
        scratch_shapes=[
            pltpu.VMEM((steps, block, width), F32),
            pltpu.VMEM((width // 128, block * steps, 128), F32),
        ],
        compiler_params=pltpu.CompilerParams(vmem_limit_bytes=VMEM_LIMIT),
    )(group, *arrays, *parameters)


def weave_kernel(group_ref, own_ref, other_ref, out_ref, frames):
    taps, block, width = own_ref.shape
    for step, value in each_step(group_ref[0], own_ref, other_ref):
        for part in range(width // 128):
            frames.at[part][pl.ds(step, block, stride=2 * taps), :] = value[
                :, part * 128 : (part + 1) * 128
            ]
    for part in range(width // 128):
        out_ref[:, part * 128 : (part + 1) * 128] = frames[part].astype(BF16)


def weave(group, own, other):
    taps, sessions, width = own.shape
    steps, block = 2 * taps, sessions // 4
    taken = pl.BlockSpec((taps, block, width), lambda i: (0, i, 0))
    return pl.pallas_call(
        weave_kernel,
        out_shape=jax.ShapeDtypeStruct((sessions * steps, width), BF16),
        grid=(4,),
        in_specs=[pl.BlockSpec(memory_space=pltpu.SMEM), taken, taken],
        out_specs=pl.BlockSpec((block * steps, width), lambda i: (i, 0)),
        scratch_shapes=[pltpu.VMEM((width // 128, block * steps, 128), F32)],
        compiler_params=pltpu.CompilerParams(vmem_limit_bytes=VMEM_LIMIT),
    )(group, own, other)


def swap(value, axis):
    return lax.ppermute(value, axis, [(0, 1), (1, 0)])


def after(value, earlier):
    return lax.optimization_barrier((value, earlier))[0]


class Ring:
    def __init__(self, count, own, other):
        order = ring_order(count)
        self.count = count
        self.pairs = []
        for p in range(count):
            here, there = order[p], order[(p + 1) % count]
            self.pairs += [(2 * here, 2 * there), (2 * there + 1, 2 * here + 1)]
        self.item = jnp.stack([own, other])
        self.blocks, self.steps, self.rounds = [own], [(0, 0)], 0

    def round(self, earlier=None):
        self.rounds += 1
        item = self.item
        if 2 * self.rounds == self.count:
            part = item.shape[1] // 2
            item = lax.dynamic_slice_in_dim(item, lax.axis_index("segment") * part, part, axis=1)
        if earlier is not None:
            item = after(item, earlier)
        item = lax.ppermute(item, ("streams", "segment"), self.pairs)
        self.item = item
        self.blocks += [item, swap(item, "segment")]
        self.steps += [(self.rounds, 0), (self.rounds, 1)]
        return item


def local(
    count,
    latent,
    conv_weight,
    conv_bias,
    tail_cache,
    input_cache,
    resume_slot,
    res_weight,
    res_bias,
    skip_weight,
    skip_bias,
):
    group = lax.axis_index("groups")
    group_word = group[None].astype(jnp.int32)
    rows, tap_count, width = conv_weight.shape
    sessions = latent.shape[0]
    taps = tap_count // 4

    halves = []
    for first in (0, tap_count // 2):
        part = lax.dynamic_slice_in_dim(conv_weight, first + group * taps, taps, axis=1)
        halves.append(part.transpose(1, 0, 2))

    use_ring = rows % 128 == 0 and count % 2 == 0
    if use_ring:
        other = swap(halves[0], "segment")
        prepared = swap(after(halves[1], other), "segment")
        up_ring, tail_ring = Ring(count, halves[0], other), Ring(count, halves[1], prepared)
    else:
        prepared = halves[1]

    portion = sessions // count
    cap = tail_cache.shape[0] // count
    half_taps, history = tail_cache.shape[1], input_cache.shape[1]
    slot_step = jnp.broadcast_to(
        resume_slot.astype(BF16)[:, None, None], (count * cap, 1, width)
    )
    filler = jnp.zeros((count * cap, half_taps - history - 1, width), BF16)
    beside = jnp.concatenate([input_cache, slot_step, filler], axis=1)
    stored = jnp.concatenate([tail_cache, beside], axis=2).reshape(count, cap * half_taps, 2 * width)
    parcel = jnp.concatenate([latent.reshape(count, portion, 2 * width), stored], axis=1)
    parcel = after(parcel, prepared)
    parcel = lax.all_to_all(parcel, "streams", split_axis=0, concat_axis=0, tiled=True)
    handed = parcel[:, :portion].reshape(sessions, 2 * width)
    stored = parcel[:, portion:].reshape(count * cap, half_taps, 2 * width)

    near_half = apply_elu(handed.astype(F32)).astype(BF16)
    far_half = swap(near_half, "groups")
    sides = (near_half, swap(near_half, "segment"), far_half, swap(far_half, "segment"))

    slots = stored[:, history, width:].astype(jnp.int32)[:, :1]
    one_hot = (slots == jnp.arange(sessions, dtype=jnp.int32)[None, :]).astype(BF16)
    packed = jnp.concatenate([stored[:, :, :width], stored[:, :history, width:]], axis=1)
    prev = jnp.einsum("js,jkc->ksc", one_hot, packed, preferred_element_type=F32).astype(BF16)

    res_theirs = swap(res_weight, "segment")

    if use_ring:
        for r in range(count // 2):
            up_ring.round()
            seen = tail_ring.round(far_half if r == count // 2 - 2 else None)
            if r == count // 2 - 2:
                nearly_done = seen
        up_ring.blocks[0] = after(up_ring.blocks[0], nearly_done)
        gathered = [(ring.blocks, ring.steps) for ring in (up_ring, tail_ring)]
    else:
        gathered = [
            ([lax.all_gather(own, "streams", axis=1, tiled=True)], [None]) for own in halves
        ]
    own_up, away_up = spread_taps(sides, *gathered[0], count, F32)
    own_tail, away_tail = spread_taps(sides, *gathered[1], count, BF16)
    other_up = swap(away_up, "groups")
    other_tail = swap(away_tail, "groups")

    own_up = after(own_up, (away_tail, res_theirs))
    bias = conv_bias[None]
    mine = excite(group_word, own_up, other_up, prev, bias)
    theirs = swap(mine, "segment")
    decoded = residual(
        group_word,
        own_up,
        other_up,
        prev,
        mine,
        theirs,
        bias,
        res_weight,
        res_theirs,
        res_bias[None],
        skip_weight,
        skip_bias[None],
    )
    decoded, other_tail = lax.optimization_barrier((decoded, other_tail))
    new_tail = weave(group_word, own_tail, other_tail)
    shape = (sessions, half_taps, width)
    return decoded.reshape(shape), new_tail.reshape(shape)


def solution(mesh):
    placed = (
        P(("groups", "streams"), "segment"),
        P("streams", None, "segment"),
        P("segment"),
        P(("groups", "streams"), None, "segment"),
        P(("groups", "streams"), None, "segment"),
        P(("groups", "streams")),
        P(None, "segment", None),
        P(),
        P(None, "segment"),
        P("segment"),
    )
    return jax.shard_map(
        functools.partial(local, mesh.shape["streams"]),
        mesh=mesh,
        in_specs=placed,
        out_specs=(
            P(("groups", "streams"), None, "segment"),
            P(("groups", "streams"), None, "segment"),
        ),
        check_vma=False,
    )
```

```python
import functools

import jax
import jax.numpy as jnp
from jax import lax
from jax.experimental import pallas as pl
from jax.experimental.pallas import tpu as pltpu
from jax.sharding import PartitionSpec as P

VMEM_LIMIT = 16 * 1024 * 1024
F32 = jnp.float32
BF16 = jnp.bfloat16
VMEM = pl.BlockSpec(memory_space=pltpu.VMEM)


def apply_elu(values):
    return jnp.where(values > 0, values, jnp.exp(jnp.minimum(values, 0.0)) - 1.0)


def ring_order(count):
    return [2 * p if p < count // 2 else 2 * (count - 1 - p) + 1 for p in range(count)]


def ring_place(stream, count):
    return jnp.where(stream % 2 == 0, stream // 2, count - 1 - stream // 2)


def ring_stream(place, count):
    return jnp.where(place < count // 2, 2 * place, 2 * (count - 1 - place) + 1)


def spread_kernel(count, steps, *refs):
    blocks = refs[: len(steps)]
    sides, (home_ref, *away_refs) = refs[len(steps) : len(steps) + 4], refs[len(steps) + 4 : -3]
    kernel_rows, inputs, sems = refs[-3:]
    taps = kernel_rows.shape[0]
    rows = blocks[0].shape[-2]
    core = lax.axis_index("segment")
    place = ring_place(lax.axis_index("streams"), count)
    copies = []
    for slot, (step, block) in enumerate(zip(steps, blocks)):
        if step is None:
            source, target = block, kernel_rows
        else:
            distance, passed = step
            taker = 1 - core if passed else core
            stream = ring_stream(
                lax.rem(place + (2 * taker - 1) * distance + count, count), count
            )
            source = block if len(block.shape) == 3 else block.at[passed]
            part = source.shape[0]
            first = 0 if part == taps else taker * part
            target = kernel_rows.at[
                pl.ds(first, part), pl.ds(pl.multiple_of(stream * rows, rows), rows), :
            ]
        copy = pltpu.make_async_copy(source, target, sems.at[slot])
        copy.start()
        copies.append(copy)
    sessions, half = sides[0].shape
    for index, side in enumerate(sides):
        column = core if index % 2 == 0 else 1 - core
        first = index // 2 * sessions
        inputs[first : first + sessions, pl.ds(pl.multiple_of(column * half, half), half)] = side[...]
    for copy in copies:
        copy.wait()

    for part, away_ref in enumerate(away_refs):

        @pl.loop(0, away_ref.shape[0])
        def _(index):
            tap = part * away_ref.shape[0] + index
            product = jnp.dot(inputs[...], kernel_rows[tap], preferred_element_type=F32)
            home_ref[tap] = product[:sessions].astype(home_ref.dtype)
            away_ref[index] = product[sessions:].astype(away_ref.dtype)


def spread_taps(sides, blocks, steps, count, home_type):
    taps, _, width = blocks[0].shape
    sessions, depth = sides[0].shape[0], 2 * sides[0].shape[1]
    return pl.pallas_call(
        functools.partial(spread_kernel, count, steps),
        out_shape=(
            jax.ShapeDtypeStruct((taps, sessions, width), home_type),
            jax.ShapeDtypeStruct((taps // 2, sessions, width), BF16),
            jax.ShapeDtypeStruct((taps // 2, sessions, width), BF16),
        ),
        in_specs=[pl.BlockSpec(memory_space=pl.ANY)] * len(blocks) + [VMEM] * 4,
        out_specs=(VMEM, VMEM, VMEM),
        scratch_shapes=[
            pltpu.VMEM((taps, depth, width), BF16),
            pltpu.VMEM((2 * sessions, depth), BF16),
            pltpu.SemaphoreType.DMA((len(blocks),)),
        ],
        compiler_params=pltpu.CompilerParams(vmem_limit_bytes=VMEM_LIMIT),
        cost_estimate=pl.CostEstimate(
            flops=4 * taps * sessions * depth * width,
            bytes_accessed=2 * taps * depth * width + 4 * sessions * depth + 6 * taps * sessions * width,
            transcendentals=0,
        ),
    )(*blocks, *sides)


def each_step(group, own_ref, other_refs):
    taps = own_ref.shape[0]
    for tap in range(taps):
        yield group * taps + tap, own_ref[tap].astype(F32)
    for tap in range(taps):
        part, index = divmod(tap, other_refs[0].shape[0])
        yield (1 - group) * taps + tap, other_refs[part][index].astype(F32)


def excite_kernel(group_ref, own_ref, first_ref, second_ref, prev_ref, bias_ref, window_ref):
    steps = 2 * own_ref.shape[0]
    history = prev_ref.shape[0] - steps
    for step in range(history):
        window_ref[step] = prev_ref[steps + step]
    for step, value in each_step(group_ref[0], own_ref, (first_ref, second_ref)):
        up = value + prev_ref[step].astype(F32) + bias_ref[...]
        window_ref[history + step] = apply_elu(up).astype(BF16)


def excite(group, own, other, prev, bias):
    return pl.pallas_call(
        excite_kernel,
        out_shape=jax.ShapeDtypeStruct(prev.shape, BF16),
        in_specs=[pl.BlockSpec(memory_space=pltpu.SMEM)] + [VMEM] * 5,
        out_specs=VMEM,
        compiler_params=pltpu.CompilerParams(vmem_limit_bytes=VMEM_LIMIT),
    )(group, own, *other, prev, bias)


def residual_kernel(
    group_ref,
    own_ref,
    first_ref,
    second_ref,
    prev_ref,
    mine_ref,
    theirs_ref,
    bias_ref,
    res_mine_ref,
    res_theirs_ref,
    res_bias_ref,
    skip_ref,
    skip_bias_ref,
    out_ref,
    products,
    frames,
):
    taps, block, width = own_ref.shape
    steps = 2 * taps
    branch = None
    for source, weights in ((mine_ref, res_mine_ref), (theirs_ref, res_theirs_ref)):
        for offset in range(weights.shape[0]):
            term = jnp.dot(
                source[offset : offset + steps].reshape(steps * block, width),
                weights[offset],
                preferred_element_type=F32,
            )
            branch = term if branch is None else branch + term
    hidden = apply_elu(branch + res_bias_ref[...]).astype(BF16)
    projected = jnp.dot(hidden, skip_ref[...], preferred_element_type=F32)
    products[...] = projected.reshape(products.shape)
    for step, value in each_step(group_ref[0], own_ref, (first_ref, second_ref)):
        up = value + prev_ref[step].astype(F32) + bias_ref[...]
        mixed = up + products[step] + skip_bias_ref[...]
        for part in range(width // 128):
            frames.at[part][pl.ds(step, block, stride=steps), :] = mixed[
                :, part * 128 : (part + 1) * 128
            ]
    for part in range(width // 128):
        out_ref[:, part * 128 : (part + 1) * 128] = frames[part].astype(BF16)


def residual(group, own, other, prev, mine, theirs, *parameters):
    taps, sessions, width = own.shape
    steps, block = 2 * taps, sessions // 4

    def blocks(array):
        return pl.BlockSpec((array.shape[0], block, width), lambda i: (0, i, 0))

    arrays = (own, *other, prev, mine, theirs)
    return pl.pallas_call(
        residual_kernel,
        out_shape=jax.ShapeDtypeStruct((sessions * steps, width), BF16),
        grid=(4,),
        in_specs=[pl.BlockSpec(memory_space=pltpu.SMEM)]
        + [blocks(array) for array in arrays]
        + [VMEM] * len(parameters),
        out_specs=pl.BlockSpec((block * steps, width), lambda i: (i, 0)),
        scratch_shapes=[
            pltpu.VMEM((steps, block, width), F32),
            pltpu.VMEM((width // 128, block * steps, 128), F32),
        ],
        compiler_params=pltpu.CompilerParams(vmem_limit_bytes=VMEM_LIMIT),
    )(group, *arrays, *parameters)


def weave_kernel(group_ref, own_ref, first_ref, second_ref, out_ref, frames):
    taps, block, width = own_ref.shape
    for step, value in each_step(group_ref[0], own_ref, (first_ref, second_ref)):
        for part in range(width // 128):
            frames.at[part][pl.ds(step, block, stride=2 * taps), :] = value[
                :, part * 128 : (part + 1) * 128
            ]
    for part in range(width // 128):
        out_ref[:, part * 128 : (part + 1) * 128] = frames[part].astype(BF16)


def weave(group, own, other):
    taps, sessions, width = own.shape
    steps, block = 2 * taps, sessions // 4
    arrays = (own, *other)
    taken = [pl.BlockSpec((array.shape[0], block, width), lambda i: (0, i, 0)) for array in arrays]
    return pl.pallas_call(
        weave_kernel,
        out_shape=jax.ShapeDtypeStruct((sessions * steps, width), BF16),
        grid=(4,),
        in_specs=[pl.BlockSpec(memory_space=pltpu.SMEM)] + taken,
        out_specs=pl.BlockSpec((block * steps, width), lambda i: (i, 0)),
        scratch_shapes=[pltpu.VMEM((width // 128, block * steps, 128), F32)],
        compiler_params=pltpu.CompilerParams(vmem_limit_bytes=VMEM_LIMIT),
    )(group, *arrays)


def swap(value, axis):
    return lax.ppermute(value, axis, [(0, 1), (1, 0)])


def after(value, earlier):
    return lax.optimization_barrier((value, earlier))[0]


class Ring:
    def __init__(self, count, own, other):
        order = ring_order(count)
        self.count = count
        self.pairs = []
        for p in range(count):
            here, there = order[p], order[(p + 1) % count]
            self.pairs += [(2 * here, 2 * there), (2 * there + 1, 2 * here + 1)]
        self.item = jnp.stack([own, other])
        self.blocks, self.steps, self.rounds = [own], [(0, 0)], 0

    def round(self, earlier=None, passed_after=None):
        self.rounds += 1
        item = self.item
        if 2 * self.rounds == self.count:
            part = item.shape[1] // 2
            item = lax.dynamic_slice_in_dim(item, lax.axis_index("segment") * part, part, axis=1)
        if earlier is not None:
            item = after(item, earlier)
        item = lax.ppermute(item, ("streams", "segment"), self.pairs)
        self.item = item
        given = item if passed_after is None else after(item, passed_after)
        self.blocks += [item, swap(given, "segment")]
        self.steps += [(self.rounds, 0), (self.rounds, 1)]
        return item


def local(
    count,
    latent,
    conv_weight,
    conv_bias,
    tail_cache,
    input_cache,
    resume_slot,
    res_weight,
    res_bias,
    skip_weight,
    skip_bias,
):
    group = lax.axis_index("groups")
    group_word = group[None].astype(jnp.int32)
    rows, tap_count, width = conv_weight.shape
    sessions = latent.shape[0]
    taps = tap_count // 4

    halves = []
    for first in (0, tap_count // 2):
        part = lax.dynamic_slice_in_dim(conv_weight, first + group * taps, taps, axis=1)
        halves.append(part.transpose(1, 0, 2))

    use_ring = rows % 128 == 0 and count % 2 == 0 and count > 4
    if use_ring:
        other = swap(halves[0], "segment")
        prepared = swap(after(halves[1], other), "segment")
        up_ring, tail_ring = Ring(count, halves[0], other), Ring(count, halves[1], prepared)
    else:
        prepared = halves[1]

    portion = sessions // count
    cap = tail_cache.shape[0] // count
    half_taps, history = tail_cache.shape[1], input_cache.shape[1]
    slot_step = jnp.broadcast_to(
        resume_slot.astype(BF16)[:, None, None], (count * cap, 1, width)
    )
    filler = jnp.zeros((count * cap, half_taps - history - 1, width), BF16)
    beside = jnp.concatenate([input_cache, slot_step, filler], axis=1)
    stored = jnp.concatenate([tail_cache, beside], axis=2).reshape(count, cap * half_taps, 2 * width)
    parcel = jnp.concatenate([latent.reshape(count, portion, 2 * width), stored], axis=1)
    parcel = after(parcel, prepared)
    parcel = lax.all_to_all(parcel, "streams", split_axis=0, concat_axis=0, tiled=True)
    handed = parcel[:, :portion].reshape(sessions, 2 * width)
    stored = parcel[:, portion:].reshape(count * cap, half_taps, 2 * width)

    near_half = apply_elu(handed.astype(F32)).astype(BF16)
    far_half = swap(near_half, "groups")
    sides = (near_half, swap(near_half, "segment"), far_half, swap(far_half, "segment"))

    slots = stored[:, history, width:].astype(jnp.int32)[:, :1]
    one_hot = (slots == jnp.arange(sessions, dtype=jnp.int32)[None, :]).astype(BF16)
    packed = jnp.concatenate([stored[:, :, :width], stored[:, :history, width:]], axis=1)
    prev = jnp.einsum("js,jkc->ksc", one_hot, packed, preferred_element_type=F32).astype(BF16)

    res_theirs = swap(res_weight, "segment")

    if use_ring:
        last = count // 2 - 1
        leading = [up_ring.round(far_half if r == last else None) for r in range(last + 1)]
        for r in range(last - 1):
            item = tail_ring.round(leading[min(r + 1, last)])
            if r == 0:
                up_ring.blocks[0] = after(up_ring.blocks[0], item)
        own_up, *away_up = spread_taps(sides, up_ring.blocks, up_ring.steps, count, F32)
        tail_ring.round(away_up)
        other_up = [swap(part, "groups") for part in away_up]
        tail_ring.round(other_up[0], passed_after=other_up[1])
        own_tail, *away_tail = spread_taps(sides, tail_ring.blocks, tail_ring.steps, count, BF16)
    else:
        whole = [lax.all_gather(own, "streams", axis=1, tiled=True) for own in halves]
        own_up, *away_up = spread_taps(sides, whole[:1], [None], count, F32)
        other_up = [swap(part, "groups") for part in away_up]
        own_tail, *away_tail = spread_taps(sides, whole[1:], [None], count, BF16)
    other_tail = [swap(part, "groups") for part in away_tail]

    own_up = after(own_up, (away_tail, res_theirs))
    bias = conv_bias[None]
    mine = excite(group_word, own_up, other_up, prev, bias)
    theirs = swap(mine, "segment")
    decoded = residual(
        group_word,
        own_up,
        other_up,
        prev,
        mine,
        theirs,
        bias,
        res_weight,
        res_theirs,
        res_bias[None],
        skip_weight,
        skip_bias[None],
    )
    decoded, other_tail = lax.optimization_barrier((decoded, other_tail))
    new_tail = weave(group_word, own_tail, other_tail)
    shape = (sessions, half_taps, width)
    return decoded.reshape(shape), new_tail.reshape(shape)


def solution(mesh):
    placed = (
        P(("groups", "streams"), "segment"),
        P("streams", None, "segment"),
        P("segment"),
        P(("groups", "streams"), None, "segment"),
        P(("groups", "streams"), None, "segment"),
        P(("groups", "streams")),
        P(None, "segment", None),
        P(),
        P(None, "segment"),
        P("segment"),
    )
    return jax.shard_map(
        functools.partial(local, mesh.shape["streams"]),
        mesh=mesh,
        in_specs=placed,
        out_specs=(
            P(("groups", "streams"), None, "segment"),
            P(("groups", "streams"), None, "segment"),
        ),
        check_vma=False,
    )
```

```python
import functools

import jax
import jax.numpy as jnp
from jax import lax
from jax.experimental import pallas as pl
from jax.experimental.pallas import tpu as pltpu
from jax.sharding import PartitionSpec as P

VMEM_LIMIT = 16 * 1024 * 1024
F32 = jnp.float32
BF16 = jnp.bfloat16
VMEM = pl.BlockSpec(memory_space=pltpu.VMEM)


def apply_elu(values):
    return jnp.where(values > 0, values, jnp.exp(jnp.minimum(values, 0.0)) - 1.0)


def ring_order(count):
    return [2 * p if p < count // 2 else 2 * (count - 1 - p) + 1 for p in range(count)]


def ring_place(stream, count):
    return jnp.where(stream % 2 == 0, stream // 2, count - 1 - stream // 2)


def ring_stream(place, count):
    return jnp.where(place < count // 2, 2 * place, 2 * (count - 1 - place) + 1)


def spread_kernel(count, steps, *refs):
    blocks = refs[: len(steps)]
    sides, (home_ref, *away_refs) = refs[len(steps) : len(steps) + 4], refs[len(steps) + 4 : -3]
    kernel_rows, inputs, sems = refs[-3:]
    taps = kernel_rows.shape[0]
    rows = blocks[0].shape[-2]
    core = lax.axis_index("segment")
    place = ring_place(lax.axis_index("streams"), count)
    copies = []
    for slot, (step, block) in enumerate(zip(steps, blocks)):
        if step is None:
            source, target = block, kernel_rows
        else:
            distance, passed = step
            taker = 1 - core if passed else core
            stream = ring_stream(
                lax.rem(place + (2 * taker - 1) * distance + count, count), count
            )
            source = block if len(block.shape) == 3 else block.at[passed]
            part = source.shape[0]
            first = 0 if part == taps else taker * part
            target = kernel_rows.at[
                pl.ds(first, part), pl.ds(pl.multiple_of(stream * rows, rows), rows), :
            ]
        copy = pltpu.make_async_copy(source, target, sems.at[slot])
        copy.start()
        copies.append(copy)
    sessions, half = sides[0].shape
    for index, side in enumerate(sides):
        column = core if index % 2 == 0 else 1 - core
        first = index // 2 * sessions
        inputs[first : first + sessions, pl.ds(pl.multiple_of(column * half, half), half)] = side[...]
    for copy in copies:
        copy.wait()

    for part, away_ref in enumerate(away_refs):

        @pl.loop(0, away_ref.shape[0])
        def _(index):
            tap = part * away_ref.shape[0] + index
            product = jnp.dot(inputs[...], kernel_rows[tap], preferred_element_type=F32)
            home_ref[tap] = product[:sessions].astype(home_ref.dtype)
            away_ref[index] = product[sessions:].astype(away_ref.dtype)


def spread_taps(sides, blocks, steps, count, home_type):
    taps, _, width = blocks[0].shape
    sessions, depth = sides[0].shape[0], 2 * sides[0].shape[1]
    return pl.pallas_call(
        functools.partial(spread_kernel, count, steps),
        out_shape=(
            jax.ShapeDtypeStruct((taps, sessions, width), home_type),
            jax.ShapeDtypeStruct((taps // 2, sessions, width), BF16),
            jax.ShapeDtypeStruct((taps // 2, sessions, width), BF16),
        ),
        in_specs=[pl.BlockSpec(memory_space=pl.ANY)] * len(blocks) + [VMEM] * 4,
        out_specs=(VMEM, VMEM, VMEM),
        scratch_shapes=[
            pltpu.VMEM((taps, depth, width), BF16),
            pltpu.VMEM((2 * sessions, depth), BF16),
            pltpu.SemaphoreType.DMA((len(blocks),)),
        ],
        compiler_params=pltpu.CompilerParams(vmem_limit_bytes=VMEM_LIMIT),
        cost_estimate=pl.CostEstimate(
            flops=4 * taps * sessions * depth * width,
            bytes_accessed=2 * taps * depth * width + 4 * sessions * depth + 6 * taps * sessions * width,
            transcendentals=0,
        ),
    )(*blocks, *sides)


def each_step(group, own_ref, other_refs):
    taps = own_ref.shape[0]
    for tap in range(taps):
        yield group * taps + tap, own_ref[tap].astype(F32)
    for tap in range(taps):
        part, index = divmod(tap, other_refs[0].shape[0])
        yield (1 - group) * taps + tap, other_refs[part][index].astype(F32)


def excite_kernel(group_ref, own_ref, first_ref, second_ref, prev_ref, bias_ref, window_ref):
    steps = 2 * own_ref.shape[0]
    history = prev_ref.shape[0] - steps
    for step in range(history):
        window_ref[step] = prev_ref[steps + step]
    for step, value in each_step(group_ref[0], own_ref, (first_ref, second_ref)):
        up = value + prev_ref[step].astype(F32) + bias_ref[...]
        window_ref[history + step] = apply_elu(up).astype(BF16)


def excite(group, own, other, prev, bias):
    return pl.pallas_call(
        excite_kernel,
        out_shape=jax.ShapeDtypeStruct(prev.shape, BF16),
        in_specs=[pl.BlockSpec(memory_space=pltpu.SMEM)] + [VMEM] * 5,
        out_specs=VMEM,
        compiler_params=pltpu.CompilerParams(vmem_limit_bytes=VMEM_LIMIT),
    )(group, own, *other, prev, bias)


def residual_kernel(
    group_ref,
    own_ref,
    first_ref,
    second_ref,
    prev_ref,
    mine_ref,
    theirs_ref,
    bias_ref,
    res_mine_ref,
    res_theirs_ref,
    res_bias_ref,
    skip_ref,
    skip_bias_ref,
    out_ref,
    products,
    frames,
):
    taps, block, width = own_ref.shape
    steps = 2 * taps
    branch = None
    for source, weights in ((mine_ref, res_mine_ref), (theirs_ref, res_theirs_ref)):
        for offset in range(weights.shape[0]):
            term = jnp.dot(
                source[offset : offset + steps].reshape(steps * block, width),
                weights[offset],
                preferred_element_type=F32,
            )
            branch = term if branch is None else branch + term
    hidden = apply_elu(branch + res_bias_ref[...]).astype(BF16)
    projected = jnp.dot(hidden, skip_ref[...], preferred_element_type=F32)
    products[...] = projected.reshape(products.shape)
    for step, value in each_step(group_ref[0], own_ref, (first_ref, second_ref)):
        up = value + prev_ref[step].astype(F32) + bias_ref[...]
        mixed = up + products[step] + skip_bias_ref[...]
        for part in range(width // 128):
            frames.at[part][pl.ds(step, block, stride=steps), :] = mixed[
                :, part * 128 : (part + 1) * 128
            ]
    for part in range(width // 128):
        out_ref[:, part * 128 : (part + 1) * 128] = frames[part].astype(BF16)


def residual(group, own, other, prev, mine, theirs, *parameters):
    taps, sessions, width = own.shape
    steps, block = 2 * taps, sessions // 4

    def blocks(array):
        return pl.BlockSpec((array.shape[0], block, width), lambda i: (0, i, 0))

    arrays = (own, *other, prev, mine, theirs)
    return pl.pallas_call(
        residual_kernel,
        out_shape=jax.ShapeDtypeStruct((sessions * steps, width), BF16),
        grid=(4,),
        in_specs=[pl.BlockSpec(memory_space=pltpu.SMEM)]
        + [blocks(array) for array in arrays]
        + [VMEM] * len(parameters),
        out_specs=pl.BlockSpec((block * steps, width), lambda i: (i, 0)),
        scratch_shapes=[
            pltpu.VMEM((steps, block, width), F32),
            pltpu.VMEM((width // 128, block * steps, 128), F32),
        ],
        compiler_params=pltpu.CompilerParams(vmem_limit_bytes=VMEM_LIMIT),
    )(group, *arrays, *parameters)


def weave_kernel(group_ref, own_ref, first_ref, second_ref, out_ref, frames):
    taps, block, width = own_ref.shape
    for step, value in each_step(group_ref[0], own_ref, (first_ref, second_ref)):
        for part in range(width // 128):
            frames.at[part][pl.ds(step, block, stride=2 * taps), :] = value[
                :, part * 128 : (part + 1) * 128
            ]
    for part in range(width // 128):
        out_ref[:, part * 128 : (part + 1) * 128] = frames[part].astype(BF16)


def weave(group, own, other):
    taps, sessions, width = own.shape
    steps, block = 2 * taps, sessions // 4
    arrays = (own, *other)
    taken = [pl.BlockSpec((array.shape[0], block, width), lambda i: (0, i, 0)) for array in arrays]
    return pl.pallas_call(
        weave_kernel,
        out_shape=jax.ShapeDtypeStruct((sessions * steps, width), BF16),
        grid=(4,),
        in_specs=[pl.BlockSpec(memory_space=pltpu.SMEM)] + taken,
        out_specs=pl.BlockSpec((block * steps, width), lambda i: (i, 0)),
        scratch_shapes=[pltpu.VMEM((width // 128, block * steps, 128), F32)],
        compiler_params=pltpu.CompilerParams(vmem_limit_bytes=VMEM_LIMIT),
    )(group, *arrays)


def swap(value, axis):
    return lax.ppermute(value, axis, [(0, 1), (1, 0)])


def after(value, earlier):
    return lax.optimization_barrier((value, earlier))[0]


class Ring:
    def __init__(self, count, own, other):
        order = ring_order(count)
        self.count = count
        self.pairs = []
        for p in range(count):
            here, there = order[p], order[(p + 1) % count]
            self.pairs += [(2 * here, 2 * there), (2 * there + 1, 2 * here + 1)]
        self.item = jnp.stack([own, other])
        self.blocks, self.steps, self.rounds = [own], [(0, 0)], 0

    def round(self, earlier=None, passed_after=None):
        self.rounds += 1
        item = self.item
        if 2 * self.rounds == self.count:
            part = item.shape[1] // 2
            item = lax.dynamic_slice_in_dim(item, lax.axis_index("segment") * part, part, axis=1)
        if earlier is not None:
            item = after(item, earlier)
        item = lax.ppermute(item, ("streams", "segment"), self.pairs)
        self.item = item
        given = item if passed_after is None else after(item, passed_after)
        self.blocks += [item, swap(given, "segment")]
        self.steps += [(self.rounds, 0), (self.rounds, 1)]
        return item


def local(
    count,
    latent,
    conv_weight,
    conv_bias,
    tail_cache,
    input_cache,
    resume_slot,
    res_weight,
    res_bias,
    skip_weight,
    skip_bias,
):
    group = lax.axis_index("groups")
    group_word = group[None].astype(jnp.int32)
    rows, tap_count, width = conv_weight.shape
    sessions = latent.shape[0]
    taps = tap_count // 4

    halves = []
    for first in (0, tap_count // 2):
        part = lax.dynamic_slice_in_dim(conv_weight, first + group * taps, taps, axis=1)
        halves.append(part.transpose(1, 0, 2))

    use_ring = rows % 128 == 0 and count % 2 == 0 and count > 4
    if use_ring:
        other = swap(halves[0], "segment")
        prepared = swap(after(halves[1], other), "segment")
        up_ring, tail_ring = Ring(count, halves[0], other), Ring(count, halves[1], prepared)
    else:
        prepared = halves[1]

    portion = sessions // count
    cap = tail_cache.shape[0] // count
    half_taps, history = tail_cache.shape[1], input_cache.shape[1]
    slot_step = jnp.broadcast_to(
        resume_slot.astype(BF16)[:, None, None], (count * cap, 1, width)
    )
    filler = jnp.zeros((count * cap, half_taps - history - 1, width), BF16)
    beside = jnp.concatenate([input_cache, slot_step, filler], axis=1)
    stored = jnp.concatenate([tail_cache, beside], axis=2).reshape(count, cap * half_taps, 2 * width)
    parcel = jnp.concatenate([latent.reshape(count, portion, 2 * width), stored], axis=1)
    parcel = after(parcel, prepared)
    parcel = lax.all_to_all(parcel, "streams", split_axis=0, concat_axis=0, tiled=True)
    handed = parcel[:, :portion].reshape(sessions, 2 * width)
    stored = parcel[:, portion:].reshape(count * cap, half_taps, 2 * width)

    near_half = apply_elu(handed.astype(F32)).astype(BF16)
    near_other = swap(near_half, "segment")
    far_half = swap(after(near_half, near_other), "groups")
    sides = (near_half, near_other, far_half, swap(far_half, "segment"))

    slots = stored[:, history, width:].astype(jnp.int32)[:, :1]
    one_hot = (slots == jnp.arange(sessions, dtype=jnp.int32)[None, :]).astype(BF16)
    packed = jnp.concatenate([stored[:, :, :width], stored[:, :history, width:]], axis=1)
    prev = jnp.einsum("js,jkc->ksc", one_hot, packed, preferred_element_type=F32).astype(BF16)

    res_theirs = swap(res_weight, "segment")

    if use_ring:
        last = count // 2 - 1
        leading = [up_ring.round(far_half if r == last else None) for r in range(last + 1)]
        for r in range(last - 1):
            item = tail_ring.round(leading[min(r + 1, last)])
            if r == 0:
                up_ring.blocks[0] = after(up_ring.blocks[0], item)
        own_up, *away_up = spread_taps(sides, up_ring.blocks, up_ring.steps, count, F32)
        tail_ring.round(away_up)
        other_up = [swap(part, "groups") for part in away_up]
        tail_ring.round(other_up[0], passed_after=other_up[1])
        own_tail, *away_tail = spread_taps(sides, tail_ring.blocks, tail_ring.steps, count, BF16)
    else:
        whole = [lax.all_gather(own, "streams", axis=1, tiled=True) for own in halves]
        own_up, *away_up = spread_taps(sides, whole[:1], [None], count, F32)
        other_up = [swap(part, "groups") for part in away_up]
        own_tail, *away_tail = spread_taps(sides, whole[1:], [None], count, BF16)
    other_tail = [swap(part, "groups") for part in away_tail]

    own_up = after(own_up, (away_tail, res_theirs))
    bias = conv_bias[None]
    mine = excite(group_word, own_up, other_up, prev, bias)
    theirs = swap(mine, "segment")
    decoded = residual(
        group_word,
        own_up,
        other_up,
        prev,
        mine,
        theirs,
        bias,
        res_weight,
        res_theirs,
        res_bias[None],
        skip_weight,
        skip_bias[None],
    )
    decoded, other_tail = lax.optimization_barrier((decoded, other_tail))
    new_tail = weave(group_word, own_tail, other_tail)
    shape = (sessions, half_taps, width)
    return decoded.reshape(shape), new_tail.reshape(shape)


def solution(mesh):
    placed = (
        P(("groups", "streams"), "segment"),
        P("streams", None, "segment"),
        P("segment"),
        P(("groups", "streams"), None, "segment"),
        P(("groups", "streams"), None, "segment"),
        P(("groups", "streams")),
        P(None, "segment", None),
        P(),
        P(None, "segment"),
        P("segment"),
    )
    return jax.shard_map(
        functools.partial(local, mesh.shape["streams"]),
        mesh=mesh,
        in_specs=placed,
        out_specs=(
            P(("groups", "streams"), None, "segment"),
            P(("groups", "streams"), None, "segment"),
        ),
        check_vma=False,
    )
```

```python
import functools

import jax
import jax.numpy as jnp
from jax import lax
from jax.experimental import pallas as pl
from jax.experimental.pallas import tpu as pltpu
from jax.sharding import PartitionSpec as P

VMEM_LIMIT = 16 * 1024 * 1024
F32 = jnp.float32
BF16 = jnp.bfloat16
VMEM = pl.BlockSpec(memory_space=pltpu.VMEM)


def apply_elu(values):
    return jnp.where(values > 0, values, jnp.exp(jnp.minimum(values, 0.0)) - 1.0)


def ring_order(count):
    return [2 * p if p < count // 2 else 2 * (count - 1 - p) + 1 for p in range(count)]


def ring_place(stream, count):
    return jnp.where(stream % 2 == 0, stream // 2, count - 1 - stream // 2)


def ring_stream(place, count):
    return jnp.where(place < count // 2, 2 * place, 2 * (count - 1 - place) + 1)


def spread_kernel(count, steps, *refs):
    blocks = refs[: len(steps)]
    sides, (home_ref, away_ref) = refs[len(steps) : len(steps) + 4], refs[len(steps) + 4 : -3]
    kernel_rows, inputs, sems = refs[-3:]
    taps = kernel_rows.shape[0]
    rows = blocks[0].shape[-2]
    core = lax.axis_index("segment")
    place = ring_place(lax.axis_index("streams"), count)
    copies = []
    for slot, (step, block) in enumerate(zip(steps, blocks)):
        if step is None:
            source, target = block, kernel_rows
        else:
            distance, passed = step
            taker = 1 - core if passed else core
            stream = ring_stream(
                lax.rem(place + (2 * taker - 1) * distance + count, count), count
            )
            source = block if len(block.shape) == 3 else block.at[passed]
            part = source.shape[0]
            first = 0 if part == taps else taker * part
            target = kernel_rows.at[
                pl.ds(first, part), pl.ds(pl.multiple_of(stream * rows, rows), rows), :
            ]
        copy = pltpu.make_async_copy(source, target, sems.at[slot])
        copy.start()
        copies.append(copy)
    sessions, half = sides[0].shape
    for index, side in enumerate(sides):
        column = core if index % 2 == 0 else 1 - core
        first = index // 2 * sessions
        inputs[first : first + sessions, pl.ds(pl.multiple_of(column * half, half), half)] = side[...]
    for copy in copies:
        copy.wait()

    @pl.loop(0, taps)
    def _(tap):
        product = jnp.dot(inputs[...], kernel_rows[tap], preferred_element_type=F32)
        home_ref[tap] = product[:sessions].astype(home_ref.dtype)
        away_ref[tap] = product[sessions:].astype(away_ref.dtype)


def spread_taps(sides, blocks, steps, count, home_type):
    taps, _, width = blocks[0].shape
    sessions, depth = sides[0].shape[0], 2 * sides[0].shape[1]
    return pl.pallas_call(
        functools.partial(spread_kernel, count, steps),
        out_shape=(
            jax.ShapeDtypeStruct((taps, sessions, width), home_type),
            jax.ShapeDtypeStruct((taps, sessions, width), BF16),
        ),
        in_specs=[pl.BlockSpec(memory_space=pl.ANY)] * len(blocks) + [VMEM] * 4,
        out_specs=(VMEM, VMEM),
        scratch_shapes=[
            pltpu.VMEM((taps, depth, width), BF16),
            pltpu.VMEM((2 * sessions, depth), BF16),
            pltpu.SemaphoreType.DMA((len(blocks),)),
        ],
        compiler_params=pltpu.CompilerParams(vmem_limit_bytes=VMEM_LIMIT),
        cost_estimate=pl.CostEstimate(
            flops=4 * taps * sessions * depth * width,
            bytes_accessed=2 * taps * depth * width + 4 * sessions * depth + 6 * taps * sessions * width,
            transcendentals=0,
        ),
    )(*blocks, *sides)


def each_step(group, own_ref, other_ref):
    taps = own_ref.shape[0]
    for index, source in enumerate((own_ref, other_ref)):
        first = (group if index == 0 else 1 - group) * taps
        for tap in range(taps):
            yield first + tap, source[tap].astype(F32)


def excite_kernel(group_ref, own_ref, other_ref, prev_ref, bias_ref, window_ref):
    steps = 2 * own_ref.shape[0]
    history = prev_ref.shape[0] - steps
    for step in range(history):
        window_ref[step] = prev_ref[steps + step]
    for step, value in each_step(group_ref[0], own_ref, other_ref):
        up = value + prev_ref[step].astype(F32) + bias_ref[...]
        window_ref[history + step] = apply_elu(up).astype(BF16)


def excite(group, own, other, prev, bias):
    return pl.pallas_call(
        excite_kernel,
        out_shape=jax.ShapeDtypeStruct(prev.shape, BF16),
        in_specs=[pl.BlockSpec(memory_space=pltpu.SMEM)] + [VMEM] * 4,
        out_specs=VMEM,
        compiler_params=pltpu.CompilerParams(vmem_limit_bytes=VMEM_LIMIT),
    )(group, own, other, prev, bias)


def residual_kernel(
    group_ref,
    own_ref,
    other_ref,
    prev_ref,
    mine_ref,
    theirs_ref,
    bias_ref,
    res_mine_ref,
    res_theirs_ref,
    res_bias_ref,
    skip_ref,
    skip_bias_ref,
    out_ref,
    products,
    frames,
):
    taps, block, width = own_ref.shape
    steps = 2 * taps
    branch = None
    for source, weights in ((mine_ref, res_mine_ref), (theirs_ref, res_theirs_ref)):
        for offset in range(weights.shape[0]):
            term = jnp.dot(
                source[offset : offset + steps].reshape(steps * block, width),
                weights[offset],
                preferred_element_type=F32,
            )
            branch = term if branch is None else branch + term
    hidden = apply_elu(branch + res_bias_ref[...]).astype(BF16)
    projected = jnp.dot(hidden, skip_ref[...], preferred_element_type=F32)
    products[...] = projected.reshape(products.shape)
    for step, value in each_step(group_ref[0], own_ref, other_ref):
        up = value + prev_ref[step].astype(F32) + bias_ref[...]
        mixed = up + products[step] + skip_bias_ref[...]
        for part in range(width // 128):
            frames.at[part][pl.ds(step, block, stride=steps), :] = mixed[
                :, part * 128 : (part + 1) * 128
            ]
    for part in range(width // 128):
        out_ref[:, part * 128 : (part + 1) * 128] = frames[part].astype(BF16)


def residual(group, own, other, prev, mine, theirs, *parameters):
    taps, sessions, width = own.shape
    steps, block = 2 * taps, sessions // 4

    def blocks(array):
        return pl.BlockSpec((array.shape[0], block, width), lambda i: (0, i, 0))

    arrays = (own, other, prev, mine, theirs)
    return pl.pallas_call(
        residual_kernel,
        out_shape=jax.ShapeDtypeStruct((sessions * steps, width), BF16),
        grid=(4,),
        in_specs=[pl.BlockSpec(memory_space=pltpu.SMEM)]
        + [blocks(array) for array in arrays]
        + [VMEM] * len(parameters),
        out_specs=pl.BlockSpec((block * steps, width), lambda i: (i, 0)),
        scratch_shapes=[
            pltpu.VMEM((steps, block, width), F32),
            pltpu.VMEM((width // 128, block * steps, 128), F32),
        ],
        compiler_params=pltpu.CompilerParams(vmem_limit_bytes=VMEM_LIMIT),
    )(group, *arrays, *parameters)


def weave_kernel(group_ref, own_ref, other_ref, out_ref, frames):
    taps, block, width = own_ref.shape
    for step, value in each_step(group_ref[0], own_ref, other_ref):
        for part in range(width // 128):
            frames.at[part][pl.ds(step, block, stride=2 * taps), :] = value[
                :, part * 128 : (part + 1) * 128
            ]
    for part in range(width // 128):
        out_ref[:, part * 128 : (part + 1) * 128] = frames[part].astype(BF16)


def weave(group, own, other):
    taps, sessions, width = own.shape
    steps, block = 2 * taps, sessions // 4
    taken = pl.BlockSpec((taps, block, width), lambda i: (0, i, 0))
    return pl.pallas_call(
        weave_kernel,
        out_shape=jax.ShapeDtypeStruct((sessions * steps, width), BF16),
        grid=(4,),
        in_specs=[pl.BlockSpec(memory_space=pltpu.SMEM), taken, taken],
        out_specs=pl.BlockSpec((block * steps, width), lambda i: (i, 0)),
        scratch_shapes=[pltpu.VMEM((width // 128, block * steps, 128), F32)],
        compiler_params=pltpu.CompilerParams(vmem_limit_bytes=VMEM_LIMIT),
    )(group, own, other)


def swap(value, axis):
    return lax.ppermute(value, axis, [(0, 1), (1, 0)])


def after(value, earlier):
    return lax.optimization_barrier((value, earlier))[0]


class Ring:
    def __init__(self, count, own, other):
        order = ring_order(count)
        self.count = count
        self.pairs = []
        for p in range(count):
            here, there = order[p], order[(p + 1) % count]
            self.pairs += [(2 * here, 2 * there), (2 * there + 1, 2 * here + 1)]
        self.item = jnp.stack([own, other])
        self.blocks, self.steps, self.rounds = [own], [(0, 0)], 0

    def round(self, earlier=None):
        self.rounds += 1
        item = self.item
        if 2 * self.rounds == self.count:
            part = item.shape[1] // 2
            item = lax.dynamic_slice_in_dim(item, lax.axis_index("segment") * part, part, axis=1)
        if earlier is not None:
            item = after(item, earlier)
        item = lax.ppermute(item, ("streams", "segment"), self.pairs)
        self.item = item
        self.blocks += [item, swap(item, "segment")]
        self.steps += [(self.rounds, 0), (self.rounds, 1)]
        return item


def local(
    count,
    latent,
    conv_weight,
    conv_bias,
    tail_cache,
    input_cache,
    resume_slot,
    res_weight,
    res_bias,
    skip_weight,
    skip_bias,
):
    group = lax.axis_index("groups")
    group_word = group[None].astype(jnp.int32)
    rows, tap_count, width = conv_weight.shape
    sessions = latent.shape[0]
    taps = tap_count // 4

    halves = []
    for first in (0, tap_count // 2):
        part = lax.dynamic_slice_in_dim(conv_weight, first + group * taps, taps, axis=1)
        halves.append(part.transpose(1, 0, 2))

    use_ring = rows % 128 == 0 and count % 2 == 0
    if use_ring:
        other = swap(halves[0], "segment")
        prepared = swap(after(halves[1], other), "segment")
        up_ring, tail_ring = Ring(count, halves[0], other), Ring(count, halves[1], prepared)
    else:
        prepared = halves[1]

    portion = sessions // count
    cap = tail_cache.shape[0] // count
    half_taps, history = tail_cache.shape[1], input_cache.shape[1]
    slot_step = jnp.broadcast_to(
        resume_slot.astype(BF16)[:, None, None], (count * cap, 1, width)
    )
    filler = jnp.zeros((count * cap, half_taps - history - 1, width), BF16)
    beside = jnp.concatenate([input_cache, slot_step, filler], axis=1)
    stored = jnp.concatenate([tail_cache, beside], axis=2).reshape(count, cap * half_taps, 2 * width)
    parcel = jnp.concatenate([latent.reshape(count, portion, 2 * width), stored], axis=1)
    parcel = after(parcel, prepared)
    parcel = lax.all_to_all(parcel, "streams", split_axis=0, concat_axis=0, tiled=True)
    handed = parcel[:, :portion].reshape(sessions, 2 * width)
    stored = parcel[:, portion:].reshape(count * cap, half_taps, 2 * width)

    near_half = apply_elu(handed.astype(F32)).astype(BF16)
    near_other = swap(near_half, "segment")
    far_half = swap(after(near_half, near_other), "groups")
    sides = (near_half, near_other, far_half, swap(far_half, "segment"))

    slots = stored[:, history, width:].astype(jnp.int32)[:, :1]
    one_hot = (slots == jnp.arange(sessions, dtype=jnp.int32)[None, :]).astype(BF16)
    packed = jnp.concatenate([stored[:, :, :width], stored[:, :history, width:]], axis=1)
    prev = jnp.einsum("js,jkc->ksc", one_hot, packed, preferred_element_type=F32).astype(BF16)

    res_theirs = swap(res_weight, "segment")

    if use_ring:
        for r in range(count // 2):
            up_ring.round(far_half if r == count // 2 - 1 else None)
            seen = tail_ring.round()
            if r == count // 2 - 2:
                nearly_done = seen
        up_ring.blocks[0] = after(up_ring.blocks[0], nearly_done)
        gathered = [(ring.blocks, ring.steps) for ring in (up_ring, tail_ring)]
    else:
        gathered = [
            ([lax.all_gather(own, "streams", axis=1, tiled=True)], [None]) for own in halves
        ]
    own_up, away_up = spread_taps(sides, *gathered[0], count, F32)
    own_tail, away_tail = spread_taps(sides, *gathered[1], count, BF16)
    other_up = swap(away_up, "groups")
    other_tail = swap(away_tail, "groups")

    own_up = after(own_up, (away_tail, res_theirs))
    bias = conv_bias[None]
    mine = excite(group_word, own_up, other_up, prev, bias)
    theirs = swap(mine, "segment")
    decoded = residual(
        group_word,
        own_up,
        other_up,
        prev,
        mine,
        theirs,
        bias,
        res_weight,
        res_theirs,
        res_bias[None],
        skip_weight,
        skip_bias[None],
    )
    decoded, other_tail = lax.optimization_barrier((decoded, other_tail))
    new_tail = weave(group_word, own_tail, other_tail)
    shape = (sessions, half_taps, width)
    return decoded.reshape(shape), new_tail.reshape(shape)


def solution(mesh):
    placed = (
        P(("groups", "streams"), "segment"),
        P("streams", None, "segment"),
        P("segment"),
        P(("groups", "streams"), None, "segment"),
        P(("groups", "streams"), None, "segment"),
        P(("groups", "streams")),
        P(None, "segment", None),
        P(),
        P(None, "segment"),
        P("segment"),
    )
    return jax.shard_map(
        functools.partial(local, mesh.shape["streams"]),
        mesh=mesh,
        in_specs=placed,
        out_specs=(
            P(("groups", "streams"), None, "segment"),
            P(("groups", "streams"), None, "segment"),
        ),
        check_vma=False,
    )
```

```python
import functools

import jax
import jax.numpy as jnp
from jax import lax
from jax.experimental import pallas as pl
from jax.experimental.pallas import tpu as pltpu
from jax.sharding import PartitionSpec as P

VMEM_LIMIT = 16 * 1024 * 1024
F32 = jnp.float32
BF16 = jnp.bfloat16
VMEM = pl.BlockSpec(memory_space=pltpu.VMEM)


def apply_elu(values):
    return jnp.where(values > 0, values, jnp.exp(jnp.minimum(values, 0.0)) - 1.0)


def ring_order(count):
    return [2 * p if p < count // 2 else 2 * (count - 1 - p) + 1 for p in range(count)]


def ring_place(stream, count):
    return jnp.where(stream % 2 == 0, stream // 2, count - 1 - stream // 2)


def ring_stream(place, count):
    return jnp.where(place < count // 2, 2 * place, 2 * (count - 1 - place) + 1)


def spread_kernel(count, steps, *refs):
    blocks = refs[: len(steps)]
    sides, (home_ref, away_ref) = refs[len(steps) : len(steps) + 4], refs[len(steps) + 4 : -3]
    kernel_rows, inputs, sems = refs[-3:]
    taps = kernel_rows.shape[0]
    rows = blocks[0].shape[-2]
    core = lax.axis_index("segment")
    place = ring_place(lax.axis_index("streams"), count)
    copies = []
    for slot, (step, block) in enumerate(zip(steps, blocks)):
        if step is None:
            source, target = block, kernel_rows
        else:
            distance, passed = step
            taker = 1 - core if passed else core
            stream = ring_stream(
                lax.rem(place + (2 * taker - 1) * distance + count, count), count
            )
            source = block if len(block.shape) == 3 else block.at[passed]
            part = source.shape[0]
            first = 0 if part == taps else taker * part
            target = kernel_rows.at[
                pl.ds(first, part), pl.ds(pl.multiple_of(stream * rows, rows), rows), :
            ]
        copy = pltpu.make_async_copy(source, target, sems.at[slot])
        copy.start()
        copies.append(copy)
    sessions, half = sides[0].shape
    for index, side in enumerate(sides):
        column = core if index % 2 == 0 else 1 - core
        first = index // 2 * sessions
        inputs[first : first + sessions, pl.ds(pl.multiple_of(column * half, half), half)] = side[...]
    for copy in copies:
        copy.wait()

    @pl.loop(0, taps)
    def _(tap):
        product = jnp.dot(inputs[...], kernel_rows[tap], preferred_element_type=F32)
        home_ref[tap] = product[:sessions].astype(home_ref.dtype)
        away_ref[tap] = product[sessions:].astype(away_ref.dtype)


def spread_taps(sides, blocks, steps, count, home_type):
    taps, _, width = blocks[0].shape
    sessions, depth = sides[0].shape[0], 2 * sides[0].shape[1]
    return pl.pallas_call(
        functools.partial(spread_kernel, count, steps),
        out_shape=(
            jax.ShapeDtypeStruct((taps, sessions, width), home_type),
            jax.ShapeDtypeStruct((taps, sessions, width), BF16),
        ),
        in_specs=[pl.BlockSpec(memory_space=pl.ANY)] * len(blocks) + [VMEM] * 4,
        out_specs=(VMEM, VMEM),
        scratch_shapes=[
            pltpu.VMEM((taps, depth, width), BF16),
            pltpu.VMEM((2 * sessions, depth), BF16),
            pltpu.SemaphoreType.DMA((len(blocks),)),
        ],
        compiler_params=pltpu.CompilerParams(vmem_limit_bytes=VMEM_LIMIT),
        cost_estimate=pl.CostEstimate(
            flops=4 * taps * sessions * depth * width,
            bytes_accessed=2 * taps * depth * width + 4 * sessions * depth + 6 * taps * sessions * width,
            transcendentals=0,
        ),
    )(*blocks, *sides)


def each_step(group, own_ref, other_ref):
    taps = own_ref.shape[0]
    for index, source in enumerate((own_ref, other_ref)):
        first = (group if index == 0 else 1 - group) * taps
        for tap in range(taps):
            yield first + tap, source[tap].astype(F32)


def excite_kernel(group_ref, own_ref, other_ref, prev_ref, bias_ref, window_ref, *part_refs):
    steps = 2 * own_ref.shape[0]
    history = prev_ref.shape[0] - steps
    for step in range(history):
        window_ref[step] = prev_ref[steps + step]
    for step, value in each_step(group_ref[0], own_ref, other_ref):
        up = value + prev_ref[step].astype(F32) + bias_ref[...]
        window_ref[history + step] = apply_elu(up).astype(BF16)
    first = 0
    for part_ref in part_refs:
        part_ref[...] = window_ref[first : first + part_ref.shape[0]]
        first += part_ref.shape[0]


def excite(group, own, other, prev, bias):
    steps, *rest = prev.shape
    sizes = (steps,) + tuple((steps + part) // 4 for part in range(4))
    return pl.pallas_call(
        excite_kernel,
        out_shape=[jax.ShapeDtypeStruct((size, *rest), BF16) for size in sizes],
        in_specs=[pl.BlockSpec(memory_space=pltpu.SMEM)] + [VMEM] * 4,
        out_specs=[VMEM] * len(sizes),
        compiler_params=pltpu.CompilerParams(vmem_limit_bytes=VMEM_LIMIT),
    )(group, own, other, prev, bias)


def residual_kernel(group_ref, own_ref, other_ref, prev_ref, mine_ref, *refs):
    parts, refs = refs[:4], refs[4:]
    bias_ref, res_mine_ref, res_theirs_ref, res_bias_ref, skip_ref, skip_bias_ref = refs[:6]
    out_ref, theirs_ref, products, frames = refs[6:]
    first = 0
    for part_ref in parts:
        theirs_ref[first : first + part_ref.shape[0]] = part_ref[...]
        first += part_ref.shape[0]
    taps, block, width = own_ref.shape
    steps = 2 * taps
    branch = None
    for source, weights in ((mine_ref, res_mine_ref), (theirs_ref, res_theirs_ref)):
        for offset in range(weights.shape[0]):
            term = jnp.dot(
                source[offset : offset + steps].reshape(steps * block, width),
                weights[offset],
                preferred_element_type=F32,
            )
            branch = term if branch is None else branch + term
    hidden = apply_elu(branch + res_bias_ref[...]).astype(BF16)
    projected = jnp.dot(hidden, skip_ref[...], preferred_element_type=F32)
    products[...] = projected.reshape(products.shape)
    for step, value in each_step(group_ref[0], own_ref, other_ref):
        up = value + prev_ref[step].astype(F32) + bias_ref[...]
        mixed = up + products[step] + skip_bias_ref[...]
        for part in range(width // 128):
            frames.at[part][pl.ds(step, block, stride=steps), :] = mixed[
                :, part * 128 : (part + 1) * 128
            ]
    for part in range(width // 128):
        out_ref[:, part * 128 : (part + 1) * 128] = frames[part].astype(BF16)


def residual(group, own, other, prev, mine, theirs, *parameters):
    taps, sessions, width = own.shape
    steps, block = 2 * taps, sessions // 4

    def blocks(array):
        return pl.BlockSpec((array.shape[0], block, width), lambda i: (0, i, 0))

    arrays = (own, other, prev, mine, *theirs)
    return pl.pallas_call(
        residual_kernel,
        out_shape=jax.ShapeDtypeStruct((sessions * steps, width), BF16),
        grid=(4,),
        in_specs=[pl.BlockSpec(memory_space=pltpu.SMEM)]
        + [blocks(array) for array in arrays]
        + [VMEM] * len(parameters),
        out_specs=pl.BlockSpec((block * steps, width), lambda i: (i, 0)),
        scratch_shapes=[
            pltpu.VMEM((mine.shape[0], block, width), BF16),
            pltpu.VMEM((steps, block, width), F32),
            pltpu.VMEM((width // 128, block * steps, 128), F32),
        ],
        compiler_params=pltpu.CompilerParams(vmem_limit_bytes=VMEM_LIMIT),
    )(group, *arrays, *parameters)


def weave_kernel(group_ref, own_ref, other_ref, out_ref, frames):
    taps, block, width = own_ref.shape
    for step, value in each_step(group_ref[0], own_ref, other_ref):
        for part in range(width // 128):
            frames.at[part][pl.ds(step, block, stride=2 * taps), :] = value[
                :, part * 128 : (part + 1) * 128
            ]
    for part in range(width // 128):
        out_ref[:, part * 128 : (part + 1) * 128] = frames[part].astype(BF16)


def weave(group, own, other):
    taps, sessions, width = own.shape
    steps, block = 2 * taps, sessions // 4
    taken = pl.BlockSpec((taps, block, width), lambda i: (0, i, 0))
    return pl.pallas_call(
        weave_kernel,
        out_shape=jax.ShapeDtypeStruct((sessions * steps, width), BF16),
        grid=(4,),
        in_specs=[pl.BlockSpec(memory_space=pltpu.SMEM), taken, taken],
        out_specs=pl.BlockSpec((block * steps, width), lambda i: (i, 0)),
        scratch_shapes=[pltpu.VMEM((width // 128, block * steps, 128), F32)],
        compiler_params=pltpu.CompilerParams(vmem_limit_bytes=VMEM_LIMIT),
    )(group, own, other)


def swap(value, axis):
    return lax.ppermute(value, axis, [(0, 1), (1, 0)])


def after(value, earlier):
    return lax.optimization_barrier((value, earlier))[0]


class Ring:
    def __init__(self, count, own, other):
        order = ring_order(count)
        self.count = count
        self.pairs = []
        for p in range(count):
            here, there = order[p], order[(p + 1) % count]
            self.pairs += [(2 * here, 2 * there), (2 * there + 1, 2 * here + 1)]
        self.item = jnp.stack([own, other])
        self.blocks, self.steps, self.rounds = [own], [(0, 0)], 0

    def round(self, earlier=None, passed_after=None):
        self.rounds += 1
        item = self.item
        if 2 * self.rounds == self.count:
            part = item.shape[1] // 2
            item = lax.dynamic_slice_in_dim(item, lax.axis_index("segment") * part, part, axis=1)
        if earlier is not None:
            item = after(item, earlier)
        item = lax.ppermute(item, ("streams", "segment"), self.pairs)
        self.item = item
        given = item if passed_after is None else after(item, passed_after)
        self.blocks += [item, swap(given, "segment")]
        self.steps += [(self.rounds, 0), (self.rounds, 1)]
        return item


def local(
    count,
    latent,
    conv_weight,
    conv_bias,
    tail_cache,
    input_cache,
    resume_slot,
    res_weight,
    res_bias,
    skip_weight,
    skip_bias,
):
    group = lax.axis_index("groups")
    group_word = group[None].astype(jnp.int32)
    rows, tap_count, width = conv_weight.shape
    sessions = latent.shape[0]
    taps = tap_count // 4

    halves = []
    for first in (0, tap_count // 2):
        part = lax.dynamic_slice_in_dim(conv_weight, first + group * taps, taps, axis=1)
        halves.append(part.transpose(1, 0, 2))

    use_ring = rows % 128 == 0 and count % 2 == 0
    if use_ring:
        other = swap(halves[0], "segment")
        prepared = swap(after(halves[1], other), "segment")
        up_ring, tail_ring = Ring(count, halves[0], other), Ring(count, halves[1], prepared)
    else:
        prepared = halves[1]

    portion = sessions // count
    cap = tail_cache.shape[0] // count
    half_taps, history = tail_cache.shape[1], input_cache.shape[1]
    slot_step = jnp.broadcast_to(
        resume_slot.astype(BF16)[:, None, None], (count * cap, 1, width)
    )
    filler = jnp.zeros((count * cap, half_taps - history - 1, width), BF16)
    beside = jnp.concatenate([input_cache, slot_step, filler], axis=1)
    stored = jnp.concatenate([tail_cache, beside], axis=2).reshape(count, cap * half_taps, 2 * width)
    parcel = jnp.concatenate([latent.reshape(count, portion, 2 * width), stored], axis=1)
    parcel = after(parcel, prepared)
    parcel = lax.all_to_all(parcel, "streams", split_axis=0, concat_axis=0, tiled=True)
    handed = parcel[:, :portion].reshape(sessions, 2 * width)
    stored = parcel[:, portion:].reshape(count * cap, half_taps, 2 * width)

    near_half = apply_elu(handed.astype(F32)).astype(BF16)
    near_other = swap(near_half, "segment")
    far_half = swap(after(near_half, near_other), "groups")
    sides = (near_half, near_other, far_half, swap(far_half, "segment"))

    slots = stored[:, history, width:].astype(jnp.int32)[:, :1]
    one_hot = (slots == jnp.arange(sessions, dtype=jnp.int32)[None, :]).astype(BF16)
    packed = jnp.concatenate([stored[:, :, :width], stored[:, :history, width:]], axis=1)
    prev = jnp.einsum("js,jkc->ksc", one_hot, packed, preferred_element_type=F32).astype(BF16)

    res_theirs = swap(res_weight, "segment")

    if use_ring:
        last = count // 2 - 1
        for _ in range(last):
            up_ring.round()
            nearly_done = tail_ring.round()
        up_ring.round(far_half)
        up_ring.blocks[0] = after(up_ring.blocks[0], nearly_done)
        own_up, away_up = spread_taps(sides, up_ring.blocks, up_ring.steps, count, F32)
        tail_ring.round(passed_after=away_up)
        own_tail, away_tail = spread_taps(sides, tail_ring.blocks, tail_ring.steps, count, BF16)
    else:
        whole = [lax.all_gather(own, "streams", axis=1, tiled=True) for own in halves]
        own_up, away_up = spread_taps(sides, whole[:1], [None], count, F32)
        own_tail, away_tail = spread_taps(sides, whole[1:], [None], count, BF16)
    other_up = swap(away_up, "groups")
    other_tail = swap(away_tail, "groups")

    own_up = after(own_up, (away_tail, res_theirs))
    bias = conv_bias[None]
    mine, *parts = excite(group_word, own_up, other_up, prev, bias)
    theirs = [swap(part, "segment") for part in parts]
    decoded = residual(
        group_word,
        own_up,
        other_up,
        prev,
        mine,
        theirs,
        bias,
        res_weight,
        res_theirs,
        res_bias[None],
        skip_weight,
        skip_bias[None],
    )
    decoded, other_tail = lax.optimization_barrier((decoded, other_tail))
    new_tail = weave(group_word, own_tail, other_tail)
    shape = (sessions, half_taps, width)
    return decoded.reshape(shape), new_tail.reshape(shape)


def solution(mesh):
    placed = (
        P(("groups", "streams"), "segment"),
        P("streams", None, "segment"),
        P("segment"),
        P(("groups", "streams"), None, "segment"),
        P(("groups", "streams"), None, "segment"),
        P(("groups", "streams")),
        P(None, "segment", None),
        P(),
        P(None, "segment"),
        P("segment"),
    )
    return jax.shard_map(
        functools.partial(local, mesh.shape["streams"]),
        mesh=mesh,
        in_specs=placed,
        out_specs=(
            P(("groups", "streams"), None, "segment"),
            P(("groups", "streams"), None, "segment"),
        ),
        check_vma=False,
    )
```

```python
import functools

import jax
import jax.numpy as jnp
from jax import lax
from jax.experimental import pallas as pl
from jax.experimental.pallas import tpu as pltpu
from jax.sharding import PartitionSpec as P

VMEM_LIMIT = 16 * 1024 * 1024
F32 = jnp.float32
BF16 = jnp.bfloat16
VMEM = pl.BlockSpec(memory_space=pltpu.VMEM)


def apply_elu(values):
    return jnp.where(values > 0, values, jnp.exp(jnp.minimum(values, 0.0)) - 1.0)


def ring_order(count):
    return [2 * p if p < count // 2 else 2 * (count - 1 - p) + 1 for p in range(count)]


def ring_place(stream, count):
    return jnp.where(stream % 2 == 0, stream // 2, count - 1 - stream // 2)


def ring_stream(place, count):
    return jnp.where(place < count // 2, 2 * place, 2 * (count - 1 - place) + 1)


def spread_kernel(count, steps, *refs):
    blocks = refs[: len(steps)]
    sides, (home_ref, away_ref) = refs[len(steps) : len(steps) + 4], refs[len(steps) + 4 : -3]
    kernel_rows, inputs, sems = refs[-3:]
    taps = kernel_rows.shape[0]
    rows = blocks[0].shape[-2]
    core = lax.axis_index("segment")
    place = ring_place(lax.axis_index("streams"), count)
    copies = []
    for slot, (step, block) in enumerate(zip(steps, blocks)):
        if step is None:
            source, target = block, kernel_rows
        else:
            distance, passed = step
            taker = 1 - core if passed else core
            stream = ring_stream(
                lax.rem(place + (2 * taker - 1) * distance + count, count), count
            )
            source = block if len(block.shape) == 3 else block.at[passed]
            part = source.shape[0]
            first = 0 if part == taps else taker * part
            target = kernel_rows.at[
                pl.ds(first, part), pl.ds(pl.multiple_of(stream * rows, rows), rows), :
            ]
        copy = pltpu.make_async_copy(source, target, sems.at[slot])
        copy.start()
        copies.append(copy)
    sessions, half = sides[0].shape
    for index, side in enumerate(sides):
        column = core if index % 2 == 0 else 1 - core
        first = index // 2 * sessions
        inputs[first : first + sessions, pl.ds(pl.multiple_of(column * half, half), half)] = side[...]
    for copy in copies:
        copy.wait()

    @pl.loop(0, taps)
    def _(tap):
        product = jnp.dot(inputs[...], kernel_rows[tap], preferred_element_type=F32)
        home_ref[tap] = product[:sessions].astype(home_ref.dtype)
        away_ref[tap] = product[sessions:].astype(away_ref.dtype)


def spread_taps(sides, blocks, steps, count, home_type):
    taps, _, width = blocks[0].shape
    sessions, depth = sides[0].shape[0], 2 * sides[0].shape[1]
    return pl.pallas_call(
        functools.partial(spread_kernel, count, steps),
        out_shape=(
            jax.ShapeDtypeStruct((taps, sessions, width), home_type),
            jax.ShapeDtypeStruct((taps, sessions, width), BF16),
        ),
        in_specs=[pl.BlockSpec(memory_space=pl.ANY)] * len(blocks) + [VMEM] * 4,
        out_specs=(VMEM, VMEM),
        scratch_shapes=[
            pltpu.VMEM((taps, depth, width), BF16),
            pltpu.VMEM((2 * sessions, depth), BF16),
            pltpu.SemaphoreType.DMA((len(blocks),)),
        ],
        compiler_params=pltpu.CompilerParams(vmem_limit_bytes=VMEM_LIMIT),
        cost_estimate=pl.CostEstimate(
            flops=4 * taps * sessions * depth * width,
            bytes_accessed=2 * taps * depth * width + 4 * sessions * depth + 6 * taps * sessions * width,
            transcendentals=0,
        ),
    )(*blocks, *sides)


def each_step(group, own_ref, other_ref):
    taps = own_ref.shape[0]
    for index, source in enumerate((own_ref, other_ref)):
        first = (group if index == 0 else 1 - group) * taps
        for tap in range(taps):
            yield first + tap, source[tap].astype(F32)


def excite_kernel(group_ref, own_ref, other_ref, prev_ref, bias_ref, window_ref, *part_refs):
    steps = 2 * own_ref.shape[0]
    history = prev_ref.shape[0] - steps
    for step in range(history):
        window_ref[step] = prev_ref[steps + step]
    for step, value in each_step(group_ref[0], own_ref, other_ref):
        up = value + prev_ref[step].astype(F32) + bias_ref[...]
        window_ref[history + step] = apply_elu(up).astype(BF16)
    first = 0
    for part_ref in part_refs:
        part_ref[...] = window_ref[first : first + part_ref.shape[0]]
        first += part_ref.shape[0]


def excite(group, own, other, prev, bias):
    steps, *rest = prev.shape
    sizes = (steps,) + tuple((steps + part) // 4 for part in range(4))
    return pl.pallas_call(
        excite_kernel,
        out_shape=[jax.ShapeDtypeStruct((size, *rest), BF16) for size in sizes],
        in_specs=[pl.BlockSpec(memory_space=pltpu.SMEM)] + [VMEM] * 4,
        out_specs=[VMEM] * len(sizes),
        compiler_params=pltpu.CompilerParams(vmem_limit_bytes=VMEM_LIMIT),
    )(group, own, other, prev, bias)


def residual_kernel(group_ref, own_ref, other_ref, prev_ref, mine_ref, *refs):
    parts, refs = refs[:4], refs[4:]
    bias_ref, res_mine_ref, res_theirs_ref, res_bias_ref, skip_ref, skip_bias_ref = refs[:6]
    out_ref, theirs_ref, products, frames = refs[6:]
    first = 0
    for part_ref in parts:
        theirs_ref[first : first + part_ref.shape[0]] = part_ref[...]
        first += part_ref.shape[0]
    taps, block, width = own_ref.shape
    steps = 2 * taps
    branch = None
    for source, weights in ((mine_ref, res_mine_ref), (theirs_ref, res_theirs_ref)):
        for offset in range(weights.shape[0]):
            term = jnp.dot(
                source[offset : offset + steps].reshape(steps * block, width),
                weights[offset],
                preferred_element_type=F32,
            )
            branch = term if branch is None else branch + term
    hidden = apply_elu(branch + res_bias_ref[...]).astype(BF16)
    projected = jnp.dot(hidden, skip_ref[...], preferred_element_type=F32)
    products[...] = projected.reshape(products.shape)
    for step, value in each_step(group_ref[0], own_ref, other_ref):
        up = value + prev_ref[step].astype(F32) + bias_ref[...]
        mixed = up + products[step] + skip_bias_ref[...]
        for part in range(width // 128):
            frames.at[part][pl.ds(step, block, stride=steps), :] = mixed[
                :, part * 128 : (part + 1) * 128
            ]
    for part in range(width // 128):
        out_ref[:, part * 128 : (part + 1) * 128] = frames[part].astype(BF16)


def residual(group, own, other, prev, mine, theirs, *parameters):
    taps, sessions, width = own.shape
    steps, block = 2 * taps, sessions // 4

    def blocks(array):
        return pl.BlockSpec((array.shape[0], block, width), lambda i: (0, i, 0))

    arrays = (own, other, prev, mine, *theirs)
    return pl.pallas_call(
        residual_kernel,
        out_shape=jax.ShapeDtypeStruct((sessions * steps, width), BF16),
        grid=(4,),
        in_specs=[pl.BlockSpec(memory_space=pltpu.SMEM)]
        + [blocks(array) for array in arrays]
        + [VMEM] * len(parameters),
        out_specs=pl.BlockSpec((block * steps, width), lambda i: (i, 0)),
        scratch_shapes=[
            pltpu.VMEM((mine.shape[0], block, width), BF16),
            pltpu.VMEM((steps, block, width), F32),
            pltpu.VMEM((width // 128, block * steps, 128), F32),
        ],
        compiler_params=pltpu.CompilerParams(vmem_limit_bytes=VMEM_LIMIT),
    )(group, *arrays, *parameters)


def weave_kernel(group_ref, own_ref, other_ref, out_ref, frames):
    taps, block, width = own_ref.shape
    for step, value in each_step(group_ref[0], own_ref, other_ref):
        for part in range(width // 128):
            frames.at[part][pl.ds(step, block, stride=2 * taps), :] = value[
                :, part * 128 : (part + 1) * 128
            ]
    for part in range(width // 128):
        out_ref[:, part * 128 : (part + 1) * 128] = frames[part].astype(BF16)


def weave(group, own, other):
    taps, sessions, width = own.shape
    steps, block = 2 * taps, sessions // 4
    taken = pl.BlockSpec((taps, block, width), lambda i: (0, i, 0))
    return pl.pallas_call(
        weave_kernel,
        out_shape=jax.ShapeDtypeStruct((sessions * steps, width), BF16),
        grid=(4,),
        in_specs=[pl.BlockSpec(memory_space=pltpu.SMEM), taken, taken],
        out_specs=pl.BlockSpec((block * steps, width), lambda i: (i, 0)),
        scratch_shapes=[pltpu.VMEM((width // 128, block * steps, 128), F32)],
        compiler_params=pltpu.CompilerParams(vmem_limit_bytes=VMEM_LIMIT),
    )(group, own, other)


def swap(value, axis):
    return lax.ppermute(value, axis, [(0, 1), (1, 0)])


def after(value, earlier):
    return lax.optimization_barrier((value, earlier))[0]


class Ring:
    def __init__(self, count, own, other):
        order = ring_order(count)
        self.count = count
        self.pairs = []
        for p in range(count):
            here, there = order[p], order[(p + 1) % count]
            self.pairs += [(2 * here, 2 * there), (2 * there + 1, 2 * here + 1)]
        self.item = jnp.stack([own, other])
        self.blocks, self.steps, self.rounds = [own], [(0, 0)], 0

    def round(self, earlier=None, whole=False):
        self.rounds += 1
        item = self.item
        if 2 * self.rounds == self.count and not whole:
            part = item.shape[1] // 2
            item = lax.dynamic_slice_in_dim(item, lax.axis_index("segment") * part, part, axis=1)
        if earlier is not None:
            item = after(item, earlier)
        item = lax.ppermute(item, ("streams", "segment"), self.pairs)
        self.item = item
        self.blocks.append(item)
        self.steps.append((self.rounds, 0))
        if not whole:
            self.blocks.append(swap(item, "segment"))
            self.steps.append((self.rounds, 1))
        return item


def local(
    count,
    latent,
    conv_weight,
    conv_bias,
    tail_cache,
    input_cache,
    resume_slot,
    res_weight,
    res_bias,
    skip_weight,
    skip_bias,
):
    group = lax.axis_index("groups")
    group_word = group[None].astype(jnp.int32)
    rows, tap_count, width = conv_weight.shape
    sessions = latent.shape[0]
    taps = tap_count // 4

    halves = []
    for first in (0, tap_count // 2):
        part = lax.dynamic_slice_in_dim(conv_weight, first + group * taps, taps, axis=1)
        halves.append(part.transpose(1, 0, 2))

    use_ring = rows % 128 == 0 and count % 2 == 0
    if use_ring:
        other = swap(halves[0], "segment")
        prepared = swap(after(halves[1], other), "segment")
        up_ring, tail_ring = Ring(count, halves[0], other), Ring(count, halves[1], prepared)
    else:
        prepared = halves[1]

    portion = sessions // count
    cap = tail_cache.shape[0] // count
    half_taps, history = tail_cache.shape[1], input_cache.shape[1]
    slot_step = jnp.broadcast_to(
        resume_slot.astype(BF16)[:, None, None], (count * cap, 1, width)
    )
    filler = jnp.zeros((count * cap, half_taps - history - 1, width), BF16)
    beside = jnp.concatenate([input_cache, slot_step, filler], axis=1)
    stored = jnp.concatenate([tail_cache, beside], axis=2).reshape(count, cap * half_taps, 2 * width)
    parcel = jnp.concatenate([latent.reshape(count, portion, 2 * width), stored], axis=1)
    parcel = after(parcel, prepared)
    parcel = lax.all_to_all(parcel, "streams", split_axis=0, concat_axis=0, tiled=True)
    handed = parcel[:, :portion].reshape(sessions, 2 * width)
    stored = parcel[:, portion:].reshape(count * cap, half_taps, 2 * width)

    near_half = apply_elu(handed.astype(F32)).astype(BF16)
    near_other = swap(near_half, "segment")
    far_half = swap(after(near_half, near_other), "groups")
    sides = (near_half, near_other, far_half, swap(far_half, "segment"))

    slots = stored[:, history, width:].astype(jnp.int32)[:, :1]
    one_hot = (slots == jnp.arange(sessions, dtype=jnp.int32)[None, :]).astype(BF16)
    packed = jnp.concatenate([stored[:, :, :width], stored[:, :history, width:]], axis=1)
    prev = jnp.einsum("js,jkc->ksc", one_hot, packed, preferred_element_type=F32).astype(BF16)

    res_theirs = swap(res_weight, "segment")

    if use_ring:
        last = count // 2 - 1
        for _ in range(last):
            up_ring.round()
            nearly_done = tail_ring.round()
        up_ring.round(far_half)
        up_ring.blocks[0] = after(up_ring.blocks[0], nearly_done)
        own_up, away_up = spread_taps(sides, up_ring.blocks, up_ring.steps, count, F32)
        tail_ring.round(whole=True)
        own_tail, away_tail = spread_taps(sides, tail_ring.blocks, tail_ring.steps, count, BF16)
    else:
        whole = [lax.all_gather(own, "streams", axis=1, tiled=True) for own in halves]
        own_up, away_up = spread_taps(sides, whole[:1], [None], count, F32)
        own_tail, away_tail = spread_taps(sides, whole[1:], [None], count, BF16)
    other_up = swap(away_up, "groups")
    other_tail = swap(away_tail, "groups")

    own_up = after(own_up, (away_tail, res_theirs))
    bias = conv_bias[None]
    mine, *parts = excite(group_word, own_up, other_up, prev, bias)
    theirs = [swap(part, "segment") for part in parts]
    decoded = residual(
        group_word,
        own_up,
        other_up,
        prev,
        mine,
        theirs,
        bias,
        res_weight,
        res_theirs,
        res_bias[None],
        skip_weight,
        skip_bias[None],
    )
    decoded, other_tail = lax.optimization_barrier((decoded, other_tail))
    new_tail = weave(group_word, own_tail, other_tail)
    shape = (sessions, half_taps, width)
    return decoded.reshape(shape), new_tail.reshape(shape)


def solution(mesh):
    placed = (
        P(("groups", "streams"), "segment"),
        P("streams", None, "segment"),
        P("segment"),
        P(("groups", "streams"), None, "segment"),
        P(("groups", "streams"), None, "segment"),
        P(("groups", "streams")),
        P(None, "segment", None),
        P(),
        P(None, "segment"),
        P("segment"),
    )
    return jax.shard_map(
        functools.partial(local, mesh.shape["streams"]),
        mesh=mesh,
        in_specs=placed,
        out_specs=(
            P(("groups", "streams"), None, "segment"),
            P(("groups", "streams"), None, "segment"),
        ),
        check_vma=False,
    )
```

```python
import functools

import jax
import jax.numpy as jnp
from jax import lax
from jax.experimental import pallas as pl
from jax.experimental.pallas import tpu as pltpu
from jax.sharding import PartitionSpec as P

VMEM_LIMIT = 16 * 1024 * 1024
F32 = jnp.float32
BF16 = jnp.bfloat16
VMEM = pl.BlockSpec(memory_space=pltpu.VMEM)


def apply_elu(values):
    return jnp.where(values > 0, values, jnp.exp(jnp.minimum(values, 0.0)) - 1.0)


def ring_order(count):
    return [2 * p if p < count // 2 else 2 * (count - 1 - p) + 1 for p in range(count)]


def ring_place(stream, count):
    return jnp.where(stream % 2 == 0, stream // 2, count - 1 - stream // 2)


def ring_stream(place, count):
    return jnp.where(place < count // 2, 2 * place, 2 * (count - 1 - place) + 1)


def spread_kernel(count, steps, *refs):
    blocks = refs[: len(steps)]
    sides, (home_ref, away_ref) = refs[len(steps) : len(steps) + 4], refs[len(steps) + 4 : -3]
    kernel_rows, inputs, sems = refs[-3:]
    taps = kernel_rows.shape[0]
    rows = blocks[0].shape[-2]
    core = lax.axis_index("segment")
    place = ring_place(lax.axis_index("streams"), count)
    copies = []
    for slot, (step, block) in enumerate(zip(steps, blocks)):
        if step is None:
            source, target = block, kernel_rows
        else:
            distance, passed = step
            taker = 1 - core if passed else core
            stream = ring_stream(
                lax.rem(place + (2 * taker - 1) * distance + count, count), count
            )
            source = block if len(block.shape) == 3 else block.at[passed]
            part = source.shape[0]
            first = 0 if part == taps else taker * part
            target = kernel_rows.at[
                pl.ds(first, part), pl.ds(pl.multiple_of(stream * rows, rows), rows), :
            ]
        copy = pltpu.make_async_copy(source, target, sems.at[slot])
        copy.start()
        copies.append(copy)
    sessions, half = sides[0].shape
    for index, side in enumerate(sides):
        column = core if index % 2 == 0 else 1 - core
        first = index // 2 * sessions
        inputs[first : first + sessions, pl.ds(pl.multiple_of(column * half, half), half)] = side[...]
    for copy in copies:
        copy.wait()

    @pl.loop(0, taps)
    def _(tap):
        product = jnp.dot(inputs[...], kernel_rows[tap], preferred_element_type=F32)
        home_ref[tap] = product[:sessions].astype(home_ref.dtype)
        away_ref[tap] = product[sessions:].astype(away_ref.dtype)


def spread_taps(sides, blocks, steps, count, home_type):
    taps, _, width = blocks[0].shape
    sessions, depth = sides[0].shape[0], 2 * sides[0].shape[1]
    return pl.pallas_call(
        functools.partial(spread_kernel, count, steps),
        out_shape=(
            jax.ShapeDtypeStruct((taps, sessions, width), home_type),
            jax.ShapeDtypeStruct((taps, sessions, width), BF16),
        ),
        in_specs=[pl.BlockSpec(memory_space=pl.ANY)] * len(blocks) + [VMEM] * 4,
        out_specs=(VMEM, VMEM),
        scratch_shapes=[
            pltpu.VMEM((taps, depth, width), BF16),
            pltpu.VMEM((2 * sessions, depth), BF16),
            pltpu.SemaphoreType.DMA((len(blocks),)),
        ],
        compiler_params=pltpu.CompilerParams(vmem_limit_bytes=VMEM_LIMIT),
        cost_estimate=pl.CostEstimate(
            flops=4 * taps * sessions * depth * width,
            bytes_accessed=2 * taps * depth * width + 4 * sessions * depth + 6 * taps * sessions * width,
            transcendentals=0,
        ),
    )(*blocks, *sides)


def each_step(group, own_ref, other_ref):
    taps = own_ref.shape[0]
    for index, source in enumerate((own_ref, other_ref)):
        first = (group if index == 0 else 1 - group) * taps
        for tap in range(taps):
            yield first + tap, source[tap].astype(F32)


def excite_kernel(group_ref, own_ref, other_ref, prev_ref, bias_ref, window_ref, *part_refs):
    steps = 2 * own_ref.shape[0]
    history = prev_ref.shape[0] - steps
    for step in range(history):
        window_ref[step] = prev_ref[steps + step]
    for step, value in each_step(group_ref[0], own_ref, other_ref):
        up = value + prev_ref[step].astype(F32) + bias_ref[...]
        window_ref[history + step] = apply_elu(up).astype(BF16)
    first = 0
    for part_ref in part_refs:
        part_ref[...] = window_ref[first : first + part_ref.shape[0]]
        first += part_ref.shape[0]


def excite(group, own, other, prev, bias):
    steps, *rest = prev.shape
    sizes = (steps,) + tuple((steps + part) // 4 for part in range(4))
    return pl.pallas_call(
        excite_kernel,
        out_shape=[jax.ShapeDtypeStruct((size, *rest), BF16) for size in sizes],
        in_specs=[pl.BlockSpec(memory_space=pltpu.SMEM)] + [VMEM] * 4,
        out_specs=[VMEM] * len(sizes),
        compiler_params=pltpu.CompilerParams(vmem_limit_bytes=VMEM_LIMIT),
    )(group, own, other, prev, bias)


def residual_kernel(group_ref, own_ref, other_ref, prev_ref, mine_ref, *refs):
    parts, refs = refs[:4], refs[4:]
    bias_ref, res_mine_ref, res_theirs_ref, res_bias_ref, skip_ref, skip_bias_ref = refs[:6]
    out_ref, theirs_ref, products, frames = refs[6:]
    first = 0
    for part_ref in parts:
        theirs_ref[first : first + part_ref.shape[0]] = part_ref[...]
        first += part_ref.shape[0]
    taps, block, width = own_ref.shape
    steps = 2 * taps
    branch = None
    for source, weights in ((mine_ref, res_mine_ref), (theirs_ref, res_theirs_ref)):
        for offset in range(weights.shape[0]):
            term = jnp.dot(
                source[offset : offset + steps].reshape(steps * block, width),
                weights[offset],
                preferred_element_type=F32,
            )
            branch = term if branch is None else branch + term
    hidden = apply_elu(branch + res_bias_ref[...]).astype(BF16)
    projected = jnp.dot(hidden, skip_ref[...], preferred_element_type=F32)
    products[...] = projected.reshape(products.shape)
    for step, value in each_step(group_ref[0], own_ref, other_ref):
        up = value + prev_ref[step].astype(F32) + bias_ref[...]
        mixed = up + products[step] + skip_bias_ref[...]
        for part in range(width // 128):
            frames.at[part][pl.ds(step, block, stride=steps), :] = mixed[
                :, part * 128 : (part + 1) * 128
            ]
    for part in range(width // 128):
        out_ref[:, part * 128 : (part + 1) * 128] = frames[part].astype(BF16)


def residual(group, own, other, prev, mine, theirs, *parameters):
    taps, sessions, width = own.shape
    steps, block = 2 * taps, sessions // 4

    def blocks(array):
        return pl.BlockSpec((array.shape[0], block, width), lambda i: (0, i, 0))

    arrays = (own, other, prev, mine, *theirs)
    return pl.pallas_call(
        residual_kernel,
        out_shape=jax.ShapeDtypeStruct((sessions * steps, width), BF16),
        grid=(4,),
        in_specs=[pl.BlockSpec(memory_space=pltpu.SMEM)]
        + [blocks(array) for array in arrays]
        + [VMEM] * len(parameters),
        out_specs=pl.BlockSpec((block * steps, width), lambda i: (i, 0)),
        scratch_shapes=[
            pltpu.VMEM((mine.shape[0], block, width), BF16),
            pltpu.VMEM((steps, block, width), F32),
            pltpu.VMEM((width // 128, block * steps, 128), F32),
        ],
        compiler_params=pltpu.CompilerParams(vmem_limit_bytes=VMEM_LIMIT),
    )(group, *arrays, *parameters)


def weave_kernel(group_ref, own_ref, other_ref, out_ref, frames):
    taps, block, width = own_ref.shape
    for step, value in each_step(group_ref[0], own_ref, other_ref):
        for part in range(width // 128):
            frames.at[part][pl.ds(step, block, stride=2 * taps), :] = value[
                :, part * 128 : (part + 1) * 128
            ]
    for part in range(width // 128):
        out_ref[:, part * 128 : (part + 1) * 128] = frames[part].astype(BF16)


def weave(group, own, other):
    taps, sessions, width = own.shape
    steps, block = 2 * taps, sessions // 4
    taken = pl.BlockSpec((taps, block, width), lambda i: (0, i, 0))
    return pl.pallas_call(
        weave_kernel,
        out_shape=jax.ShapeDtypeStruct((sessions * steps, width), BF16),
        grid=(4,),
        in_specs=[pl.BlockSpec(memory_space=pltpu.SMEM), taken, taken],
        out_specs=pl.BlockSpec((block * steps, width), lambda i: (i, 0)),
        scratch_shapes=[pltpu.VMEM((width // 128, block * steps, 128), F32)],
        compiler_params=pltpu.CompilerParams(vmem_limit_bytes=VMEM_LIMIT),
    )(group, own, other)


def swap(value, axis):
    return lax.ppermute(value, axis, [(0, 1), (1, 0)])


def after(value, earlier):
    return lax.optimization_barrier((value, earlier))[0]


class Ring:
    def __init__(self, count, own, other):
        order = ring_order(count)
        self.count = count
        self.pairs = []
        for p in range(count):
            here, there = order[p], order[(p + 1) % count]
            self.pairs += [(2 * here, 2 * there), (2 * there + 1, 2 * here + 1)]
        self.item = jnp.stack([own, other])
        self.blocks, self.steps, self.rounds = [own], [(0, 0)], 0

    def round(self, earlier=None, whole=False):
        self.rounds += 1
        item = self.item
        if 2 * self.rounds == self.count and not whole:
            part = item.shape[1] // 2
            item = lax.dynamic_slice_in_dim(item, lax.axis_index("segment") * part, part, axis=1)
        if earlier is not None:
            item = after(item, earlier)
        item = lax.ppermute(item, ("streams", "segment"), self.pairs)
        self.item = item
        self.blocks.append(item)
        self.steps.append((self.rounds, 0))
        if not whole:
            self.blocks.append(swap(item, "segment"))
            self.steps.append((self.rounds, 1))
        return item


def local(
    count,
    latent,
    conv_weight,
    conv_bias,
    tail_cache,
    input_cache,
    resume_slot,
    res_weight,
    res_bias,
    skip_weight,
    skip_bias,
):
    group = lax.axis_index("groups")
    group_word = group[None].astype(jnp.int32)
    rows, tap_count, width = conv_weight.shape
    sessions = latent.shape[0]
    taps = tap_count // 4

    halves = []
    for first in (0, tap_count // 2):
        part = lax.dynamic_slice_in_dim(conv_weight, first + group * taps, taps, axis=1)
        halves.append(part.transpose(1, 0, 2))

    use_ring = rows % 128 == 0 and count % 2 == 0
    if use_ring:
        other = swap(halves[0], "segment")
        prepared = swap(after(halves[1], other), "segment")
        up_ring, tail_ring = Ring(count, halves[0], other), Ring(count, halves[1], prepared)
    else:
        prepared = halves[1]

    portion = sessions // count
    cap = tail_cache.shape[0] // count
    half_taps, history = tail_cache.shape[1], input_cache.shape[1]
    slot_step = jnp.broadcast_to(
        resume_slot.astype(BF16)[:, None, None], (count * cap, 1, width)
    )
    filler = jnp.zeros((count * cap, half_taps - history - 1, width), BF16)
    beside = jnp.concatenate([input_cache, slot_step, filler], axis=1)
    stored = jnp.concatenate([tail_cache, beside], axis=2).reshape(count, cap * half_taps, 2 * width)
    parcel = jnp.concatenate([latent.reshape(count, portion, 2 * width), stored], axis=1)
    parcel = after(parcel, prepared)
    parcel = lax.all_to_all(parcel, "streams", split_axis=0, concat_axis=0, tiled=True)
    handed = parcel[:, :portion].reshape(sessions, 2 * width)
    stored = parcel[:, portion:].reshape(count * cap, half_taps, 2 * width)

    near_half = apply_elu(handed.astype(F32)).astype(BF16)
    near_other = swap(near_half, "segment")
    far_half = swap(after(near_half, near_other), "groups")
    sides = (near_half, near_other, far_half, swap(far_half, "segment"))

    slots = stored[:, history, width:].astype(jnp.int32)[:, :1]
    one_hot = (slots == jnp.arange(sessions, dtype=jnp.int32)[None, :]).astype(BF16)
    packed = jnp.concatenate([stored[:, :, :width], stored[:, :history, width:]], axis=1)
    prev = jnp.einsum("js,jkc->ksc", one_hot, packed, preferred_element_type=F32).astype(BF16)

    res_theirs = swap(res_weight, "segment")

    if use_ring:
        last = count // 2 - 1
        for _ in range(last):
            up_ring.round()
            nearly_done = tail_ring.round()
        up_ring.round(far_half)
        up_ring.blocks[0] = after(up_ring.blocks[0], nearly_done)
        own_up, away_up = spread_taps(sides, up_ring.blocks, up_ring.steps, count, F32)
        tail_ring.round(away_up, whole=True)
        own_tail, away_tail = spread_taps(sides, tail_ring.blocks, tail_ring.steps, count, BF16)
    else:
        whole = [lax.all_gather(own, "streams", axis=1, tiled=True) for own in halves]
        own_up, away_up = spread_taps(sides, whole[:1], [None], count, F32)
        own_tail, away_tail = spread_taps(sides, whole[1:], [None], count, BF16)
    other_up = swap(away_up, "groups")
    other_tail = swap(away_tail, "groups")

    own_up = after(own_up, (away_tail, res_theirs))
    bias = conv_bias[None]
    mine, *parts = excite(group_word, own_up, other_up, prev, bias)
    theirs = [swap(part, "segment") for part in parts]
    decoded = residual(
        group_word,
        own_up,
        other_up,
        prev,
        mine,
        theirs,
        bias,
        res_weight,
        res_theirs,
        res_bias[None],
        skip_weight,
        skip_bias[None],
    )
    decoded, other_tail = lax.optimization_barrier((decoded, other_tail))
    new_tail = weave(group_word, own_tail, other_tail)
    shape = (sessions, half_taps, width)
    return decoded.reshape(shape), new_tail.reshape(shape)


def solution(mesh):
    placed = (
        P(("groups", "streams"), "segment"),
        P("streams", None, "segment"),
        P("segment"),
        P(("groups", "streams"), None, "segment"),
        P(("groups", "streams"), None, "segment"),
        P(("groups", "streams")),
        P(None, "segment", None),
        P(),
        P(None, "segment"),
        P("segment"),
    )
    return jax.shard_map(
        functools.partial(local, mesh.shape["streams"]),
        mesh=mesh,
        in_specs=placed,
        out_specs=(
            P(("groups", "streams"), None, "segment"),
            P(("groups", "streams"), None, "segment"),
        ),
        check_vma=False,
    )
```

```python
import functools

import jax
import jax.numpy as jnp
from jax import lax
from jax.experimental import pallas as pl
from jax.experimental.pallas import tpu as pltpu
from jax.sharding import PartitionSpec as P

VMEM_LIMIT = 16 * 1024 * 1024
F32 = jnp.float32
BF16 = jnp.bfloat16
VMEM = pl.BlockSpec(memory_space=pltpu.VMEM)


def apply_elu(values):
    return jnp.where(values > 0, values, jnp.exp(jnp.minimum(values, 0.0)) - 1.0)


def ring_order(count):
    return [2 * p if p < count // 2 else 2 * (count - 1 - p) + 1 for p in range(count)]


def ring_place(stream, count):
    return jnp.where(stream % 2 == 0, stream // 2, count - 1 - stream // 2)


def ring_stream(place, count):
    return jnp.where(place < count // 2, 2 * place, 2 * (count - 1 - place) + 1)


def spread_kernel(count, steps, *refs):
    blocks = refs[: len(steps)]
    sides, (home_ref, away_ref) = refs[len(steps) : len(steps) + 4], refs[len(steps) + 4 : -3]
    kernel_rows, inputs, sems = refs[-3:]
    taps = kernel_rows.shape[0]
    rows = blocks[0].shape[-2]
    core = lax.axis_index("segment")
    place = ring_place(lax.axis_index("streams"), count)
    copies = []
    for slot, (step, block) in enumerate(zip(steps, blocks)):
        if step is None:
            source, target = block, kernel_rows
        else:
            distance, passed = step
            taker = 1 - core if passed else core
            stream = ring_stream(
                lax.rem(place + (2 * taker - 1) * distance + count, count), count
            )
            source = block if len(block.shape) == 3 else block.at[passed]
            part = source.shape[0]
            first = 0 if part == taps else taker * part
            target = kernel_rows.at[
                pl.ds(first, part), pl.ds(pl.multiple_of(stream * rows, rows), rows), :
            ]
        copy = pltpu.make_async_copy(source, target, sems.at[slot])
        copy.start()
        copies.append(copy)
    sessions, half = sides[0].shape
    for index, side in enumerate(sides):
        column = core if index % 2 == 0 else 1 - core
        first = index // 2 * sessions
        inputs[first : first + sessions, pl.ds(pl.multiple_of(column * half, half), half)] = side[...]
    for copy in copies:
        copy.wait()

    @pl.loop(0, taps)
    def _(tap):
        product = jnp.dot(inputs[...], kernel_rows[tap], preferred_element_type=F32)
        home_ref[tap] = product[:sessions].astype(home_ref.dtype)
        away_ref[tap] = product[sessions:].astype(away_ref.dtype)


def spread_taps(sides, blocks, steps, count, home_type):
    taps, _, width = blocks[0].shape
    sessions, depth = sides[0].shape[0], 2 * sides[0].shape[1]
    return pl.pallas_call(
        functools.partial(spread_kernel, count, steps),
        out_shape=(
            jax.ShapeDtypeStruct((taps, sessions, width), home_type),
            jax.ShapeDtypeStruct((taps, sessions, width), BF16),
        ),
        in_specs=[pl.BlockSpec(memory_space=pl.ANY)] * len(blocks) + [VMEM] * 4,
        out_specs=(VMEM, VMEM),
        scratch_shapes=[
            pltpu.VMEM((taps, depth, width), BF16),
            pltpu.VMEM((2 * sessions, depth), BF16),
            pltpu.SemaphoreType.DMA((len(blocks),)),
        ],
        compiler_params=pltpu.CompilerParams(vmem_limit_bytes=VMEM_LIMIT),
        cost_estimate=pl.CostEstimate(
            flops=4 * taps * sessions * depth * width,
            bytes_accessed=2 * taps * depth * width + 4 * sessions * depth + 6 * taps * sessions * width,
            transcendentals=0,
        ),
    )(*blocks, *sides)


def each_step(group, own_ref, other_ref):
    taps = own_ref.shape[0]
    for index, source in enumerate((own_ref, other_ref)):
        first = (group if index == 0 else 1 - group) * taps
        for tap in range(taps):
            yield first + tap, source[tap].astype(F32)


def excite_kernel(group_ref, own_ref, other_ref, prev_ref, bias_ref, window_ref, *part_refs):
    steps = 2 * own_ref.shape[0]
    history = prev_ref.shape[0] - steps
    for step in range(history):
        window_ref[step] = prev_ref[steps + step]
    for step, value in each_step(group_ref[0], own_ref, other_ref):
        up = value + prev_ref[step].astype(F32) + bias_ref[...]
        window_ref[history + step] = apply_elu(up).astype(BF16)
    first = 0
    for part_ref in part_refs:
        part_ref[...] = window_ref[first : first + part_ref.shape[0]]
        first += part_ref.shape[0]


def excite(group, own, other, prev, bias):
    steps, *rest = prev.shape
    sizes = (steps,) + tuple((steps + part) // 4 for part in range(4))
    return pl.pallas_call(
        excite_kernel,
        out_shape=[jax.ShapeDtypeStruct((size, *rest), BF16) for size in sizes],
        in_specs=[pl.BlockSpec(memory_space=pltpu.SMEM)] + [VMEM] * 4,
        out_specs=[VMEM] * len(sizes),
        compiler_params=pltpu.CompilerParams(vmem_limit_bytes=VMEM_LIMIT),
    )(group, own, other, prev, bias)


def residual_kernel(group_ref, own_ref, other_ref, prev_ref, mine_ref, *refs):
    parts, refs = refs[:4], refs[4:]
    bias_ref, res_mine_ref, res_theirs_ref, res_bias_ref, skip_ref, skip_bias_ref = refs[:6]
    out_ref, theirs_ref, products, frames = refs[6:]
    first = 0
    for part_ref in parts:
        theirs_ref[first : first + part_ref.shape[0]] = part_ref[...]
        first += part_ref.shape[0]
    taps, block, width = own_ref.shape
    steps = 2 * taps
    branch = None
    for source, weights in ((mine_ref, res_mine_ref), (theirs_ref, res_theirs_ref)):
        for offset in range(weights.shape[0]):
            term = jnp.dot(
                source[offset : offset + steps].reshape(steps * block, width),
                weights[offset],
                preferred_element_type=F32,
            )
            branch = term if branch is None else branch + term
    hidden = apply_elu(branch + res_bias_ref[...]).astype(BF16)
    projected = jnp.dot(hidden, skip_ref[...], preferred_element_type=F32)
    products[...] = projected.reshape(products.shape)
    for step, value in each_step(group_ref[0], own_ref, other_ref):
        up = value + prev_ref[step].astype(F32) + bias_ref[...]
        mixed = up + products[step] + skip_bias_ref[...]
        for part in range(width // 128):
            frames.at[part][pl.ds(step, block, stride=steps), :] = mixed[
                :, part * 128 : (part + 1) * 128
            ]
    for part in range(width // 128):
        out_ref[:, part * 128 : (part + 1) * 128] = frames[part].astype(BF16)


def residual(group, own, other, prev, mine, theirs, *parameters):
    taps, sessions, width = own.shape
    steps, block = 2 * taps, sessions // 2

    def blocks(array):
        return pl.BlockSpec((array.shape[0], block, width), lambda i: (0, i, 0))

    arrays = (own, other, prev, mine, *theirs)
    return pl.pallas_call(
        residual_kernel,
        out_shape=jax.ShapeDtypeStruct((sessions * steps, width), BF16),
        grid=(2,),
        in_specs=[pl.BlockSpec(memory_space=pltpu.SMEM)]
        + [blocks(array) for array in arrays]
        + [VMEM] * len(parameters),
        out_specs=pl.BlockSpec((block * steps, width), lambda i: (i, 0)),
        scratch_shapes=[
            pltpu.VMEM((mine.shape[0], block, width), BF16),
            pltpu.VMEM((steps, block, width), F32),
            pltpu.VMEM((width // 128, block * steps, 128), F32),
        ],
        compiler_params=pltpu.CompilerParams(vmem_limit_bytes=VMEM_LIMIT),
    )(group, *arrays, *parameters)


def weave_kernel(group_ref, own_ref, other_ref, out_ref, frames):
    taps, block, width = own_ref.shape
    for step, value in each_step(group_ref[0], own_ref, other_ref):
        for part in range(width // 128):
            frames.at[part][pl.ds(step, block, stride=2 * taps), :] = value[
                :, part * 128 : (part + 1) * 128
            ]
    for part in range(width // 128):
        out_ref[:, part * 128 : (part + 1) * 128] = frames[part].astype(BF16)


def weave(group, own, other):
    taps, sessions, width = own.shape
    steps, block = 2 * taps, sessions // 2
    taken = pl.BlockSpec((taps, block, width), lambda i: (0, i, 0))
    return pl.pallas_call(
        weave_kernel,
        out_shape=jax.ShapeDtypeStruct((sessions * steps, width), BF16),
        grid=(2,),
        in_specs=[pl.BlockSpec(memory_space=pltpu.SMEM), taken, taken],
        out_specs=pl.BlockSpec((block * steps, width), lambda i: (i, 0)),
        scratch_shapes=[pltpu.VMEM((width // 128, block * steps, 128), F32)],
        compiler_params=pltpu.CompilerParams(vmem_limit_bytes=VMEM_LIMIT),
    )(group, own, other)


def swap(value, axis):
    return lax.ppermute(value, axis, [(0, 1), (1, 0)])


def after(value, earlier):
    return lax.optimization_barrier((value, earlier))[0]


class Ring:
    def __init__(self, count, own, other):
        order = ring_order(count)
        self.count = count
        self.pairs = []
        for p in range(count):
            here, there = order[p], order[(p + 1) % count]
            self.pairs += [(2 * here, 2 * there), (2 * there + 1, 2 * here + 1)]
        self.item = jnp.stack([own, other])
        self.blocks, self.steps, self.rounds = [own], [(0, 0)], 0

    def round(self, earlier=None, whole=False):
        self.rounds += 1
        item = self.item
        if 2 * self.rounds == self.count and not whole:
            part = item.shape[1] // 2
            item = lax.dynamic_slice_in_dim(item, lax.axis_index("segment") * part, part, axis=1)
        if earlier is not None:
            item = after(item, earlier)
        item = lax.ppermute(item, ("streams", "segment"), self.pairs)
        self.item = item
        self.blocks.append(item)
        self.steps.append((self.rounds, 0))
        if not whole:
            self.blocks.append(swap(item, "segment"))
            self.steps.append((self.rounds, 1))
        return item


def local(
    count,
    latent,
    conv_weight,
    conv_bias,
    tail_cache,
    input_cache,
    resume_slot,
    res_weight,
    res_bias,
    skip_weight,
    skip_bias,
):
    group = lax.axis_index("groups")
    group_word = group[None].astype(jnp.int32)
    rows, tap_count, width = conv_weight.shape
    sessions = latent.shape[0]
    taps = tap_count // 4

    halves = []
    for first in (0, tap_count // 2):
        part = lax.dynamic_slice_in_dim(conv_weight, first + group * taps, taps, axis=1)
        halves.append(part.transpose(1, 0, 2))

    use_ring = rows % 128 == 0 and count % 2 == 0
    if use_ring:
        other = swap(halves[0], "segment")
        prepared = swap(after(halves[1], other), "segment")
        up_ring, tail_ring = Ring(count, halves[0], other), Ring(count, halves[1], prepared)
    else:
        prepared = halves[1]

    portion = sessions // count
    cap = tail_cache.shape[0] // count
    half_taps, history = tail_cache.shape[1], input_cache.shape[1]
    slot_step = jnp.broadcast_to(
        resume_slot.astype(BF16)[:, None, None], (count * cap, 1, width)
    )
    filler = jnp.zeros((count * cap, half_taps - history - 1, width), BF16)
    beside = jnp.concatenate([input_cache, slot_step, filler], axis=1)
    stored = jnp.concatenate([tail_cache, beside], axis=2).reshape(count, cap * half_taps, 2 * width)
    parcel = jnp.concatenate([latent.reshape(count, portion, 2 * width), stored], axis=1)
    parcel = after(parcel, prepared)
    parcel = lax.all_to_all(parcel, "streams", split_axis=0, concat_axis=0, tiled=True)
    handed = parcel[:, :portion].reshape(sessions, 2 * width)
    stored = parcel[:, portion:].reshape(count * cap, half_taps, 2 * width)

    near_half = apply_elu(handed.astype(F32)).astype(BF16)
    near_other = swap(near_half, "segment")
    far_half = swap(after(near_half, near_other), "groups")
    sides = (near_half, near_other, far_half, swap(far_half, "segment"))

    slots = stored[:, history, width:].astype(jnp.int32)[:, :1]
    one_hot = (slots == jnp.arange(sessions, dtype=jnp.int32)[None, :]).astype(BF16)
    packed = jnp.concatenate([stored[:, :, :width], stored[:, :history, width:]], axis=1)
    prev = jnp.einsum("js,jkc->ksc", one_hot, packed, preferred_element_type=F32).astype(BF16)

    res_theirs = swap(res_weight, "segment")

    if use_ring:
        last = count // 2 - 1
        for _ in range(last):
            up_ring.round()
            nearly_done = tail_ring.round()
        up_ring.round(far_half)
        up_ring.blocks[0] = after(up_ring.blocks[0], nearly_done)
        own_up, away_up = spread_taps(sides, up_ring.blocks, up_ring.steps, count, F32)
        tail_ring.round(whole=True)
        own_tail, away_tail = spread_taps(sides, tail_ring.blocks, tail_ring.steps, count, BF16)
    else:
        whole = [lax.all_gather(own, "streams", axis=1, tiled=True) for own in halves]
        own_up, away_up = spread_taps(sides, whole[:1], [None], count, F32)
        own_tail, away_tail = spread_taps(sides, whole[1:], [None], count, BF16)
    other_up = swap(away_up, "groups")
    other_tail = swap(away_tail, "groups")

    own_up = after(own_up, (away_tail, res_theirs))
    bias = conv_bias[None]
    mine, *parts = excite(group_word, own_up, other_up, prev, bias)
    theirs = [swap(part, "segment") for part in parts]
    decoded = residual(
        group_word,
        own_up,
        other_up,
        prev,
        mine,
        theirs,
        bias,
        res_weight,
        res_theirs,
        res_bias[None],
        skip_weight,
        skip_bias[None],
    )
    decoded, other_tail = lax.optimization_barrier((decoded, other_tail))
    new_tail = weave(group_word, own_tail, other_tail)
    shape = (sessions, half_taps, width)
    return decoded.reshape(shape), new_tail.reshape(shape)


def solution(mesh):
    placed = (
        P(("groups", "streams"), "segment"),
        P("streams", None, "segment"),
        P("segment"),
        P(("groups", "streams"), None, "segment"),
        P(("groups", "streams"), None, "segment"),
        P(("groups", "streams")),
        P(None, "segment", None),
        P(),
        P(None, "segment"),
        P("segment"),
    )
    return jax.shard_map(
        functools.partial(local, mesh.shape["streams"]),
        mesh=mesh,
        in_specs=placed,
        out_specs=(
            P(("groups", "streams"), None, "segment"),
            P(("groups", "streams"), None, "segment"),
        ),
        check_vma=False,
    )
```

```python
import functools

import jax
import jax.numpy as jnp
from jax import lax
from jax.experimental import pallas as pl
from jax.experimental.pallas import tpu as pltpu
from jax.sharding import PartitionSpec as P

VMEM_LIMIT = 16 * 1024 * 1024
F32 = jnp.float32
BF16 = jnp.bfloat16
VMEM = pl.BlockSpec(memory_space=pltpu.VMEM)


def apply_elu(values):
    return jnp.where(values > 0, values, jnp.exp(jnp.minimum(values, 0.0)) - 1.0)


def ring_order(count):
    return [2 * p if p < count // 2 else 2 * (count - 1 - p) + 1 for p in range(count)]


def ring_place(stream, count):
    return jnp.where(stream % 2 == 0, stream // 2, count - 1 - stream // 2)


def ring_stream(place, count):
    return jnp.where(place < count // 2, 2 * place, 2 * (count - 1 - place) + 1)


def spread_kernel(count, steps, *refs):
    blocks = refs[: len(steps)]
    sides, (home_ref, away_ref) = refs[len(steps) : len(steps) + 4], refs[len(steps) + 4 : -3]
    kernel_rows, inputs, sems = refs[-3:]
    taps = kernel_rows.shape[0]
    rows = blocks[0].shape[-2]
    core = lax.axis_index("segment")
    place = ring_place(lax.axis_index("streams"), count)
    copies = []
    for slot, (step, block) in enumerate(zip(steps, blocks)):
        if step is None:
            source, target = block, kernel_rows
        else:
            distance, passed = step
            taker = 1 - core if passed else core
            stream = ring_stream(
                lax.rem(place + (2 * taker - 1) * distance + count, count), count
            )
            source = block if len(block.shape) == 3 else block.at[passed]
            part = source.shape[0]
            first = 0 if part == taps else taker * part
            target = kernel_rows.at[
                pl.ds(first, part), pl.ds(pl.multiple_of(stream * rows, rows), rows), :
            ]
        copy = pltpu.make_async_copy(source, target, sems.at[slot])
        copy.start()
        copies.append(copy)
    sessions, half = sides[0].shape
    for index, side in enumerate(sides):
        column = core if index % 2 == 0 else 1 - core
        first = index // 2 * sessions
        inputs[first : first + sessions, pl.ds(pl.multiple_of(column * half, half), half)] = side[...]
    for copy in copies:
        copy.wait()

    @pl.loop(0, taps)
    def _(tap):
        product = jnp.dot(inputs[...], kernel_rows[tap], preferred_element_type=F32)
        home_ref[tap] = product[:sessions].astype(home_ref.dtype)
        away_ref[tap] = product[sessions:].astype(away_ref.dtype)


def spread_taps(sides, blocks, steps, count, home_type):
    taps, _, width = blocks[0].shape
    sessions, depth = sides[0].shape[0], 2 * sides[0].shape[1]
    return pl.pallas_call(
        functools.partial(spread_kernel, count, steps),
        out_shape=(
            jax.ShapeDtypeStruct((taps, sessions, width), home_type),
            jax.ShapeDtypeStruct((taps, sessions, width), BF16),
        ),
        in_specs=[pl.BlockSpec(memory_space=pl.ANY)] * len(blocks) + [VMEM] * 4,
        out_specs=(VMEM, VMEM),
        scratch_shapes=[
            pltpu.VMEM((taps, depth, width), BF16),
            pltpu.VMEM((2 * sessions, depth), BF16),
            pltpu.SemaphoreType.DMA((len(blocks),)),
        ],
        compiler_params=pltpu.CompilerParams(vmem_limit_bytes=VMEM_LIMIT),
        cost_estimate=pl.CostEstimate(
            flops=4 * taps * sessions * depth * width,
            bytes_accessed=2 * taps * depth * width + 4 * sessions * depth + 6 * taps * sessions * width,
            transcendentals=0,
        ),
    )(*blocks, *sides)


def each_step(group, own_ref, other_ref):
    taps = own_ref.shape[0]
    for index, source in enumerate((own_ref, other_ref)):
        first = (group if index == 0 else 1 - group) * taps
        for tap in range(taps):
            yield first + tap, source[tap].astype(F32)


def excite_kernel(group_ref, own_ref, other_ref, prev_ref, bias_ref, window_ref, *part_refs):
    steps = 2 * own_ref.shape[0]
    history = prev_ref.shape[0] - steps
    for step in range(history):
        window_ref[step] = prev_ref[steps + step]
    for step, value in each_step(group_ref[0], own_ref, other_ref):
        up = value + prev_ref[step].astype(F32) + bias_ref[...]
        window_ref[history + step] = apply_elu(up).astype(BF16)
    first = 0
    for part_ref in part_refs:
        part_ref[...] = window_ref[first : first + part_ref.shape[0]]
        first += part_ref.shape[0]


def excite(group, own, other, prev, bias):
    steps, *rest = prev.shape
    sizes = (steps,) + tuple((steps + part) // 4 for part in range(4))
    return pl.pallas_call(
        excite_kernel,
        out_shape=[jax.ShapeDtypeStruct((size, *rest), BF16) for size in sizes],
        in_specs=[pl.BlockSpec(memory_space=pltpu.SMEM)] + [VMEM] * 4,
        out_specs=[VMEM] * len(sizes),
        compiler_params=pltpu.CompilerParams(vmem_limit_bytes=VMEM_LIMIT),
    )(group, own, other, prev, bias)


def residual_kernel(group_ref, own_ref, other_ref, prev_ref, mine_ref, *refs):
    parts, refs = refs[:4], refs[4:]
    bias_ref, res_mine_ref, res_theirs_ref, res_bias_ref, skip_ref, skip_bias_ref = refs[:6]
    out_ref, theirs_ref, products, frames = refs[6:]
    first = 0
    for part_ref in parts:
        theirs_ref[first : first + part_ref.shape[0]] = part_ref[...]
        first += part_ref.shape[0]
    taps, block, width = own_ref.shape
    steps = 2 * taps
    branch = None
    for source, weights in ((mine_ref, res_mine_ref), (theirs_ref, res_theirs_ref)):
        for offset in range(weights.shape[0]):
            term = jnp.dot(
                source[offset : offset + steps].reshape(steps * block, width),
                weights[offset],
                preferred_element_type=F32,
            )
            branch = term if branch is None else branch + term
    hidden = apply_elu(branch + res_bias_ref[...]).astype(BF16)
    projected = jnp.dot(hidden, skip_ref[...], preferred_element_type=F32)
    products[...] = projected.reshape(products.shape)
    for step, value in each_step(group_ref[0], own_ref, other_ref):
        up = value + prev_ref[step].astype(F32) + bias_ref[...]
        mixed = up + products[step] + skip_bias_ref[...]
        for part in range(width // 128):
            frames.at[part][pl.ds(step, block, stride=steps), :] = mixed[
                :, part * 128 : (part + 1) * 128
            ]
    for part in range(width // 128):
        out_ref[:, part * 128 : (part + 1) * 128] = frames[part].astype(BF16)


def residual(group, own, other, prev, mine, theirs, *parameters):
    taps, sessions, width = own.shape
    steps, block = 2 * taps, sessions // 2

    def blocks(array):
        return pl.BlockSpec((array.shape[0], block, width), lambda i: (0, i, 0))

    arrays = (own, other, prev, mine, *theirs)
    return pl.pallas_call(
        residual_kernel,
        out_shape=jax.ShapeDtypeStruct((sessions * steps, width), BF16),
        grid=(2,),
        in_specs=[pl.BlockSpec(memory_space=pltpu.SMEM)]
        + [blocks(array) for array in arrays]
        + [VMEM] * len(parameters),
        out_specs=pl.BlockSpec((block * steps, width), lambda i: (i, 0)),
        scratch_shapes=[
            pltpu.VMEM((mine.shape[0], block, width), BF16),
            pltpu.VMEM((steps, block, width), F32),
            pltpu.VMEM((width // 128, block * steps, 128), F32),
        ],
        compiler_params=pltpu.CompilerParams(vmem_limit_bytes=VMEM_LIMIT),
    )(group, *arrays, *parameters)


def weave_kernel(group_ref, own_ref, other_ref, out_ref, frames):
    taps, block, width = own_ref.shape
    for step, value in each_step(group_ref[0], own_ref, other_ref):
        for part in range(width // 128):
            frames.at[part][pl.ds(step, block, stride=2 * taps), :] = value[
                :, part * 128 : (part + 1) * 128
            ]
    for part in range(width // 128):
        out_ref[:, part * 128 : (part + 1) * 128] = frames[part].astype(BF16)


def weave(group, own, other):
    taps, sessions, width = own.shape
    steps, block = 2 * taps, sessions
    taken = pl.BlockSpec((taps, block, width), lambda i: (0, i, 0))
    return pl.pallas_call(
        weave_kernel,
        out_shape=jax.ShapeDtypeStruct((sessions * steps, width), BF16),
        grid=(1,),
        in_specs=[pl.BlockSpec(memory_space=pltpu.SMEM), taken, taken],
        out_specs=pl.BlockSpec((block * steps, width), lambda i: (i, 0)),
        scratch_shapes=[pltpu.VMEM((width // 128, block * steps, 128), F32)],
        compiler_params=pltpu.CompilerParams(vmem_limit_bytes=VMEM_LIMIT),
    )(group, own, other)


def swap(value, axis):
    return lax.ppermute(value, axis, [(0, 1), (1, 0)])


def after(value, earlier):
    return lax.optimization_barrier((value, earlier))[0]


class Ring:
    def __init__(self, count, own, other):
        order = ring_order(count)
        self.count = count
        self.pairs = []
        for p in range(count):
            here, there = order[p], order[(p + 1) % count]
            self.pairs += [(2 * here, 2 * there), (2 * there + 1, 2 * here + 1)]
        self.item = jnp.stack([own, other])
        self.blocks, self.steps, self.rounds = [own], [(0, 0)], 0

    def round(self, earlier=None, whole=False):
        self.rounds += 1
        item = self.item
        if 2 * self.rounds == self.count and not whole:
            part = item.shape[1] // 2
            item = lax.dynamic_slice_in_dim(item, lax.axis_index("segment") * part, part, axis=1)
        if earlier is not None:
            item = after(item, earlier)
        item = lax.ppermute(item, ("streams", "segment"), self.pairs)
        self.item = item
        self.blocks.append(item)
        self.steps.append((self.rounds, 0))
        if not whole:
            self.blocks.append(swap(item, "segment"))
            self.steps.append((self.rounds, 1))
        return item


def local(
    count,
    latent,
    conv_weight,
    conv_bias,
    tail_cache,
    input_cache,
    resume_slot,
    res_weight,
    res_bias,
    skip_weight,
    skip_bias,
):
    group = lax.axis_index("groups")
    group_word = group[None].astype(jnp.int32)
    rows, tap_count, width = conv_weight.shape
    sessions = latent.shape[0]
    taps = tap_count // 4

    halves = []
    for first in (0, tap_count // 2):
        part = lax.dynamic_slice_in_dim(conv_weight, first + group * taps, taps, axis=1)
        halves.append(part.transpose(1, 0, 2))

    use_ring = rows % 128 == 0 and count % 2 == 0
    if use_ring:
        other = swap(halves[0], "segment")
        prepared = swap(after(halves[1], other), "segment")
        up_ring, tail_ring = Ring(count, halves[0], other), Ring(count, halves[1], prepared)
    else:
        prepared = halves[1]

    portion = sessions // count
    cap = tail_cache.shape[0] // count
    half_taps, history = tail_cache.shape[1], input_cache.shape[1]
    slot_step = jnp.broadcast_to(
        resume_slot.astype(BF16)[:, None, None], (count * cap, 1, width)
    )
    filler = jnp.zeros((count * cap, half_taps - history - 1, width), BF16)
    beside = jnp.concatenate([input_cache, slot_step, filler], axis=1)
    stored = jnp.concatenate([tail_cache, beside], axis=2).reshape(count, cap * half_taps, 2 * width)
    parcel = jnp.concatenate([latent.reshape(count, portion, 2 * width), stored], axis=1)
    parcel = after(parcel, prepared)
    parcel = lax.all_to_all(parcel, "streams", split_axis=0, concat_axis=0, tiled=True)
    handed = parcel[:, :portion].reshape(sessions, 2 * width)
    stored = parcel[:, portion:].reshape(count * cap, half_taps, 2 * width)

    near_half = apply_elu(handed.astype(F32)).astype(BF16)
    near_other = swap(near_half, "segment")
    far_half = swap(after(near_half, near_other), "groups")
    sides = (near_half, near_other, far_half, swap(far_half, "segment"))

    slots = stored[:, history, width:].astype(jnp.int32)[:, :1]
    one_hot = (slots == jnp.arange(sessions, dtype=jnp.int32)[None, :]).astype(BF16)
    packed = jnp.concatenate([stored[:, :, :width], stored[:, :history, width:]], axis=1)
    prev = jnp.einsum("js,jkc->ksc", one_hot, packed, preferred_element_type=F32).astype(BF16)

    res_theirs = swap(res_weight, "segment")

    if use_ring:
        last = count // 2 - 1
        for _ in range(last):
            up_ring.round()
            nearly_done = tail_ring.round()
        up_ring.round(far_half)
        up_ring.blocks[0] = after(up_ring.blocks[0], nearly_done)
        own_up, away_up = spread_taps(sides, up_ring.blocks, up_ring.steps, count, F32)
        tail_ring.round(away_up, whole=True)
        own_tail, away_tail = spread_taps(sides, tail_ring.blocks, tail_ring.steps, count, BF16)
    else:
        whole = [lax.all_gather(own, "streams", axis=1, tiled=True) for own in halves]
        own_up, away_up = spread_taps(sides, whole[:1], [None], count, F32)
        own_tail, away_tail = spread_taps(sides, whole[1:], [None], count, BF16)
    other_up = swap(away_up, "groups")
    other_tail = swap(away_tail, "groups")

    own_up = after(own_up, (away_tail, res_theirs))
    bias = conv_bias[None]
    mine, *parts = excite(group_word, own_up, other_up, prev, bias)
    theirs = [swap(part, "segment") for part in parts]
    decoded = residual(
        group_word,
        own_up,
        other_up,
        prev,
        mine,
        theirs,
        bias,
        res_weight,
        res_theirs,
        res_bias[None],
        skip_weight,
        skip_bias[None],
    )
    decoded, other_tail = lax.optimization_barrier((decoded, other_tail))
    new_tail = weave(group_word, own_tail, other_tail)
    shape = (sessions, half_taps, width)
    return decoded.reshape(shape), new_tail.reshape(shape)


def solution(mesh):
    placed = (
        P(("groups", "streams"), "segment"),
        P("streams", None, "segment"),
        P("segment"),
        P(("groups", "streams"), None, "segment"),
        P(("groups", "streams"), None, "segment"),
        P(("groups", "streams")),
        P(None, "segment", None),
        P(),
        P(None, "segment"),
        P("segment"),
    )
    return jax.shard_map(
        functools.partial(local, mesh.shape["streams"]),
        mesh=mesh,
        in_specs=placed,
        out_specs=(
            P(("groups", "streams"), None, "segment"),
            P(("groups", "streams"), None, "segment"),
        ),
        check_vma=False,
    )
```
